32 devices in a mesh: dp: 4 (over z), seq: 8 (over y, x, core).
Axes of the slice: x: 2, y: 2, z: 4, core: 2. Of those that a mesh axis runs over, the one named last changes fastest.
Arguments:
- tokens: bfloat16 [4, 2048, 384], P('dp', 'seq'), may hold values from -6 to 6
- lengths: int32 [4, 5], P('dp'), may hold values from 64 to 1792, as said below
- order: int32 [4, 2048], P('dp', 'seq'), may hold values from 0 to 2047, as said below
- norm_gain: float32 [384], replicated, may hold values from 0.5 to 1.5
- w_in: bfloat16 [384, 1536], replicated, may hold values from -0.3125 to 0.3125
- conv_weight: float32 [768, 4], replicated, may hold values from -3 to 3
- conv_bias: float32 [768], replicated, may hold values from -1.8 to 1.8
- w_x: bfloat16 [768, 56], replicated, may hold values from -0.21875 to 0.21875
- w_dt: bfloat16 [24, 768], replicated, may hold values from -1.25 to 1.25
- dt_bias: float32 [768], replicated, may hold values from -6 to -2
- a_log: float32 [768, 16], replicated, may hold values from -6.9 to 2.8
- d_skip: float32 [768], replicated, may hold values from 0.5 to 1.5
- w_out: bfloat16 [768, 384], replicated, may hold values from -0.21875 to 0.21875
- cotangent: bfloat16 [4, 2048, 384], P('dp', 'seq'), may hold values from -6 to 6
Outputs:
- output: bfloat16 [4, 2048, 384], P('dp', 'seq')
- input_grad: bfloat16 [4, 2048, 384], P('dp', 'seq')
- gain_grad: float32 [384], replicated
- w_in_grad: float32 [384, 1536], replicated
- conv_weight_grad: float32 [768, 4], replicated
- conv_bias_grad: float32 [768], replicated
- w_x_grad: float32 [768, 56], replicated
- w_dt_grad: float32 [24, 768], replicated
- dt_bias_grad: float32 [768], replicated
- a_log_grad: float32 [768, 16], replicated
- d_skip_grad: float32 [768], replicated
- w_out_grad: float32 [768, 384], replicated
The draws below stay inside these ranges and needn't reach their ends.
Inputs may be any that keep to these rules, and one draw needn't show every extreme that they name: `lengths`: each group is two objects, one scene and two objects, in that order; each object holds 64 to 127 tokens and the scene the rest of 2048; in the first group every object holds exactly 64. `order`: in each group a permutation of its places that maps the places of every cloud onto themselves.
All inputs are finite; a program needn't handle non-finite values.
Results may differ from the reference program's by a relative error of at most 0.0089.
Values may be sent and summed in bfloat16 or wider, within the bound.
No kernel may reach another device: no remote copies, remote signals or barrier semaphores. Data moves between devices by JAX's collectives and lax.ppermute only.
A program may use at most 256 MiB of HBM per device.

```python
import jax
import jax.numpy as jnp
from jax import lax

D = 384
E = 768
N = 16
R = 24
K = 4
TOK_DEV = 256
CLOUDS = 5
GROUPS = 4
GROUP_TOK = 2048


def cloud_lengths(key):
    objects = jax.random.randint(key, (GROUPS, CLOUDS - 1), TOK_DEV // 4, TOK_DEV // 2)
    objects = objects.at[0].set(TOK_DEV // 4)
    scene = GROUP_TOK - jnp.sum(objects, axis=1, keepdims=True)
    return jnp.concatenate([objects[:, :2], scene, objects[:, 2:]], axis=1).astype(jnp.int32)


def draw_lengths(key, part):
    lengths = cloud_lengths(key)
    return lengths


def draw_order(key, part):
    lengths = cloud_lengths(key)
    key = jax.random.fold_in(key, 5)
    ends = jnp.cumsum(lengths, axis=1)
    positions = jnp.arange(GROUP_TOK, dtype=jnp.int32)
    segment = jnp.sum((positions[None, :, None] >= ends[:, None, :]).astype(jnp.int32), axis=2)
    noise = jax.random.randint(key, (GROUPS, GROUP_TOK), 0, 64)
    score = segment * (GROUP_TOK * 64) + noise * GROUP_TOK + positions[None, :]
    return jnp.argsort(score, axis=1, stable=True).astype(jnp.int32)


def level_of(stream_key, extent, cuts, least, largest):
    factor_of, own = 1.0, jax.random.fold_in(stream_key, 6)
    for dim, blocks in cuts:
        steps = jnp.exp(jax.random.uniform(jax.random.fold_in(own, dim), (blocks,), jnp.float32, least / len(cuts), largest / len(cuts)))
        factor_of = factor_of * jnp.repeat(steps, extent[dim] // blocks).reshape([-1 if axis == dim else 1 for axis in range(len(extent))])
    return factor_of


def gaussian(rng, extent, spread, most, cuts=(), kind=jnp.bfloat16):
    array = spread * jax.random.normal(rng, extent, jnp.float32)
    if cuts:
        array = array * level_of(rng, extent, cuts, -0.22, 0.18)
    return jnp.clip(array, -most, most).astype(kind)


def setup_inputs(seed: int = 0) -> dict:
    arg_keys = jax.random.split(jax.random.key(seed), 15)
    tokens = gaussian(arg_keys[0], (GROUPS, GROUP_TOK, D), 1.0, 6.0, ((0, 4), (1, 8)))
    lengths = draw_lengths(jax.random.fold_in(arg_keys[14], 71), 0)
    order = draw_order(jax.random.fold_in(arg_keys[14], 71), 0)
    norm_gain = jnp.clip(1.0 + 0.1 * jax.random.normal(arg_keys[3], (D,), jnp.float32), 0.5, 1.5)
    w_in = gaussian(arg_keys[4], (D, 2 * E), D ** -0.5, 0.3125)
    conv_weight = gaussian(arg_keys[5], (E, K), K ** -0.5, 3.0, (), jnp.float32)
    conv_bias = gaussian(arg_keys[6], (E,), 0.3, 1.8, (), jnp.float32)
    w_x = gaussian(arg_keys[7], (E, R + 2 * N), E ** -0.5, 0.21875)
    w_dt = gaussian(arg_keys[8], (R, E), R ** -0.5, 1.25)
    dt_bias = jnp.clip(jax.random.uniform(arg_keys[9], (E,), jnp.float32, -6.0, -2.0), -6.0, -2.0)
    a_log = jnp.clip(jax.random.uniform(arg_keys[10], (E, N), jnp.float32, -6.9, 2.8), -6.9, 2.8)
    d_skip = jnp.clip(jax.random.uniform(arg_keys[11], (E,), jnp.float32, 0.5, 1.5), 0.5, 1.5)
    w_out = gaussian(arg_keys[12], (E, D), E ** -0.5, 0.21875)
    cotangent = gaussian(arg_keys[13], (GROUPS, GROUP_TOK, D), 1.0, 6.0, ((0, 4), (1, 8)))
    return dict(tokens=tokens, lengths=lengths, order=order, norm_gain=norm_gain, w_in=w_in, conv_weight=conv_weight, conv_bias=conv_bias, w_x=w_x, w_dt=w_dt, dt_bias=dt_bias, a_log=a_log, d_skip=d_skip, w_out=w_out, cotangent=cotangent)


EPSILON = 1e-05
PRECISE = lax.Precision.HIGHEST

@jax.custom_vjp
def low(v):
    return lax.optimization_barrier(v.astype(jnp.bfloat16)).astype(jnp.float32)

@jax.custom_vjp
def low_back(v):
    return v

def low_keep(v):
    return (low(v), None)

def low_pass(kept, grad):
    return (grad,)

def back_keep(v):
    return (v, None)

def back_low(kept, grad):
    return (low(grad),)
low.defvjp(low_keep, low_pass)
low_back.defvjp(back_keep, back_low)

def combine(earlier, later):
    return (earlier[0] * later[0], later[0] * earlier[1] + later[1])

def silu(value):
    return value * jax.nn.sigmoid(value)

def branch_group(weights_all, group_x, group_lengths, group_order):
    norm_gain, w_in, conv_weight, conv_bias, w_x, w_dt, dt_bias, a_log, d_skip, w_out = weights_all
    trans_x = low_back(group_x[group_order])
    positions = jnp.arange(GROUP_TOK, dtype=jnp.int32)
    starts = (jnp.cumsum(group_lengths) - group_lengths).astype(jnp.int32)
    seg_start = lax.optimization_barrier(jnp.max(jnp.where(starts[None, :] <= positions[:, None], starts[None, :], 0), axis=1))
    keep_mask = (positions != seg_start).astype(jnp.float32)
    inv_rms = lax.rsqrt(lax.optimization_barrier(jnp.mean(trans_x * trans_x, axis=1, keepdims=True)) + EPSILON)
    normed = low(trans_x * inv_rms * norm_gain)
    projected = low_back(jnp.dot(normed, w_in, precision=PRECISE))
    conv_in = low(projected[:, :E])
    gate_z = projected[:, E:]
    conv_out = conv_bias + jnp.zeros((GROUP_TOK, E), jnp.float32)
    for tap_index in range(K):
        lag_rows = K - 1 - tap_index
        shifted_in = jnp.concatenate([jnp.zeros((lag_rows, E), jnp.float32), conv_in[:GROUP_TOK - lag_rows]], axis=0)
        valid_tap = (positions - lag_rows >= seg_start).astype(jnp.float32)[:, None]
        conv_out = conv_out + conv_weight[:, tap_index] * shifted_in * valid_tap
    activated = low(silu(conv_out))
    x_proj = low_back(jnp.dot(activated, w_x, precision=PRECISE))
    dt_low = low(x_proj[:, :R])
    b_coeff = x_proj[:, R:R + N]
    c_coeff = x_proj[:, R + N:]
    step_size = jax.nn.softplus(low_back(jnp.dot(dt_low, w_dt, precision=PRECISE) + dt_bias))
    a_matrix = -jnp.exp(a_log)
    block_len = min(256, TOK_DEV)
    block_count = GROUP_TOK // block_len

    def scan_step(state_now, pieces):
        step_blk, inb_blk, outc_blk, act_blk, keep_blk = pieces
        decay_rate = jnp.exp(step_blk[:, :, None] * a_matrix[None]) * keep_blk[:, None, None]
        drive_term = step_blk[:, :, None] * inb_blk[:, None, :] * act_blk[:, :, None]
        drive_term = drive_term.at[0].add(decay_rate[0] * state_now)
        unused_prod, state_seq = lax.associative_scan(combine, (decay_rate, drive_term))
        return (state_seq[-1], jnp.einsum('len,ln->le', state_seq, outc_blk, precision=PRECISE))
    pieces = (step_size.reshape(block_count, block_len, E), b_coeff.reshape(block_count, block_len, N), c_coeff.reshape(block_count, block_len, N), activated.reshape(block_count, block_len, E), keep_mask.reshape(block_count, block_len))
    unused_state, scan_out = lax.scan(jax.checkpoint(scan_step), jnp.zeros((E, N), jnp.float32), pieces)
    mixed_out = scan_out.reshape(GROUP_TOK, E) + d_skip * activated
    gated = low(mixed_out * silu(gate_z))
    branch_out = low(jnp.dot(gated, w_out, precision=PRECISE))
    return jnp.zeros((GROUP_TOK, D), jnp.float32).at[group_order].set(branch_out)

def reference(tokens, lengths, order, norm_gain, w_in, conv_weight, conv_bias, w_x, w_dt, dt_bias, a_log, d_skip, w_out, cotangent):
    weights_all = tuple((value.astype(jnp.float32) for value in (norm_gain, w_in, conv_weight, conv_bias, w_x, w_dt, dt_bias, a_log, d_skip, w_out)))
    input_f = tokens.astype(jnp.float32)

    def whole_block(weights_now, inputs_now):
        branches = lax.map(lambda group_args: branch_group(weights_now, group_args[0], group_args[1], group_args[2]), (inputs_now, lengths, order))
        return inputs_now + branches
    output, backward_fn = jax.vjp(whole_block, weights_all, input_f)
    gradients, input_grad = backward_fn(cotangent.astype(jnp.float32))
    return (output.astype(jnp.bfloat16), input_grad.astype(jnp.bfloat16), gradients[0], gradients[1], gradients[2], gradients[3], gradients[4], gradients[5], gradients[6], gradients[7], gradients[8], gradients[9])
```

```python
import functools

import jax
import jax.numpy as jnp
from jax import lax
from jax.experimental import pallas as pl
from jax.experimental.pallas import tpu as pltpu
from jax.sharding import PartitionSpec as P

EPSILON = 1e-05
LOG2E = 1.4426950408889634
FAR = 1e30
CHUNKS = 8
LANES = 128
BLOCK = 16
ORDER_ROWS = 16
F32, BF16 = jnp.float32, jnp.bfloat16
VMEM_BYTES = 60 * 1024 * 1024


def dot(a, b, contract=((1,), (0,))):
    return lax.dot_general(a, b, (contract, ((), ())), preferred_element_type=F32)


def wide(tile, width):
    return jnp.concatenate([tile] * (width // LANES), axis=1)


def sigmoid(v):
    return 1.0 / (1.0 + jnp.exp(-v))


def places(first, rows, r0, steps):
    r = r0 + lax.broadcasted_iota(jnp.int32, (rows, LANES), 0)
    return first + lax.rem(r, CHUNKS) * steps + lax.div(r, CHUNKS)


def cloud_start(meta, clouds, place):
    start = jnp.zeros_like(place)
    for k in range(clouds):
        begin = meta[1 + k]
        start = jnp.maximum(start, jnp.where(begin <= place, begin, 0))
    return start


def fill_valid(valid, meta, clouds, rows, lags):
    steps = rows // CHUNKS

    def body(j, carry):
        r0 = pl.multiple_of(j * BLOCK, BLOCK)
        place = places(meta[0], BLOCK, r0, steps)
        begin = cloud_start(meta, clouds, place)
        for k in range(1, lags + 1):
            valid[k - 1, pl.ds(r0, BLOCK), :] = (place - k >= begin).astype(F32)
        return carry

    lax.fori_loop(0, rows // BLOCK, body, 0)


def own_column(order8, rows):
    steps = rows // CHUNKS
    both = order8[...]
    return jnp.concatenate([both[:, i : i + 1] for i in range(steps)], axis=0)


def gather_rows(column, pieces, src, rows):
    total = None
    lane = lax.broadcasted_iota(jnp.int32, (column.shape[0], rows), 1)
    for p, piece in enumerate(pieces):
        mine = (column - src[p] * rows == lane).astype(F32).astype(BF16)
        part = dot(mine, piece)
        total = part if total is None else total + part
    return total


def fill_broadcast(out, xproj, first, count, rows):
    def body(j, carry):
        r0 = pl.multiple_of(j * BLOCK, BLOCK)
        block = xproj[pl.ds(r0, BLOCK), :]
        for n in range(count):
            out[pl.ds(r0, BLOCK), n * LANES : (n + 1) * LANES] = jnp.broadcast_to(
                block[:, first + n : first + n + 1], (BLOCK, LANES)
            )
        return carry

    lax.fori_loop(0, rows // BLOCK, body, 0)


def rates(alog):
    return -jnp.exp(alog[...])


def chunk_of(ref, c, count):
    return jnp.concatenate([ref[b, pl.ds(c, count, stride=CHUNKS), :] for b in range(ref.shape[0])], axis=1)


def set_chunk(ref, c, value):
    for b in range(ref.shape[0]):
        ref[b, pl.ds(c, value.shape[0], stride=CHUNKS), :] = value[:, b * LANES : (b + 1) * LANES]


def pre_kernel(
    sizes, n_pieces, meta, src, order8, *refs
):
    rows, width, inner, rank, state, lags, clouds = sizes
    steps = rows // CHUNKS
    pieces = refs[:n_pieces]
    (gain, w_in, conv_w, conv_b, w_x, w_dt, dt_b, alog) = refs[n_pieces : n_pieces + 8]
    (trans_o, normed_o, gate_o, ext_o, conv_o, act_o, step_o, xproj_o, chunkf_o, sums_o, f_o, orders_o) = refs[
        n_pieces + 8 : n_pieces + 20
    ]
    conv_in, valid, far, use, bbc, a2 = refs[n_pieces + 20 :]
    me = lax.div(meta[0], rows)
    halo = jnp.full((1, 1), -1.0, F32)
    halos = [halo] * (lags + 1)
    for p in range(n_pieces):
        tail = pieces[p][rows : rows + ORDER_ROWS, :rows].astype(F32)
        row = tail[0:1] * 128.0 + tail[1:2]
        orders_o[p : p + 1, :] = row
        behind = src[p] == me - 1
        for k in range(1, lags + 1):
            r = (steps - k) * CHUNKS + CHUNKS - 1
            halos[k] = jnp.where(behind, row[:, r : r + 1], halos[k])
    sub = lax.broadcasted_iota(jnp.int32, (BLOCK, 1), 0)
    extra = jnp.full((BLOCK, 1), -1.0, F32)
    for k in range(1, lags + 1):
        extra = jnp.where(sub == k, halos[k], extra)
    column = jnp.concatenate([own_column(order8, rows), extra.astype(jnp.int32)], axis=0)
    trans = gather_rows(column, [p[0:rows, :] for p in pieces], src, rows)
    trans_o[...] = trans[:rows].astype(BF16)
    inv_rms = lax.rsqrt(jnp.mean(trans * trans, axis=1, keepdims=True) + EPSILON)
    normed = (trans * inv_rms * gain[...]).astype(BF16)
    normed_o[...] = normed[:rows]
    conv_in[...] = dot(normed, w_in[:, :inner]).astype(BF16).astype(F32)
    gate_o[...] = dot(normed[:rows], w_in[:, inner:])
    pad = lags * CHUNKS
    ext_o[pad : pad + rows, :] = conv_in[:rows, :]
    first_sub = lax.broadcasted_iota(jnp.int32, (CHUNKS, inner), 0) == 0
    for k in range(1, lags + 1):
        tile = conv_in[(steps - k) * CHUNKS : (steps - k + 1) * CHUNKS, :]
        before = conv_in[rows + k : rows + k + 1, :]
        ext_o[(lags - k) * CHUNKS : (lags - k + 1) * CHUNKS, :] = jnp.where(
            first_sub, before, pltpu.roll(tile, 1, 0)
        )
    fill_valid(valid, meta, clouds, rows, lags)

    def conv_body(j, carry):
        r0 = pl.multiple_of(j * BLOCK, BLOCK)
        out = conv_b[...] + conv_w[lags : lags + 1, :] * ext_o[pl.ds(r0 + pad, BLOCK), :]
        for k in range(1, lags + 1):
            ok = wide(valid[k - 1, pl.ds(r0, BLOCK), :], inner)
            shifted = ext_o[pl.ds(pl.multiple_of(r0 + pad - k * CHUNKS, CHUNKS), BLOCK), :]
            out = out + conv_w[lags - k : lags - k + 1, :] * shifted * ok
        conv_o[pl.ds(r0, BLOCK), :] = out
        act_o[pl.ds(r0, BLOCK), :] = (out * sigmoid(out)).astype(BF16)
        return carry

    lax.fori_loop(0, rows // BLOCK, conv_body, 0)
    xproj = dot(act_o[...], w_x[...])
    xproj_o[...] = xproj
    step_o[...] = dot(xproj.astype(BF16), w_dt[...])

    def step_body(j, carry):
        r0 = pl.multiple_of(j * BLOCK, BLOCK)
        pre = step_o[pl.ds(r0, BLOCK), :] + dt_b[...]
        step = jnp.maximum(pre, 0.0) + jnp.log1p(jnp.exp(-jnp.abs(pre)))
        step_o[pl.ds(r0, BLOCK), :] = step
        keep = wide(valid[0, pl.ds(r0, BLOCK), :], inner)
        distance = jnp.where(keep > 0.5, step, FAR)
        far[pl.ds(r0, BLOCK), :] = distance
        use[pl.ds(r0, BLOCK), :] = step * act_o[pl.ds(r0, BLOCK), :].astype(F32)
        return carry + distance[:CHUNKS] + distance[CHUNKS:]

    sums_o[...] = lax.fori_loop(0, rows // BLOCK, step_body, jnp.zeros((CHUNKS, inner), F32))
    fill_broadcast(bbc, xproj_o, rank, state, rows)
    a2[...] = rates(alog) * LOG2E
    for lb in range(inner // LANES):
        ls = slice(lb * LANES, (lb + 1) * LANES)
        rate = [jnp.broadcast_to(a2[n : n + 1, ls], (CHUNKS, LANES)) for n in range(state)]

        def scan_body(i, states):
            r = pl.ds(pl.multiple_of(i * CHUNKS, CHUNKS), CHUNKS)
            distance, u = far[r, ls], use[r, ls]
            return tuple(
                jnp.exp2(distance * rate[n]) * states[n] + u * bbc[r, n * LANES : (n + 1) * LANES]
                for n in range(state)
            )

        zero = jnp.zeros((CHUNKS, LANES), F32)
        last = lax.fori_loop(0, steps, scan_body, (zero,) * state, unroll=2)
        for n in range(state):
            chunkf_o[lb, n * CHUNKS : (n + 1) * CHUNKS, :] = last[n]
    total = jnp.zeros((state, inner), F32)
    for c in range(CHUNKS):
        total = jnp.exp2(a2[...] * sums_o[c : c + 1, :]) * total + chunk_of(chunkf_o, c, state)
    f_o[...] = total


def back_kernel(sizes, n_pieces, meta, src, order8, *refs):
    rows, width, inner, rank, state, lags, clouds = sizes
    steps = rows // CHUNKS
    pieces = refs[:n_pieces]
    gate, step, xproj, alog, w_out, sums, f = refs[n_pieces : n_pieces + 7]
    dy_o, gg_o, chunkb_o, carry_o = refs[n_pieces + 7 : n_pieces + 11]
    valid, far, gm, cbc, a2 = refs[n_pieces + 11 :]
    trans_dy = gather_rows(own_column(order8, rows), [p[...] for p in pieces], src, rows).astype(BF16)
    dy_o[...] = trans_dy
    gg_o[...] = dot(trans_dy, w_out[...], ((1,), (1,)))
    fill_valid(valid, meta, clouds, rows, 1)

    def body(j, carry):
        r = pl.ds(pl.multiple_of(j * BLOCK, BLOCK), BLOCK)
        z = gate[r, :]
        gm[r, :] = gg_o[r, :] * (z * sigmoid(z))
        far[r, :] = jnp.where(wide(valid[0, r, :], inner) > 0.5, step[r, :], FAR)
        return carry

    lax.fori_loop(0, rows // BLOCK, body, 0)
    fill_broadcast(cbc, xproj, rank + state, state, rows)
    a2[...] = rates(alog) * LOG2E
    for lb in range(inner // LANES):
        ls = slice(lb * LANES, (lb + 1) * LANES)
        rate = [jnp.broadcast_to(a2[n : n + 1, ls], (CHUNKS, LANES)) for n in range(state)]

        def scan_body(k, flows):
            r = pl.ds(pl.multiple_of((steps - 1 - k) * CHUNKS, CHUNKS), CHUNKS)
            distance, g = far[r, ls], gm[r, ls]
            return tuple(
                jnp.exp2(distance * rate[n]) * (flows[n] + g * cbc[r, n * LANES : (n + 1) * LANES])
                for n in range(state)
            )

        zero = jnp.zeros((CHUNKS, LANES), F32)
        last = lax.fori_loop(0, steps, scan_body, (zero,) * state, unroll=2)
        for n in range(state):
            chunkb_o[lb, n * CHUNKS : (n + 1) * CHUNKS, :] = last[n]
    total = jnp.zeros((state, inner), F32)
    for c in reversed(range(CHUNKS)):
        total = jnp.exp2(a2[...] * sums[c : c + 1, :]) * total + chunk_of(chunkb_o, c, state)
    carry_o[:state, :] = f[...]
    carry_o[state : 2 * state, :] = total
    carry_o[2 * state :, :] = jnp.broadcast_to(
        jnp.sum(sums[...], axis=0, keepdims=True), (CHUNKS, inner)
    )


def main_kernel(sizes, n_pieces, meta, src, *refs):
    rows, width, inner, rank, state, lags, clouds = sizes
    steps = rows // CHUNKS
    carries = refs[:n_pieces]
    (trans_dy, gg, gate, ext, conv, act, step, xproj, chunkf, chunkb, sums, alog, skip, w_out, w_x, w_dt, conv_w) = refs[
        n_pieces : n_pieces + 17
    ]
    (branch_o, gz_o, gci_o, rim_o, wout_o, wx_o, wdt_o, small_o, galog_o) = refs[n_pieces + 17 : n_pieces + 26]
    (valid, far, use, gm, bbc, cbc, a2, states, decays, mixed, gs, lamb, gb, gc, sstart, gstart, gated, held) = refs[
        n_pieces + 26 :
    ]
    me = lax.div(meta[0], rows)
    devices = n_pieces
    a2[...] = rates(alog) * LOG2E
    state_in = jnp.zeros((state, inner), F32)
    flow_in = jnp.zeros((state, inner), F32)
    size = 2 * state + CHUNKS
    for p in range(devices):
        held[pl.ds(pl.multiple_of(src[p] * size, CHUNKS), size), :] = carries[p][...]

    def ahead(s, flow):
        base = pl.multiple_of(s * size, CHUNKS)
        p_s = jnp.exp2(a2[...] * held[pl.ds(base + 2 * state, 1), :])
        return jnp.where(s < me, p_s * flow + held[pl.ds(base, state), :], flow)

    state_in = lax.fori_loop(0, devices, ahead, state_in)

    def behind(k, flow):
        s = devices - 1 - k
        base = pl.multiple_of(s * size, CHUNKS)
        p_s = jnp.exp2(a2[...] * held[pl.ds(base + 2 * state, 1), :])
        return jnp.where(s > me, p_s * flow + held[pl.ds(pl.multiple_of(base + state, CHUNKS), state), :], flow)

    flow_in = lax.fori_loop(0, devices, behind, flow_in)
    now = state_in
    for c in range(CHUNKS):
        set_chunk(sstart, c, now)
        now = jnp.exp2(a2[...] * sums[c : c + 1, :]) * now + chunk_of(chunkf, c, state)
    now = flow_in
    for c in reversed(range(CHUNKS)):
        set_chunk(gstart, c, now)
        now = jnp.exp2(a2[...] * sums[c : c + 1, :]) * now + chunk_of(chunkb, c, state)
    fill_valid(valid, meta, clouds, rows, lags)

    def prepare(j, carry):
        r = pl.ds(pl.multiple_of(j * BLOCK, BLOCK), BLOCK)
        z = gate[r, :]
        gm[r, :] = gg[r, :] * (z * sigmoid(z))
        far[r, :] = jnp.where(wide(valid[0, r, :], inner) > 0.5, step[r, :], FAR)
        use[r, :] = step[r, :] * act[r, :].astype(F32)
        return carry

    lax.fori_loop(0, rows // BLOCK, prepare, 0)
    fill_broadcast(bbc, xproj, rank, state, rows)
    fill_broadcast(cbc, xproj, rank + state, state, rows)
    for lb in range(inner // LANES):
        ls = slice(lb * LANES, (lb + 1) * LANES)
        rate = [jnp.broadcast_to(a2[n : n + 1, ls], (CHUNKS, LANES)) for n in range(state)]
        begin = []
        for n in range(state):
            tile = sstart[lb, n * CHUNKS : (n + 1) * CHUNKS, :]
            states[n, 0:CHUNKS, ls] = tile
            begin.append(tile)

        def forward(i, now):
            r0 = pl.multiple_of(i * CHUNKS, CHUNKS)
            r = pl.ds(r0, CHUNKS)
            after = pl.ds(pl.multiple_of(r0 + CHUNKS, CHUNKS), CHUNKS)
            distance, u = far[r, ls], use[r, ls]
            new, out = [], None
            for n in range(state):
                decay = jnp.exp2(distance * rate[n])
                value = decay * now[n] + u * bbc[r, n * LANES : (n + 1) * LANES]
                decays[n, r, ls] = decay
                states[n, after, ls] = value
                part = value * cbc[r, n * LANES : (n + 1) * LANES]
                out = part if out is None else out + part
                new.append(value)
            mixed[r, ls] = out
            return tuple(new)

        lax.fori_loop(0, steps, forward, tuple(begin), unroll=2)

    def gating(j, carry):
        r = pl.ds(pl.multiple_of(j * BLOCK, BLOCK), BLOCK)
        z, a = gate[r, :], act[r, :].astype(F32)
        s = sigmoid(z)
        m = mixed[r, :] + skip[...] * a
        gated[r, :] = (m * (z * s)).astype(BF16)
        gz_o[r, :] = (gg[r, :] * m * s * (1.0 + z * (1.0 - s))).astype(BF16)
        part = gm[r, :] * a
        return carry + part[:CHUNKS] + part[CHUNKS:]

    skip_sum = lax.fori_loop(0, rows // BLOCK, gating, jnp.zeros((CHUNKS, inner), F32))
    branch_o[...] = dot(gated[...], w_out[...]).astype(BF16)
    wout_o[...] = dot(gated[...], trans_dy[...], ((0,), (0,)))
    group = 3
    pair = 4
    for lg in range(inner // LANES // group):
        lanes = [slice((lg * group + k) * LANES, (lg * group + k + 1) * LANES) for k in range(group)]
        for ng in range(state // pair):
            ns = [ng * pair + k for k in range(pair)]
            rate = [[jnp.broadcast_to(a2[n : n + 1, ls] * (1.0 / LOG2E), (CHUNKS, LANES)) for ls in lanes] for n in ns]
            begin = [gstart[lg * group + k, n * CHUNKS : (n + 1) * CHUNKS, :] for n in ns for k in range(group)]
            zero = jnp.zeros((CHUNKS, LANES), F32)

            def backward(k, carry):
                flows, sums_a = carry
                r0 = pl.multiple_of((steps - 1 - k) * CHUNKS, CHUNKS)
                r = pl.ds(r0, CHUNKS)
                after = pl.ds(pl.multiple_of(r0 + CHUNKS, CHUNKS), CHUNKS)
                gs_t = [None] * group
                lamb_t = [None] * group
                g_t = [gm[r, ls] for ls in lanes]
                u_t = [use[r, ls] for ls in lanes]
                d_t = [step[r, ls] for ls in lanes]
                new_flows, new_sums = [], []
                for q, n in enumerate(ns):
                    b = bbc[r, n * LANES : (n + 1) * LANES]
                    c = cbc[r, n * LANES : (n + 1) * LANES]
                    gb_t = gc_t = None
                    for x, ls in enumerate(lanes):
                        lam = g_t[x] * c + flows[q * group + x]
                        flow = decays[n, r, ls] * lam
                        part = flow * states[n, r, ls]
                        one, two = part * rate[q][x], lam * b
                        gs_t[x] = one if gs_t[x] is None else gs_t[x] + one
                        lamb_t[x] = two if lamb_t[x] is None else lamb_t[x] + two
                        three, four = lam * u_t[x], g_t[x] * states[n, after, ls]
                        gb_t = three if gb_t is None else gb_t + three
                        gc_t = four if gc_t is None else gc_t + four
                        new_flows.append(flow)
                        new_sums.append(sums_a[q * group + x] + part * d_t[x])
                    nl = slice(n * LANES, (n + 1) * LANES)
                    if lg == 0:
                        gb[r, nl] = gb_t
                        gc[r, nl] = gc_t
                    else:
                        gb[r, nl] += gb_t
                        gc[r, nl] += gc_t
                for x, ls in enumerate(lanes):
                    if ng == 0:
                        gs[r, ls] = gs_t[x]
                        lamb[r, ls] = lamb_t[x]
                    else:
                        gs[r, ls] += gs_t[x]
                        lamb[r, ls] += lamb_t[x]
                return tuple(new_flows), tuple(new_sums)

            flows, sums_a = lax.fori_loop(
                0, steps, backward, (tuple(begin), (zero,) * (pair * group))
            )
            for q, n in enumerate(ns):
                for x, ls in enumerate(lanes):
                    galog_o[n : n + 1, ls] = (
                        jnp.sum(sums_a[q * group + x], axis=0, keepdims=True) * rate[q][x][0:1]
                    )
    col = lax.broadcasted_iota(jnp.int32, (state * LANES, LANES), 1)
    row = lax.div(lax.broadcasted_iota(jnp.int32, (state * LANES, LANES), 0), LANES)
    pick_b = (col == row + rank).astype(F32).astype(BF16)
    pick_c = (col == row + rank + state).astype(F32).astype(BF16)

    def lane_sums(ref, pick):
        whole = ref[...]
        high = whole.astype(BF16)
        low = (whole - high.astype(F32)).astype(BF16)
        return dot(high, pick) + dot(low, pick)

    grad_bc = lane_sums(gb, pick_b) + lane_sums(gc, pick_c)
    gpre = gated

    def pre_body(j, carry):
        r = pl.ds(pl.multiple_of(j * BLOCK, BLOCK), BLOCK)
        grad_step = gs[r, :] + lamb[r, :] * act[r, :].astype(F32)
        grad_pre = (grad_step * (1.0 - jnp.exp(-step[r, :]))).astype(BF16)
        gpre[r, :] = grad_pre
        part = grad_pre.astype(F32)
        return carry + part[:CHUNKS] + part[CHUNKS:]

    dt_sum = lax.fori_loop(0, rows // BLOCK, pre_body, jnp.zeros((CHUNKS, inner), F32))
    dt_low = xproj[...].astype(BF16)
    wdt_o[...] = dot(dt_low, gpre[...], ((0,), (0,)))
    grad_xproj = (dot(gpre[...], w_dt[...], ((1,), (1,))) + grad_bc).astype(BF16)
    wx_o[...] = dot(grad_xproj, act[...], ((0,), (0,)))
    gs[...] = dot(grad_xproj, w_x[...], ((1,), (1,)))
    gconv = mixed

    def conv_body(j, carry):
        r0 = pl.multiple_of(j * BLOCK, BLOCK)
        r = pl.ds(r0, BLOCK)
        grad_act = gm[r, :] * skip[...] + lamb[r, :] * step[r, :] + gs[r, :]
        v = conv[r, :]
        s = sigmoid(v)
        grad = grad_act * (s * (1.0 + v * (1.0 - s)))
        gconv[r, :] = grad
        new = [carry[0] + grad[:CHUNKS] + grad[CHUNKS:]]
        for k in range(lags + 1):
            masked = grad if k == 0 else grad * wide(valid[k - 1, r, :], inner)
            part = masked * ext[pl.ds(pl.multiple_of(r0 + (lags - k) * CHUNKS, CHUNKS), BLOCK), :]
            new.append(carry[1 + k] + part[:CHUNKS] + part[CHUNKS:])
        return tuple(new)

    conv_sums = lax.fori_loop(
        0, rows // BLOCK, conv_body, (jnp.zeros((CHUNKS, inner), F32),) * (lags + 2)
    )
    small = [skip_sum, dt_sum, conv_sums[0]] + [conv_sums[1 + lags - t] for t in range(lags + 1)]
    for k, part in enumerate(small):
        small_o[k : k + 1, :] = jnp.sum(part, axis=0, keepdims=True)
    small_o[len(small) :, :] = jnp.zeros((small_o.shape[0] - len(small), inner), F32)

    def masked_tile(i, k):
        r = pl.ds(pl.multiple_of(i * CHUNKS, CHUNKS), CHUNKS)
        tile = gconv[r, :] * conv_w[lags - k : lags - k + 1, :]
        return tile if k == 0 else tile * wide(valid[k - 1, r, :], inner)

    def spread(i, carry):
        total = masked_tile(i, 0)
        for k in range(1, lags + 1):
            total = total + masked_tile(i + k, k)
        gci_o[pl.ds(pl.multiple_of(i * CHUNKS, CHUNKS), CHUNKS), :] = total
        return carry

    lax.fori_loop(0, steps - lags, spread, 0)
    sub = lax.broadcasted_iota(jnp.int32, (CHUNKS, inner), 0)
    for i in range(steps - lags, steps):
        total = masked_tile(i, 0)
        for k in range(1, lags + 1):
            if i + k < steps:
                total = total + masked_tile(i + k, k)
            else:
                moved = pltpu.roll(masked_tile(i + k - steps, k), CHUNKS - 1, 0)
                total = total + jnp.where(sub == CHUNKS - 1, 0.0, moved)
        gci_o[i * CHUNKS : (i + 1) * CHUNKS, :] = total
    rim_o[...] = jnp.zeros((CHUNKS, inner), F32)
    for b in range(1, lags + 1):
        total = jnp.zeros((1, inner), F32)
        for k in range(b, lags + 1):
            total = total + masked_tile(k - b, k)[0:1]
        rim_o[b : b + 1, :] = total


def final_kernel(sizes, trans, normed, gci, gz, rim, gain, w_in, back_o, win_o, gain_o):
    rows, width, inner, rank, state, lags, clouds = sizes
    steps = rows // CHUNKS
    r = lax.broadcasted_iota(jnp.int32, (rows, inner), 0)
    total = gci[...]
    for k in range(1, lags + 1):
        total = total + jnp.where(r == (steps - k) * CHUNKS + CHUNKS - 1, rim[k : k + 1, :], 0.0)
    grad_ci = total.astype(BF16)
    grad_z = gz[...]
    win_o[:, :inner] = dot(normed[...], grad_ci, ((0,), (0,)))
    win_o[:, inner:] = dot(normed[...], grad_z, ((0,), (0,)))
    grad_normed = dot(grad_ci, w_in[:, :inner], ((1,), (1,))) + dot(grad_z, w_in[:, inner:], ((1,), (1,)))
    x = trans[...].astype(F32)
    inv_rms = lax.rsqrt(jnp.mean(x * x, axis=1, keepdims=True) + EPSILON)
    gain_o[...] = jnp.sum(grad_normed * x * inv_rms, axis=0, keepdims=True)
    scaled = grad_normed * gain[...]
    back_o[...] = (
        inv_rms * scaled
        - inv_rms * inv_rms * inv_rms * x * jnp.mean(scaled * x, axis=1, keepdims=True)
    ).astype(BF16)


def place_kernel(rows, n_pieces, meta, here, orders, *refs):
    pieces, out = refs[:n_pieces], refs[n_pieces]
    place = meta[0] + lax.broadcasted_iota(jnp.int32, (rows, rows), 0)
    total = here[...].astype(F32)
    for p in range(n_pieces):
        mine = (orders[p : p + 1, :].astype(jnp.int32) == place).astype(F32).astype(BF16)
        total = total + dot(mine, pieces[p][...])
    out[...] = total.astype(BF16)


def call(kernel, outs, scratch, n_smem, name):
    vmem = pl.BlockSpec(memory_space=pltpu.VMEM)
    smem = pl.BlockSpec(memory_space=pltpu.SMEM)

    def run(*args):
        return pl.pallas_call(
            kernel,
            out_shape=[jax.ShapeDtypeStruct(s, t) for s, t in outs],
            in_specs=[smem] * n_smem + [vmem] * (len(args) - n_smem),
            out_specs=[vmem] * len(outs),
            scratch_shapes=[pltpu.VMEM(s, t) for s, t in scratch],
            compiler_params=pltpu.CompilerParams(vmem_limit_bytes=VMEM_BYTES),
            name=name,
        )(*args)

    return run


def swap(block, axis, distance):
    devices = lax.axis_size(axis)
    return lax.ppermute(block, axis, [(i, i ^ distance) for i in range(devices)])


def spread_pieces(block, axis):
    devices, index = lax.axis_size(axis), lax.axis_index(axis)
    if devices == 8:
        across = [block] + [swap(block, axis, d) for d in (2, 4, 6)]
        pieces = across + [swap(part, axis, 1) for part in across]
        return pieces, [index ^ d for d in (0, 2, 4, 6, 1, 3, 5, 7)]
    whole = lax.all_gather(block, axis)
    return [whole[i] for i in range(devices)], [jnp.int32(i) for i in range(devices)]


def from_behind(block, axis, distance):
    devices = range(lax.axis_size(axis))
    route = [(i - distance, i) for i in devices if i - distance in devices]
    return lax.ppermute(block, axis, route)


def shards(
    tokens,
    lengths,
    order,
    norm_gain,
    w_in,
    conv_weight,
    conv_bias,
    w_x,
    w_dt,
    dt_bias,
    a_log,
    d_skip,
    w_out,
    cotangent,
):
    rows, width = tokens.shape[1:]
    inner, rank, state, taps = w_out.shape[0], w_dt.shape[0], a_log.shape[1], conv_weight.shape[1]
    lags, clouds, steps = taps - 1, lengths.shape[1], rows // CHUNKS
    sizes = (rows, width, inner, rank, state, lags, clouds)
    devices, me = lax.axis_size("seq"), lax.axis_index("seq")
    here_x, here_dy = tokens[0], cotangent[0]
    order8 = order.reshape(CHUNKS, steps)
    order_row = order8.T.reshape(1, rows)
    order_rows = jnp.concatenate([order_row // 128, order_row % 128], axis=0).astype(BF16)
    order_rows = jnp.pad(order_rows, ((0, ORDER_ROWS - 2), (0, width - rows)))
    pieces_x, sources = spread_pieces(jnp.concatenate([here_x, order_rows], axis=0), "seq")
    pieces_dy, _ = spread_pieces(here_dy, "seq")
    n = len(pieces_x)
    src = jnp.stack(sources).astype(jnp.int32)
    starts = jnp.cumsum(lengths[0]) - lengths[0]
    meta = jnp.concatenate([(me * rows)[None], starts]).astype(jnp.int32)
    alog_t = a_log.T
    conv_w = conv_weight.T
    w_x_pad = jnp.pad(w_x, ((0, 0), (0, LANES - w_x.shape[1])))
    w_dt_pad = jnp.pad(w_dt, ((0, LANES - rank), (0, 0)))
    row = lambda v: v[None, :]
    big, lane = (rows, inner), (rows, LANES)
    carried = (inner // LANES, state * CHUNKS, LANES)
    spread = (rows, state * LANES)
    ext_rows = rows + lags * CHUNKS
    (trans, normed, gate, ext, conv, act, step, xproj, chunkf, sums, f, orders) = call(
        functools.partial(pre_kernel, sizes, n),
        [
            ((rows, width), BF16),
            ((rows, width), BF16),
            (big, F32),
            ((ext_rows, inner), F32),
            (big, F32),
            (big, BF16),
            (big, F32),
            (lane, F32),
            (carried, F32),
            ((CHUNKS, inner), F32),
            ((state, inner), F32),
            ((n, rows), F32),
        ],
        [
            ((rows + BLOCK, inner), F32),
            ((lags, rows, LANES), F32),
            (big, F32),
            (big, F32),
            (spread, F32),
            ((state, inner), F32),
        ],
        2,
        "forward_local",
    )(meta, src, order8, *pieces_x, row(norm_gain), w_in, conv_w, row(conv_bias), w_x_pad, w_dt_pad, row(dt_bias), alog_t)
    trans_dy, gg, chunkb, carry = call(
        functools.partial(back_kernel, sizes, n),
        [
            ((rows, width), BF16),
            (big, F32),
            (carried, F32),
            ((2 * state + CHUNKS, inner), F32),
        ],
        [
            ((1, rows, LANES), F32),
            (big, F32),
            (big, F32),
            (spread, F32),
            ((state, inner), F32),
        ],
        2,
        "backward_local",
    )(meta, src, order8, *pieces_dy, gate, step, xproj, alog_t, w_out, sums, f)
    carries, _ = spread_pieces(carry, "seq")
    branch, gz, gci, rim, wout_g, wx_g, wdt_g, small, galog = call(
        functools.partial(main_kernel, sizes, n),
        [
            ((rows, width), BF16),
            (big, BF16),
            (big, F32),
            ((CHUNKS, inner), F32),
            ((inner, width), F32),
            ((LANES, inner), F32),
            ((LANES, inner), F32),
            ((CHUNKS, inner), F32),
            ((state, inner), F32),
        ],
        [
            ((lags, rows, LANES), F32),
            (big, F32),
            (big, F32),
            (big, F32),
            (spread, F32),
            (spread, F32),
            ((state, inner), F32),
            ((state, rows + CHUNKS, inner), F32),
            ((state, rows, inner), F32),
            (big, F32),
            (big, F32),
            (big, F32),
            (spread, F32),
            (spread, F32),
            (carried, F32),
            (carried, F32),
            (big, BF16),
            ((n * (2 * state + CHUNKS), inner), F32),
        ],
        2,
        "scan_both",
    )(
        meta, src, *carries, trans_dy, gg, gate, ext, conv, act, step, xproj, chunkf, chunkb, sums, alog_t,
        row(d_skip), w_out, w_x_pad, w_dt_pad, conv_w,
    )
    rim = from_behind(rim, "seq", -1)
    back, win_g, gain_g = call(
        functools.partial(final_kernel, sizes),
        [((rows, width), BF16), ((width, 2 * inner), F32), ((1, width), F32)],
        [],
        0,
        "input_projection_grads",
    )(trans, normed, gci, gz, rim, row(norm_gain), w_in)
    place = call(functools.partial(place_kernel, rows, n), [((rows, width), BF16)], [], 1, "to_hilbert")
    pieces_b, _ = spread_pieces(branch, "seq")
    pieces_g, _ = spread_pieces(back, "seq")
    (output,) = place(meta, here_x, orders, *pieces_b)
    (input_grad,) = place(meta, here_dy, orders, *pieces_g)
    s_gain, s_win, s_wx, s_wdt, s_small, s_alog, s_wout = lax.psum(
        (gain_g, win_g, wx_g[: w_x.shape[1]], wdt_g[:rank], small, galog, wout_g), ("dp", "seq")
    )
    return (
        output[None],
        input_grad[None],
        s_gain[0],
        s_win,
        s_small[3 : 4 + lags].T,
        s_small[2],
        s_wx.T,
        s_wdt,
        s_small[1],
        s_alog.T,
        s_small[0],
        s_wout,
    )


def solution(mesh):
    placed = (
        P("dp", "seq", None),
        P("dp", None),
        P("dp", "seq"),
        P(),
        P(),
        P(),
        P(),
        P(),
        P(),
        P(),
        P(),
        P(),
        P(),
        P("dp", "seq", None),
    )
    return jax.shard_map(
        shards,
        mesh=mesh,
        in_specs=placed,
        out_specs=(
            P("dp", "seq", None),
            P("dp", "seq", None),
            P(),
            P(),
            P(),
            P(),
            P(),
            P(),
            P(),
            P(),
            P(),
            P(),
        ),
        check_vma=False,
    )
```

```python
import functools

import jax
import jax.numpy as jnp
from jax import lax
from jax.experimental import pallas as pl
from jax.experimental.pallas import tpu as pltpu
from jax.sharding import PartitionSpec as P

EPSILON = 1e-05
LOG2E = 1.4426950408889634
FAR = 1e30
CHUNKS = 8
LANES = 128
BLOCK = 16
CUBE = (0, 2, 4, 6, 1, 3, 5, 7)
SENT = (2, 4, 6, 1)
ORDER_ROWS = 16
F32, BF16 = jnp.float32, jnp.bfloat16
VMEM_BYTES = 60 * 1024 * 1024


def dot(a, b, contract=((1,), (0,))):
    return lax.dot_general(a, b, (contract, ((), ())), preferred_element_type=F32)


def wide(tile, width):
    return jnp.concatenate([tile] * (width // LANES), axis=1)


def sigmoid(v):
    return 1.0 / (1.0 + jnp.exp(-v))


def scalars(me, lengths, rows):
    begin, meta = jnp.int32(0), [me[0] * rows]
    for k in range(lengths.shape[1]):
        meta.append(begin)
        begin = begin + lengths[0, k]
    return meta


def source(me, p, n_pieces):
    return jnp.bitwise_xor(me[0], CUBE[p]) if n_pieces == len(CUBE) else jnp.int32(p)


def places(first, rows, r0, steps):
    r = r0 + lax.broadcasted_iota(jnp.int32, (rows, LANES), 0)
    return first + lax.rem(r, CHUNKS) * steps + lax.div(r, CHUNKS)


def cloud_start(meta, clouds, place):
    start = jnp.zeros_like(place)
    for k in range(clouds):
        begin = meta[1 + k]
        start = jnp.maximum(start, jnp.where(begin <= place, begin, 0))
    return start


def fill_valid(valid, meta, clouds, rows, lags):
    steps = rows // CHUNKS

    def body(j, carry):
        r0 = pl.multiple_of(j * BLOCK, BLOCK)
        place = places(meta[0], BLOCK, r0, steps)
        begin = cloud_start(meta, clouds, place)
        for k in range(1, lags + 1):
            valid[k - 1, pl.ds(r0, BLOCK), :] = (place - k >= begin).astype(F32)
        return carry

    lax.fori_loop(0, rows // BLOCK, body, 0)


def row_of_place(rows):
    place = lax.broadcasted_iota(jnp.int32, (rows, rows), 0)
    row = lax.broadcasted_iota(jnp.int32, (rows, rows), 1)
    return (place == lax.rem(row, CHUNKS) * (rows // CHUNKS) + lax.div(row, CHUNKS)).astype(F32).astype(BF16)


def gather_rows(column, pieces, me, rows):
    lane = lax.broadcasted_iota(jnp.int32, (column.shape[0], rows), 1).astype(F32)
    mine = [
        (column - (source(me, p, len(pieces)) * rows).astype(F32) == lane).astype(F32).astype(BF16)
        for p in range(len(pieces))
    ]
    return dot(jnp.concatenate(mine, axis=1), jnp.concatenate(pieces, axis=0))


def fill_broadcast(out, xproj, first, count):
    whole = xproj[...]
    high = whole.astype(BF16)
    low = (whole - high.astype(F32)).astype(BF16)
    row = lax.rem(lax.broadcasted_iota(jnp.int32, (2 * LANES, LANES), 0), LANES)
    for n in range(count):
        pick = (row == first + n).astype(F32).astype(BF16)
        out[:, n * LANES : (n + 1) * LANES] = dot(jnp.concatenate([high, low], axis=1), pick)


def rates(alog):
    return -jnp.exp(alog[...])


def chunk_of(ref, c, count):
    return jnp.concatenate([ref[b, pl.ds(c, count, stride=CHUNKS), :] for b in range(ref.shape[0])], axis=1)


def set_chunk(ref, c, value):
    for b in range(ref.shape[0]):
        ref[b, pl.ds(c, value.shape[0], stride=CHUNKS), :] = value[:, b * LANES : (b + 1) * LANES]


def refs_own(pieces, me, rows, n_pieces):
    if n_pieces == len(CUBE):
        return pieces[0][rows : rows + ORDER_ROWS, :rows]
    digits = jnp.zeros((ORDER_ROWS, rows), F32)
    for p in range(n_pieces):
        part = pieces[p][rows : rows + ORDER_ROWS, :rows].astype(F32)
        digits = jnp.where(me[0] == p, part, digits)
    return digits.astype(BF16)


def pre_kernel(sizes, n_pieces, me, lengths, *refs):
    rows, width, inner, rank, state, lags, clouds = sizes
    steps = rows // CHUNKS
    pieces = refs[:n_pieces]
    (gain, w_in, conv_w, conv_b, w_x, w_dt, dt_b, alog) = refs[n_pieces : n_pieces + 8]
    (trans_o, normed_o, gate_o, ext_o, conv_o, act_o, step_o, xproj_o, chunkf_o, sums_o, f_o, orders_o, column_o) = refs[
        n_pieces + 8 : n_pieces + 21
    ]
    conv_in, valid, far, use, bbc, a2 = refs[n_pieces + 21 :]
    meta = scalars(me, lengths, rows)
    to_row = row_of_place(rows)
    halos = [jnp.full((1, 1), -1.0, F32)] * (lags + 1)
    for p in range(n_pieces):
        row = dot(pieces[p][rows : rows + ORDER_ROWS, :rows], to_row)
        row = row[0:1] * 128.0 + row[1:2]
        orders_o[p : p + 1, :] = row
        behind = source(me, p, n_pieces) == me[0] - 1
        for k in range(1, lags + 1):
            r = (steps - k) * CHUNKS + CHUNKS - 1
            halos[k] = jnp.where(behind, row[:, r : r + 1], halos[k])
    sub = lax.broadcasted_iota(jnp.int32, (BLOCK, LANES), 0)
    extra = jnp.full((BLOCK, LANES), -1.0, F32)
    for k in range(1, lags + 1):
        extra = jnp.where(sub == k, halos[k], extra)
    digits = refs_own(pieces, me, rows, n_pieces)
    both = dot(to_row, digits, ((0,), (1,)))
    own = jnp.broadcast_to(both[:, 0:1] * 128.0 + both[:, 1:2], (rows, LANES))
    column_o[...] = own
    column = jnp.concatenate([own, extra], axis=0)
    trans = gather_rows(wide(column, rows), [p[0:rows, :] for p in pieces], me, rows)
    trans_o[...] = trans[:rows].astype(BF16)
    inv_rms = lax.rsqrt(jnp.mean(trans * trans, axis=1, keepdims=True) + EPSILON)
    normed = (trans * inv_rms * gain[...]).astype(BF16)
    normed_o[...] = normed[:rows]
    conv_in[...] = dot(normed, w_in[:, :inner]).astype(BF16).astype(F32)
    gate_o[...] = dot(normed[:rows], w_in[:, inner:])
    pad = lags * CHUNKS
    ext_o[pad : pad + rows, :] = conv_in[:rows, :]
    first_sub = lax.broadcasted_iota(jnp.int32, (CHUNKS, inner), 0) == 0
    for k in range(1, lags + 1):
        tile = conv_in[(steps - k) * CHUNKS : (steps - k + 1) * CHUNKS, :]
        before = conv_in[rows + k : rows + k + 1, :]
        ext_o[(lags - k) * CHUNKS : (lags - k + 1) * CHUNKS, :] = jnp.where(
            first_sub, before, pltpu.roll(tile, 1, 0)
        )
    fill_valid(valid, meta, clouds, rows, lags)

    def conv_body(j, carry):
        r0 = pl.multiple_of(j * BLOCK, BLOCK)
        out = conv_b[...] + conv_w[lags : lags + 1, :] * ext_o[pl.ds(r0 + pad, BLOCK), :]
        for k in range(1, lags + 1):
            ok = wide(valid[k - 1, pl.ds(r0, BLOCK), :], inner)
            shifted = ext_o[pl.ds(pl.multiple_of(r0 + pad - k * CHUNKS, CHUNKS), BLOCK), :]
            out = out + conv_w[lags - k : lags - k + 1, :] * shifted * ok
        conv_o[pl.ds(r0, BLOCK), :] = out
        act_o[pl.ds(r0, BLOCK), :] = (out * sigmoid(out)).astype(BF16)
        return carry

    lax.fori_loop(0, rows // BLOCK, conv_body, 0)
    xproj = dot(act_o[...], w_x[...])
    xproj_o[...] = xproj
    step_o[...] = dot(xproj.astype(BF16), w_dt[...])

    def step_body(j, carry):
        r0 = pl.multiple_of(j * BLOCK, BLOCK)
        pre = step_o[pl.ds(r0, BLOCK), :] + dt_b[...]
        step = jnp.maximum(pre, 0.0) + jnp.log1p(jnp.exp(-jnp.abs(pre)))
        step_o[pl.ds(r0, BLOCK), :] = step
        keep = wide(valid[0, pl.ds(r0, BLOCK), :], inner)
        distance = jnp.where(keep > 0.5, step, FAR)
        far[pl.ds(r0, BLOCK), :] = distance
        use[pl.ds(r0, BLOCK), :] = step * act_o[pl.ds(r0, BLOCK), :].astype(F32)
        return carry + distance[:CHUNKS] + distance[CHUNKS:]

    sums_o[...] = lax.fori_loop(0, rows // BLOCK, step_body, jnp.zeros((CHUNKS, inner), F32))
    fill_broadcast(bbc, xproj_o, rank, state)
    a2[...] = rates(alog) * LOG2E
    for lb in range(inner // LANES):
        ls = slice(lb * LANES, (lb + 1) * LANES)
        rate = [jnp.broadcast_to(a2[n : n + 1, ls], (CHUNKS, LANES)) for n in range(state)]

        def scan_body(i, states):
            r = pl.ds(pl.multiple_of(i * CHUNKS, CHUNKS), CHUNKS)
            distance, u = far[r, ls], use[r, ls]
            return tuple(
                jnp.exp2(distance * rate[n]) * states[n] + u * bbc[r, n * LANES : (n + 1) * LANES]
                for n in range(state)
            )

        zero = jnp.zeros((CHUNKS, LANES), F32)
        last = lax.fori_loop(0, steps, scan_body, (zero,) * state, unroll=2)
        for n in range(state):
            chunkf_o[lb, n * CHUNKS : (n + 1) * CHUNKS, :] = last[n]
    total = jnp.zeros((state, inner), F32)
    for c in range(CHUNKS):
        total = jnp.exp2(a2[...] * sums_o[c : c + 1, :]) * total + chunk_of(chunkf_o, c, state)
    f_o[...] = total


def back_kernel(sizes, n_pieces, me, lengths, *refs):
    rows, width, inner, rank, state, lags, clouds = sizes
    steps = rows // CHUNKS
    pieces = refs[:n_pieces]
    gate, step, xproj, alog, w_out, sums, f, column = refs[n_pieces : n_pieces + 8]
    n_out = (len(CUBE) - 4 if n_pieces == len(CUBE) else 1)
    dy_o, gg_o, chunkb_o = refs[n_pieces + 8 : n_pieces + 11]
    carries_o = refs[n_pieces + 11 : n_pieces + 11 + n_out]
    valid, far, gm, cbc, a2 = refs[n_pieces + 11 + n_out :]
    meta = scalars(me, lengths, rows)
    trans_dy = gather_rows(wide(column[...], rows), [p[...] for p in pieces], me, rows).astype(BF16)
    dy_o[...] = trans_dy
    gg_o[...] = dot(trans_dy, w_out[...], ((1,), (1,)))
    fill_valid(valid, meta, clouds, rows, 1)

    def body(j, carry):
        r = pl.ds(pl.multiple_of(j * BLOCK, BLOCK), BLOCK)
        z = gate[r, :]
        gm[r, :] = gg_o[r, :] * (z * sigmoid(z))
        far[r, :] = jnp.where(wide(valid[0, r, :], inner) > 0.5, step[r, :], FAR)
        return carry

    lax.fori_loop(0, rows // BLOCK, body, 0)
    fill_broadcast(cbc, xproj, rank + state, state)
    a2[...] = rates(alog) * LOG2E
    for lb in range(inner // LANES):
        ls = slice(lb * LANES, (lb + 1) * LANES)
        rate = [jnp.broadcast_to(a2[n : n + 1, ls], (CHUNKS, LANES)) for n in range(state)]

        def scan_body(k, flows):
            r = pl.ds(pl.multiple_of((steps - 1 - k) * CHUNKS, CHUNKS), CHUNKS)
            distance, g = far[r, ls], gm[r, ls]
            return tuple(
                jnp.exp2(distance * rate[n]) * (flows[n] + g * cbc[r, n * LANES : (n + 1) * LANES])
                for n in range(state)
            )

        zero = jnp.zeros((CHUNKS, LANES), F32)
        last = lax.fori_loop(0, steps, scan_body, (zero,) * state, unroll=2)
        for n in range(state):
            chunkb_o[lb, n * CHUNKS : (n + 1) * CHUNKS, :] = last[n]
    total = jnp.zeros((state, inner), F32)
    for c in reversed(range(CHUNKS)):
        total = jnp.exp2(a2[...] * sums[c : c + 1, :]) * total + chunk_of(chunkb_o, c, state)
    passed = jnp.broadcast_to(jnp.sum(sums[...], axis=0, keepdims=True), (CHUNKS, inner))
    if n_out == 1:
        carries_o[0][:state, :] = f[...]
        carries_o[0][state : 2 * state, :] = total
        carries_o[0][2 * state :, :] = passed
        return
    for out, d in zip(carries_o, SENT):
        later = jnp.bitwise_xor(me[0], d) > me[0]
        out[:state, :] = jnp.where(later, f[...], total)
        out[state:, :] = passed


def core_of(me, devices):
    return jnp.bitwise_and(me, 1) if devices == len(CUBE) else jnp.int32(0)


def main_kernel(sizes, n_pieces, me_ref, lengths, *refs):
    rows, width, inner, rank, state, lags, clouds = sizes
    steps = rows // CHUNKS
    carries = refs[:n_pieces]
    (trans_dy, normed, gg, gate, ext, conv, act, step, xproj, chunkf, chunkb, sums, alog, skip, w_out, w_x, w_dt, conv_w) = refs[
        n_pieces : n_pieces + 18
    ]
    (branch_o, gz_o, gci_o, rim_o, keep_o, send_o, small_o) = refs[n_pieces + 18 : n_pieces + 25]
    (valid, far, use, gm, bbc, cbc, a2, states, decays, mixed, gs, lamb, gb, gc, sstart, gstart, gated, held) = refs[
        n_pieces + 25 :
    ]
    meta = scalars(me_ref, lengths, rows)
    me = me_ref[0]
    devices = len(CUBE) if n_pieces == len(CUBE) - 1 else n_pieces
    a2[...] = rates(alog) * LOG2E
    state_in = jnp.zeros((state, inner), F32)
    flow_in = jnp.zeros((state, inner), F32)
    size = carries[0].shape[0]
    back = size - CHUNKS - state
    for p in range(n_pieces):
        whence = source(me_ref, p + 1, devices) if devices > n_pieces else p
        held[pl.ds(pl.multiple_of(whence * size, CHUNKS), size), :] = carries[p][...]

    def ahead(s, flow):
        base = pl.multiple_of(s * size, CHUNKS)
        p_s = jnp.exp2(a2[...] * held[pl.ds(base + size - CHUNKS, 1), :])
        return jnp.where(s < me, p_s * flow + held[pl.ds(base, state), :], flow)

    state_in = lax.fori_loop(0, devices, ahead, state_in)

    def behind(k, flow):
        s = devices - 1 - k
        base = pl.multiple_of(s * size, CHUNKS)
        p_s = jnp.exp2(a2[...] * held[pl.ds(base + size - CHUNKS, 1), :])
        return jnp.where(s > me, p_s * flow + held[pl.ds(pl.multiple_of(base + back, CHUNKS), state), :], flow)

    flow_in = lax.fori_loop(0, devices, behind, flow_in)
    now = state_in
    for c in range(CHUNKS):
        set_chunk(sstart, c, now)
        now = jnp.exp2(a2[...] * sums[c : c + 1, :]) * now + chunk_of(chunkf, c, state)
    now = flow_in
    for c in reversed(range(CHUNKS)):
        set_chunk(gstart, c, now)
        now = jnp.exp2(a2[...] * sums[c : c + 1, :]) * now + chunk_of(chunkb, c, state)
    fill_valid(valid, meta, clouds, rows, lags)

    def prepare(j, carry):
        r = pl.ds(pl.multiple_of(j * BLOCK, BLOCK), BLOCK)
        z = gate[r, :]
        gm[r, :] = gg[r, :] * (z * sigmoid(z))
        far[r, :] = jnp.where(wide(valid[0, r, :], inner) > 0.5, step[r, :], FAR)
        use[r, :] = step[r, :] * act[r, :].astype(F32)
        return carry

    lax.fori_loop(0, rows // BLOCK, prepare, 0)
    fill_broadcast(bbc, xproj, rank, state)
    fill_broadcast(cbc, xproj, rank + state, state)
    for lb in range(inner // LANES):
        ls = slice(lb * LANES, (lb + 1) * LANES)
        rate = [jnp.broadcast_to(a2[n : n + 1, ls], (CHUNKS, LANES)) for n in range(state)]
        begin = []
        for n in range(state):
            tile = sstart[lb, n * CHUNKS : (n + 1) * CHUNKS, :]
            states[n, 0:CHUNKS, ls] = tile
            begin.append(tile)

        def forward(i, now):
            r0 = pl.multiple_of(i * CHUNKS, CHUNKS)
            r = pl.ds(r0, CHUNKS)
            after = pl.ds(pl.multiple_of(r0 + CHUNKS, CHUNKS), CHUNKS)
            distance, u = far[r, ls], use[r, ls]
            new, out = [], None
            for n in range(state):
                decay = jnp.exp2(distance * rate[n])
                value = decay * now[n] + u * bbc[r, n * LANES : (n + 1) * LANES]
                decays[n, r, ls] = decay
                states[n, after, ls] = value
                part = value * cbc[r, n * LANES : (n + 1) * LANES]
                out = part if out is None else out + part
                new.append(value)
            mixed[r, ls] = out
            return tuple(new)

        lax.fori_loop(0, steps, forward, tuple(begin), unroll=2)

    def gating(j, carry):
        r = pl.ds(pl.multiple_of(j * BLOCK, BLOCK), BLOCK)
        z, a = gate[r, :], act[r, :].astype(F32)
        s = sigmoid(z)
        m = mixed[r, :] + skip[...] * a
        gated[r, :] = (m * (z * s)).astype(BF16)
        gz_o[r, :] = (gg[r, :] * m * s * (1.0 + z * (1.0 - s))).astype(BF16)
        part = gm[r, :] * a
        return carry + part[:CHUNKS] + part[CHUNKS:]

    skip_sum = lax.fori_loop(0, rows // BLOCK, gating, jnp.zeros((CHUNKS, inner), F32))
    branch_o[...] = dot(gated[...], w_out[...]).astype(BF16)
    wout_g = dot(trans_dy[...], gated[...], ((0,), (0,))).astype(BF16)
    gate_g = dot(normed[...], gz_o[...], ((0,), (0,))).astype(BF16)
    second = core_of(me, devices) == 1
    keep_o[...] = jnp.where(second, gate_g, wout_g)
    send_o[...] = jnp.where(second, wout_g, gate_g)
    group = 3
    pair = 4
    for lg in range(inner // LANES // group):
        lanes = [slice((lg * group + k) * LANES, (lg * group + k + 1) * LANES) for k in range(group)]
        for ng in range(state // pair):
            ns = [ng * pair + k for k in range(pair)]
            rate = [[jnp.broadcast_to(a2[n : n + 1, ls] * (1.0 / LOG2E), (CHUNKS, LANES)) for ls in lanes] for n in ns]
            begin = [gstart[lg * group + k, n * CHUNKS : (n + 1) * CHUNKS, :] for n in ns for k in range(group)]
            zero = jnp.zeros((CHUNKS, LANES), F32)

            def backward(k, carry):
                flows, sums_a = carry
                r0 = pl.multiple_of((steps - 1 - k) * CHUNKS, CHUNKS)
                r = pl.ds(r0, CHUNKS)
                after = pl.ds(pl.multiple_of(r0 + CHUNKS, CHUNKS), CHUNKS)
                gs_t = [None] * group
                lamb_t = [None] * group
                g_t = [gm[r, ls] for ls in lanes]
                u_t = [use[r, ls] for ls in lanes]
                d_t = [step[r, ls] for ls in lanes]
                new_flows, new_sums = [], []
                for q, n in enumerate(ns):
                    b = bbc[r, n * LANES : (n + 1) * LANES]
                    c = cbc[r, n * LANES : (n + 1) * LANES]
                    gb_t = gc_t = None
                    for x, ls in enumerate(lanes):
                        lam = g_t[x] * c + flows[q * group + x]
                        flow = decays[n, r, ls] * lam
                        part = flow * states[n, r, ls]
                        one, two = part * rate[q][x], lam * b
                        gs_t[x] = one if gs_t[x] is None else gs_t[x] + one
                        lamb_t[x] = two if lamb_t[x] is None else lamb_t[x] + two
                        three, four = lam * u_t[x], g_t[x] * states[n, after, ls]
                        gb_t = three if gb_t is None else gb_t + three
                        gc_t = four if gc_t is None else gc_t + four
                        new_flows.append(flow)
                        new_sums.append(sums_a[q * group + x] + part * d_t[x])
                    nl = slice(n * LANES, (n + 1) * LANES)
                    if lg == 0:
                        gb[r, nl] = gb_t
                        gc[r, nl] = gc_t
                    else:
                        gb[r, nl] += gb_t
                        gc[r, nl] += gc_t
                for x, ls in enumerate(lanes):
                    if ng == 0:
                        gs[r, ls] = gs_t[x]
                        lamb[r, ls] = lamb_t[x]
                    else:
                        gs[r, ls] += gs_t[x]
                        lamb[r, ls] += lamb_t[x]
                return tuple(new_flows), tuple(new_sums)

            flows, sums_a = lax.fori_loop(
                0, steps, backward, (tuple(begin), (zero,) * (pair * group))
            )
            for q, n in enumerate(ns):
                for x, ls in enumerate(lanes):
                    small_o[n : n + 1, ls] = (
                        jnp.sum(sums_a[q * group + x], axis=0, keepdims=True) * rate[q][x][0:1]
                    )
    col = lax.broadcasted_iota(jnp.int32, (state * LANES, LANES), 1)
    row = lax.div(lax.broadcasted_iota(jnp.int32, (state * LANES, LANES), 0), LANES)
    pick_b = (col == row + rank).astype(F32).astype(BF16)
    pick_c = (col == row + rank + state).astype(F32).astype(BF16)

    def lane_sums(ref, pick):
        whole = ref[...]
        high = whole.astype(BF16)
        low = (whole - high.astype(F32)).astype(BF16)
        return dot(high, pick) + dot(low, pick)

    grad_bc = lane_sums(gb, pick_b) + lane_sums(gc, pick_c)
    gpre = gated

    def pre_body(j, carry):
        r = pl.ds(pl.multiple_of(j * BLOCK, BLOCK), BLOCK)
        grad_step = gs[r, :] + lamb[r, :] * act[r, :].astype(F32)
        grad_pre = (grad_step * (1.0 - jnp.exp(-step[r, :]))).astype(BF16)
        gpre[r, :] = grad_pre
        part = grad_pre.astype(F32)
        return carry + part[:CHUNKS] + part[CHUNKS:]

    dt_sum = lax.fori_loop(0, rows // BLOCK, pre_body, jnp.zeros((CHUNKS, inner), F32))
    dt_low = xproj[...].astype(BF16)
    wdt_g = dot(dt_low, gpre[...], ((0,), (0,)))
    grad_xproj = (dot(gpre[...], w_dt[...], ((1,), (1,))) + grad_bc).astype(BF16)
    wx_g = dot(grad_xproj, act[...], ((0,), (0,)))
    at = state
    small_o[at : at + rank + 2 * state, :] = wx_g[: rank + 2 * state]
    at += rank + 2 * state
    small_o[at : at + rank, :] = wdt_g[:rank]
    at += rank
    gs[...] = dot(grad_xproj, w_x[...], ((1,), (1,)))
    gconv = mixed

    def conv_body(j, carry):
        r0 = pl.multiple_of(j * BLOCK, BLOCK)
        r = pl.ds(r0, BLOCK)
        grad_act = gm[r, :] * skip[...] + lamb[r, :] * step[r, :] + gs[r, :]
        v = conv[r, :]
        s = sigmoid(v)
        grad = grad_act * (s * (1.0 + v * (1.0 - s)))
        gconv[r, :] = grad
        new = [carry[0] + grad[:CHUNKS] + grad[CHUNKS:]]
        for k in range(lags + 1):
            masked = grad if k == 0 else grad * wide(valid[k - 1, r, :], inner)
            part = masked * ext[pl.ds(pl.multiple_of(r0 + (lags - k) * CHUNKS, CHUNKS), BLOCK), :]
            new.append(carry[1 + k] + part[:CHUNKS] + part[CHUNKS:])
        return tuple(new)

    conv_sums = lax.fori_loop(
        0, rows // BLOCK, conv_body, (jnp.zeros((CHUNKS, inner), F32),) * (lags + 2)
    )
    small = [skip_sum, dt_sum, conv_sums[0]] + [conv_sums[1 + lags - t] for t in range(lags + 1)]
    for k, part in enumerate(small):
        small_o[at + k : at + k + 1, :] = jnp.sum(part, axis=0, keepdims=True)
    small_o[at + len(small) :, :] = jnp.zeros((small_o.shape[0] - at - len(small), inner), F32)

    def masked_tile(i, k):
        r = pl.ds(pl.multiple_of(i * CHUNKS, CHUNKS), CHUNKS)
        tile = gconv[r, :] * conv_w[lags - k : lags - k + 1, :]
        return tile if k == 0 else tile * wide(valid[k - 1, r, :], inner)

    def spread(i, carry):
        total = masked_tile(i, 0)
        for k in range(1, lags + 1):
            total = total + masked_tile(i + k, k)
        gci_o[pl.ds(pl.multiple_of(i * CHUNKS, CHUNKS), CHUNKS), :] = total
        return carry

    lax.fori_loop(0, steps - lags, spread, 0)
    sub = lax.broadcasted_iota(jnp.int32, (CHUNKS, inner), 0)
    for i in range(steps - lags, steps):
        total = masked_tile(i, 0)
        for k in range(1, lags + 1):
            if i + k < steps:
                total = total + masked_tile(i + k, k)
            else:
                moved = pltpu.roll(masked_tile(i + k - steps, k), CHUNKS - 1, 0)
                total = total + jnp.where(sub == CHUNKS - 1, 0.0, moved)
        gci_o[i * CHUNKS : (i + 1) * CHUNKS, :] = total
    rim_o[...] = jnp.zeros((CHUNKS, inner), F32)
    for b in range(1, lags + 1):
        total = jnp.zeros((1, inner), F32)
        for k in range(b, lags + 1):
            total = total + masked_tile(k - b, k)[0:1]
        rim_o[b : b + 1, :] = total


def final_kernel(sizes, devices, me, trans, normed, gci, gz, rim, small, gain, w_in, back_o, keep_o, send_o, both):
    rows, width, inner, rank, state, lags, clouds = sizes
    steps = rows // CHUNKS
    r = lax.broadcasted_iota(jnp.int32, (rows, inner), 0)
    total = gci[...]
    for k in range(1, lags + 1):
        total = total + jnp.where(r == (steps - k) * CHUNKS + CHUNKS - 1, rim[k : k + 1, :], 0.0)
    grad_ci = total.astype(BF16)
    grad_z = gz[...]
    grad_normed = dot(grad_ci, w_in[:, :inner], ((1,), (1,))) + dot(grad_z, w_in[:, inner:], ((1,), (1,)))
    x = trans[...].astype(F32)
    inv_rms = lax.rsqrt(jnp.mean(x * x, axis=1, keepdims=True) + EPSILON)
    scaled = grad_normed * gain[...]
    back_o[...] = (
        inv_rms * scaled
        - inv_rms * inv_rms * inv_rms * x * jnp.mean(scaled * x, axis=1, keepdims=True)
    ).astype(BF16)
    both[0:width, :] = dot(normed[...], grad_ci, ((0,), (0,))).astype(BF16)
    gain_row = jnp.sum(grad_normed * x * inv_rms, axis=0, keepdims=True)
    gain_row = jnp.concatenate([gain_row, jnp.zeros((1, inner - width), F32)], axis=1)
    n_small = small.shape[0]
    last = lax.broadcasted_iota(jnp.int32, (n_small, inner), 0) == n_small - 1
    both[width : width + n_small, :] = jnp.where(last, gain_row, small[...]).astype(BF16)
    half = keep_o.shape[0]
    core = core_of(me[0], devices)
    keep_o[...] = both[pl.ds(pl.multiple_of(core * half, BLOCK), half), :]
    send_o[...] = both[pl.ds(pl.multiple_of((1 - core) * half, BLOCK), half), :]


def halves_kernel(me, kept, got, own_o, *sent_o):
    part = own_o.shape[0]
    chip = lax.div(me[0], 2)
    for d, out in enumerate((own_o,) + sent_o):
        r = pl.ds(pl.multiple_of(jnp.bitwise_xor(chip, d) * part, BLOCK), part)
        out[...] = (kept[r, :].astype(F32) + got[r, :].astype(F32)).astype(BF16)


def sum_kernel(a, b, c, d, out):
    out[...] = ((a[...].astype(F32) + b[...].astype(F32)) + (c[...].astype(F32) + d[...].astype(F32))).astype(BF16)


def unpack_kernel(sizes, n_pieces, n_small, me, *refs):
    rows, width, inner, rank, state, lags, clouds = sizes
    one, two = refs[:n_pieces], refs[n_pieces : 2 * n_pieces]
    win_o, wout_o, small_o, all_one, all_two = refs[2 * n_pieces :]
    for pieces, whole in ((one, all_one), (two, all_two)):
        part = pieces[0].shape[0]
        for p, piece in enumerate(pieces):
            s = source(me, p, n_pieces)
            if n_pieces == len(CUBE):
                s = jnp.bitwise_and(s, 1) * (n_pieces // 2) + lax.div(s, 2)
            whole[pl.ds(pl.multiple_of(s * part, BLOCK), part), :] = piece[...]
    wout_o[...] = all_one[0:width, :].astype(F32).T
    win_o[:, inner:] = all_one[width : 2 * width, :].astype(F32)
    win_o[:, :inner] = all_two[0:width, :].astype(F32)
    small_o[...] = all_two[width : width + n_small, :].astype(F32)


def place_kernel(rows, n_pieces, me, here, orders, *refs):
    pieces, out = refs[:n_pieces], refs[n_pieces]
    place = (me[0] * rows + lax.broadcasted_iota(jnp.int32, (rows, rows), 0)).astype(F32)
    mine = [(orders[p : p + 1, :] == place).astype(F32).astype(BF16) for p in range(n_pieces)]
    moved = dot(jnp.concatenate(mine, axis=1), jnp.concatenate([p[...] for p in pieces], axis=0))
    out[...] = (here[...].astype(F32) + moved).astype(BF16)


def call(kernel, outs, scratch, n_smem, name):
    vmem = pl.BlockSpec(memory_space=pltpu.VMEM)
    smem = pl.BlockSpec(memory_space=pltpu.SMEM)

    def run(*args):
        return pl.pallas_call(
            kernel,
            out_shape=[jax.ShapeDtypeStruct(s, t) for s, t in outs],
            in_specs=[smem] * n_smem + [vmem] * (len(args) - n_smem),
            out_specs=[vmem] * len(outs),
            scratch_shapes=[pltpu.VMEM(s, t) for s, t in scratch],
            compiler_params=pltpu.CompilerParams(vmem_limit_bytes=VMEM_BYTES),
            name=name,
        )(*args)

    return run


def swap(block, axis, distance):
    devices = lax.axis_size(axis)
    return lax.ppermute(block, axis, [(i, i ^ distance) for i in range(devices)])


def spread_pieces(block, axis):
    devices = lax.axis_size(axis)
    if devices == len(CUBE):
        across = [block] + [swap(block, axis, d) for d in CUBE[1:4]]
        return across + [swap(part, axis, 1) for part in across]
    whole = lax.all_gather(block, axis)
    return [whole[i] for i in range(devices)]


def spread_carries(blocks, axis):
    if len(blocks) == 1:
        return spread_pieces(blocks[0], axis)
    across = [swap(block, axis, d) for block, d in zip(blocks, SENT)]
    return across[:3] + [across[3]] + [swap(part, axis, 1) for part in across[:3]]


def total_pieces(kept, sent):
    if lax.axis_size("seq") != len(CUBE) or lax.axis_size("dp") != 4:
        return [lax.psum(half.astype(F32), ("dp", "seq")).astype(BF16) for half in (kept, sent)]
    me = lax.axis_index("seq").astype(jnp.int32)[None]
    part = (kept.shape[0] // 4, kept.shape[1])
    got = swap(sent, "seq", 1)
    own, *away = call(halves_kernel, [(part, BF16)] * 4, [], 1, "add_halves")(me, kept, got)
    add = call(sum_kernel, [(part, BF16)], [], 0, "add_parts")
    (mine,) = add(own, *[swap(block, "seq", 2 * d) for d, block in zip((1, 2, 3), away)])
    (mine,) = add(mine, *[swap(mine, "dp", d) for d in (1, 2, 3)])
    return spread_pieces(mine, "seq")


def from_behind(block, axis, distance):
    devices = range(lax.axis_size(axis))
    route = [(i - distance, i) for i in devices if i - distance in devices]
    return lax.ppermute(block, axis, route)


def shards(
    tokens,
    lengths,
    order,
    norm_gain,
    w_in,
    conv_weight,
    conv_bias,
    w_x,
    w_dt,
    dt_bias,
    a_log,
    d_skip,
    w_out,
    cotangent,
):
    rows, width = tokens.shape[1:]
    inner, rank, state, taps = w_out.shape[0], w_dt.shape[0], a_log.shape[1], conv_weight.shape[1]
    lags, clouds, steps = taps - 1, lengths.shape[1], rows // CHUNKS
    sizes = (rows, width, inner, rank, state, lags, clouds)
    devices = lax.axis_size("seq")
    me = lax.axis_index("seq").astype(jnp.int32)[None]
    here_x, here_dy = tokens[0], cotangent[0]
    digits = jnp.concatenate([order >> 7, order & 127], axis=0).astype(BF16)
    digits = jnp.pad(digits, ((0, ORDER_ROWS - 2), (0, width - rows)))
    pieces_x = spread_pieces(jnp.concatenate([here_x, digits], axis=0), "seq")
    pieces_dy = spread_pieces(here_dy, "seq")
    n = len(pieces_x)
    alog_t = a_log.T
    conv_w = conv_weight.T
    w_x_pad = jnp.pad(w_x, ((0, 0), (0, LANES - w_x.shape[1])))
    w_dt_pad = jnp.pad(w_dt, ((0, LANES - rank), (0, 0)))
    row = lambda v: v[None, :]
    big, lane = (rows, inner), (rows, LANES)
    carried = (inner // LANES, state * CHUNKS, LANES)
    spread = (rows, state * LANES)
    ext_rows = rows + lags * CHUNKS
    (trans, normed, gate, ext, conv, act, step, xproj, chunkf, sums, f, orders, column) = call(
        functools.partial(pre_kernel, sizes, n),
        [
            ((rows, width), BF16),
            ((rows, width), BF16),
            (big, F32),
            ((ext_rows, inner), F32),
            (big, F32),
            (big, BF16),
            (big, F32),
            (lane, F32),
            (carried, F32),
            ((CHUNKS, inner), F32),
            ((state, inner), F32),
            ((n, rows), F32),
            (lane, F32),
        ],
        [
            ((rows + BLOCK, inner), F32),
            ((lags, rows, LANES), F32),
            (big, F32),
            (big, F32),
            (spread, F32),
            ((state, inner), F32),
        ],
        2,
        "forward_local",
    )(me, lengths, *pieces_x, row(norm_gain), w_in, conv_w, row(conv_bias), w_x_pad, w_dt_pad, row(dt_bias), alog_t)
    carry_rows = (state + CHUNKS, 2 * state + CHUNKS)[n != len(CUBE)]
    n_sent = (len(SENT), 1)[n != len(CUBE)]
    trans_dy, gg, chunkb, *carries = call(
        functools.partial(back_kernel, sizes, n),
        [((rows, width), BF16), (big, F32), (carried, F32)] + [((carry_rows, inner), F32)] * n_sent,
        [
            ((1, rows, LANES), F32),
            (big, F32),
            (big, F32),
            (spread, F32),
            ((state, inner), F32),
        ],
        2,
        "backward_local",
    )(me, lengths, *pieces_dy, gate, step, xproj, alog_t, w_out, sums, f, column)
    carries = spread_carries(carries, "seq")
    n_small = state + (rank + 2 * state) + rank + 3 + taps + 1
    branch, gz, gci, rim, keep, send, small = call(
        functools.partial(main_kernel, sizes, len(carries)),
        [
            ((rows, width), BF16),
            (big, BF16),
            (big, F32),
            ((CHUNKS, inner), F32),
            ((width, inner), BF16),
            ((width, inner), BF16),
            ((n_small, inner), F32),
        ],
        [
            ((lags, rows, LANES), F32),
            (big, F32),
            (big, F32),
            (big, F32),
            (spread, F32),
            (spread, F32),
            ((state, inner), F32),
            ((state, rows + CHUNKS, inner), F32),
            ((state, rows, inner), F32),
            (big, F32),
            (big, F32),
            (big, F32),
            (spread, F32),
            (spread, F32),
            (carried, F32),
            (carried, F32),
            (big, BF16),
            ((n * carry_rows, inner), F32),
        ],
        2,
        "scan_both",
    )(
        me, lengths, *carries, trans_dy, normed, gg, gate, ext, conv, act, step, xproj, chunkf, chunkb, sums, alog_t,
        row(d_skip), w_out, w_x_pad, w_dt_pad, conv_w,
    )
    rim = from_behind(rim, "seq", -1)
    one = total_pieces(keep, send)
    half = -(-(width + n_small) // (8 * BLOCK)) * (4 * BLOCK)
    back, keep, send = call(
        functools.partial(final_kernel, sizes, devices),
        [((rows, width), BF16), ((half, inner), BF16), ((half, inner), BF16)],
        [((2 * half, inner), BF16)],
        1,
        "input_projection_grads",
    )(me, trans, normed, gci, gz, rim, small, row(norm_gain), w_in)
    place = call(functools.partial(place_kernel, rows, n), [((rows, width), BF16)], [], 1, "to_hilbert")
    pieces_b = spread_pieces(branch, "seq")
    (output,) = place(me, here_x, orders, *pieces_b)
    pieces_g = spread_pieces(back, "seq")
    two = total_pieces(keep, send)
    (input_grad,) = place(me, here_dy, orders, *pieces_g)
    win_g, wout_g, small = call(
        functools.partial(unpack_kernel, sizes, len(one), n_small),
        [((width, 2 * inner), F32), ((inner, width), F32), ((n_small, inner), F32)],
        [((2 * width, inner), BF16), ((2 * half, inner), BF16)],
        1,
        "unpack_sums",
    )(me, *one, *two)
    cuts = [state, rank + 2 * state, rank, 1, 1, 1, taps]
    at = [sum(cuts[:k]) for k in range(len(cuts) + 1)]
    g_alog, g_wx, g_wdt, g_skip, g_dtb, g_convb, g_taps = [small[at[k] : at[k + 1]] for k in range(len(cuts))]
    return (
        output[None],
        input_grad[None],
        small[n_small - 1, :width],
        win_g,
        g_taps.T,
        g_convb[0],
        g_wx.T,
        g_wdt,
        g_dtb[0],
        g_alog.T,
        g_skip[0],
        wout_g,
    )


def solution(mesh):
    placed = (
        P("dp", "seq", None),
        P("dp", None),
        P("dp", "seq"),
        P(),
        P(),
        P(),
        P(),
        P(),
        P(),
        P(),
        P(),
        P(),
        P(),
        P("dp", "seq", None),
    )
    return jax.shard_map(
        shards,
        mesh=mesh,
        in_specs=placed,
        out_specs=(
            P("dp", "seq", None),
            P("dp", "seq", None),
            P(),
            P(),
            P(),
            P(),
            P(),
            P(),
            P(),
            P(),
            P(),
            P(),
        ),
        check_vma=False,
    )
```

```python
import functools

import jax
import jax.numpy as jnp
from jax import lax
from jax.experimental import pallas as pl
from jax.experimental.pallas import tpu as pltpu
from jax.sharding import PartitionSpec as P

EPSILON = 1e-05
LOG2E = 1.4426950408889634
FAR = 1e30
CHUNKS = 8
LANES = 128
BLOCK = 16
CUBE = (0, 2, 4, 6, 1, 3, 5, 7)
SENT = (2, 4, 6, 1)
ORDER_ROWS = 16
F32, BF16 = jnp.float32, jnp.bfloat16
MIB = 1024 * 1024


def dot(a, b, contract=((1,), (0,))):
    return lax.dot_general(a, b, (contract, ((), ())), preferred_element_type=F32)


def as_row(ref):
    return ref[...].reshape(1, ref.shape[0])


def wide(tile, width):
    return jnp.concatenate([tile] * (width // LANES), axis=1)


def sigmoid(v):
    return 1.0 / (1.0 + jnp.exp(-v))


def scalars(me, lengths, rows):
    begin, meta = jnp.int32(0), [me[0] * rows]
    for k in range(lengths.shape[1]):
        meta.append(begin)
        begin = begin + lengths[0, k]
    return meta


def source(me, p, n_pieces):
    return jnp.bitwise_xor(me[0], CUBE[p]) if n_pieces == len(CUBE) else jnp.int32(p)


def places(first, rows, r0, steps):
    r = r0 + lax.broadcasted_iota(jnp.int32, (rows, LANES), 0)
    return first + lax.rem(r, CHUNKS) * steps + lax.div(r, CHUNKS)


def cloud_start(meta, clouds, place):
    start = jnp.zeros_like(place)
    for k in range(clouds):
        begin = meta[1 + k]
        start = jnp.maximum(start, jnp.where(begin <= place, begin, 0))
    return start


def fill_valid(valid, meta, clouds, rows, lags):
    steps = rows // CHUNKS

    def body(j, carry):
        r0 = pl.multiple_of(j * BLOCK, BLOCK)
        place = places(meta[0], BLOCK, r0, steps)
        begin = cloud_start(meta, clouds, place)
        for k in range(1, lags + 1):
            valid[k - 1, pl.ds(r0, BLOCK), :] = (place - k >= begin).astype(F32)
        return carry

    lax.fori_loop(0, rows // BLOCK, body, 0)


def row_of_place(rows):
    place = lax.broadcasted_iota(jnp.int32, (rows, rows), 0)
    row = lax.broadcasted_iota(jnp.int32, (rows, rows), 1)
    return (place == lax.rem(row, CHUNKS) * (rows // CHUNKS) + lax.div(row, CHUNKS)).astype(F32).astype(BF16)


def gather_rows(column, pieces, me, rows):
    lane = lax.broadcasted_iota(jnp.int32, (column.shape[0], rows), 1).astype(F32)
    mine = [
        (column - (source(me, p, len(pieces)) * rows).astype(F32) == lane).astype(F32).astype(BF16)
        for p in range(len(pieces))
    ]
    return dot(jnp.concatenate(mine, axis=1), jnp.concatenate(pieces, axis=0))


def fill_broadcast(out, xproj, first, count):
    whole = xproj[...]
    high = whole.astype(BF16)
    low = (whole - high.astype(F32)).astype(BF16)
    row = lax.rem(lax.broadcasted_iota(jnp.int32, (2 * LANES, LANES), 0), LANES)
    for n in range(count):
        pick = (row == first + n).astype(F32).astype(BF16)
        out[:, n * LANES : (n + 1) * LANES] = dot(jnp.concatenate([high, low], axis=1), pick)


def rates(alog):
    return -jnp.exp(alog[...])


def chunk_of(ref, c, count):
    return jnp.concatenate([ref[b, pl.ds(c, count, stride=CHUNKS), :] for b in range(ref.shape[0])], axis=1)


def set_chunk(ref, c, value):
    for b in range(ref.shape[0]):
        ref[b, pl.ds(c, value.shape[0], stride=CHUNKS), :] = value[:, b * LANES : (b + 1) * LANES]


def refs_own(pieces, me, rows, n_pieces):
    if n_pieces == len(CUBE):
        return pieces[0][rows : rows + ORDER_ROWS, :rows]
    digits = jnp.zeros((ORDER_ROWS, rows), F32)
    for p in range(n_pieces):
        part = pieces[p][rows : rows + ORDER_ROWS, :rows].astype(F32)
        digits = jnp.where(me[0] == p, part, digits)
    return digits.astype(BF16)


def pre_kernel(sizes, n_pieces, n_far, me, *refs):
    rows, width, inner, rank, state, lags, clouds = sizes
    steps = rows // CHUNKS
    pieces = refs[:n_pieces]
    far_refs, refs = refs[n_pieces : n_pieces + n_far], refs[:n_pieces] + refs[n_pieces + n_far :]
    near_refs, copied, refs = refs[-n_far - 1 : -1], refs[-1], refs[: -n_far - 1]
    copies = [pltpu.make_async_copy(a, b, copied.at[k]) for k, (a, b) in enumerate(zip(far_refs, near_refs))]
    for copy in copies:
        copy.start()
    (lengths, gain, w_in, conv_w, conv_b, w_x, w_dt, dt_b, alog, skip) = near_refs
    (trans_o, normed_o, gate_o, ext_o, conv_o, act_o, step_o, xproj_o, chunkf_o, sums_o, f_o, orders_o, column_o,
     valid, far, use, bbc, wx_o, wdt_o, a2, rows_o, conv_in) = refs[n_pieces:]
    to_row = row_of_place(rows)
    halos = [jnp.full((1, 1), -1.0, F32)] * (lags + 1)
    for p in range(n_pieces):
        row = dot(pieces[p][rows : rows + ORDER_ROWS, :rows], to_row)
        row = row[0:1] * 128.0 + row[1:2]
        orders_o[p : p + 1, :] = row
        behind = source(me, p, n_pieces) == me[0] - 1
        for k in range(1, lags + 1):
            r = (steps - k) * CHUNKS + CHUNKS - 1
            halos[k] = jnp.where(behind, row[:, r : r + 1], halos[k])
    sub = lax.broadcasted_iota(jnp.int32, (BLOCK, LANES), 0)
    extra = jnp.full((BLOCK, LANES), -1.0, F32)
    for k in range(1, lags + 1):
        extra = jnp.where(sub == k, halos[k], extra)
    digits = refs_own(pieces, me, rows, n_pieces)
    both = dot(to_row, digits, ((0,), (1,)))
    own = jnp.broadcast_to(both[:, 0:1] * 128.0 + both[:, 1:2], (rows, LANES))
    column_o[...] = own
    column = jnp.concatenate([own, extra], axis=0)
    trans = gather_rows(wide(column, rows), [p[0:rows, :] for p in pieces], me, rows)
    trans_o[...] = trans[:rows].astype(BF16)
    for copy in copies:
        copy.wait()
    meta = scalars(me, lengths, rows)
    bias, dt_bias = as_row(conv_b), as_row(dt_b)
    rows_o[0 : lags + 1, :] = conv_w[...]
    rows_o[lags + 1 : lags + 2, :] = as_row(skip)
    inv_rms = lax.rsqrt(jnp.mean(trans * trans, axis=1, keepdims=True) + EPSILON)
    normed = (trans * inv_rms * as_row(gain)).astype(BF16)
    normed_o[...] = normed[:rows]
    conv_in[...] = dot(normed, w_in[:, :inner]).astype(BF16).astype(F32)
    gate_o[...] = dot(normed[:rows], w_in[:, inner:])
    pad = lags * CHUNKS
    ext_o[pad : pad + rows, :] = conv_in[:rows, :]
    first_sub = lax.broadcasted_iota(jnp.int32, (CHUNKS, inner), 0) == 0
    for k in range(1, lags + 1):
        tile = conv_in[(steps - k) * CHUNKS : (steps - k + 1) * CHUNKS, :]
        before = conv_in[rows + k : rows + k + 1, :]
        ext_o[(lags - k) * CHUNKS : (lags - k + 1) * CHUNKS, :] = jnp.where(
            first_sub, before, pltpu.roll(tile, 1, 0)
        )
    for thin, full in ((w_x, wx_o), (w_dt, wdt_o)):
        blank = jnp.zeros((LANES - thin.shape[0], inner), F32)
        full[...] = jnp.concatenate([thin[...].astype(F32), blank], axis=0).astype(BF16)
    fill_valid(valid, meta, clouds, rows, lags)

    def conv_body(j, carry):
        r0 = pl.multiple_of(j * BLOCK, BLOCK)
        out = bias + conv_w[lags : lags + 1, :] * ext_o[pl.ds(r0 + pad, BLOCK), :]
        for k in range(1, lags + 1):
            ok = wide(valid[k - 1, pl.ds(r0, BLOCK), :], inner)
            shifted = ext_o[pl.ds(pl.multiple_of(r0 + pad - k * CHUNKS, CHUNKS), BLOCK), :]
            out = out + conv_w[lags - k : lags - k + 1, :] * shifted * ok
        conv_o[pl.ds(r0, BLOCK), :] = out
        act_o[pl.ds(r0, BLOCK), :] = (out * sigmoid(out)).astype(BF16)
        return carry

    lax.fori_loop(0, rows // BLOCK, conv_body, 0)
    xproj = dot(act_o[...], wx_o[...], ((1,), (1,)))
    xproj_o[...] = xproj
    step_o[...] = dot(xproj.astype(BF16), wdt_o[...])

    def step_body(j, carry):
        r0 = pl.multiple_of(j * BLOCK, BLOCK)
        pre = step_o[pl.ds(r0, BLOCK), :] + dt_bias
        step = jnp.maximum(pre, 0.0) + jnp.log1p(jnp.exp(-jnp.abs(pre)))
        step_o[pl.ds(r0, BLOCK), :] = step
        keep = wide(valid[0, pl.ds(r0, BLOCK), :], inner)
        distance = jnp.where(keep > 0.5, step, FAR)
        far[pl.ds(r0, BLOCK), :] = distance
        use[pl.ds(r0, BLOCK), :] = step * act_o[pl.ds(r0, BLOCK), :].astype(F32)
        return carry + distance[:CHUNKS] + distance[CHUNKS:]

    sums_o[...] = lax.fori_loop(0, rows // BLOCK, step_body, jnp.zeros((CHUNKS, inner), F32))
    fill_broadcast(bbc, xproj_o, rank, state)
    a2[...] = rates(alog) * LOG2E
    for lb in range(inner // LANES):
        ls = slice(lb * LANES, (lb + 1) * LANES)
        rate = [jnp.broadcast_to(a2[n : n + 1, ls], (CHUNKS, LANES)) for n in range(state)]

        def scan_body(i, states):
            r = pl.ds(pl.multiple_of(i * CHUNKS, CHUNKS), CHUNKS)
            distance, u = far[r, ls], use[r, ls]
            return tuple(
                jnp.exp2(distance * rate[n]) * states[n] + u * bbc[r, n * LANES : (n + 1) * LANES]
                for n in range(state)
            )

        zero = jnp.zeros((CHUNKS, LANES), F32)
        last = lax.fori_loop(0, steps, scan_body, (zero,) * state, unroll=2)
        for n in range(state):
            chunkf_o[lb, n * CHUNKS : (n + 1) * CHUNKS, :] = last[n]
    total = jnp.zeros((state, inner), F32)
    for c in range(CHUNKS):
        total = jnp.exp2(a2[...] * sums_o[c : c + 1, :]) * total + chunk_of(chunkf_o, c, state)
    f_o[...] = total


def back_kernel(sizes, n_pieces, me, *refs):
    rows, width, inner, rank, state, lags, clouds = sizes
    steps = rows // CHUNKS
    pieces = refs[:n_pieces]
    gate, far, xproj, a2, w_out, sums, f, column = refs[n_pieces : n_pieces + 8]
    n_out = (len(CUBE) - 4 if n_pieces == len(CUBE) else 1)
    dy_o, gg_o, gm, cbc, chunkb_o = refs[n_pieces + 8 : n_pieces + 13]
    carries_o = refs[n_pieces + 13 : n_pieces + 13 + n_out]
    near_out, copied = refs[n_pieces + 13 + n_out :]
    copy = pltpu.make_async_copy(w_out, near_out, copied)
    copy.start()
    trans_dy = gather_rows(wide(column[...], rows), [p[...] for p in pieces], me, rows).astype(BF16)
    dy_o[...] = trans_dy
    copy.wait()
    gg_o[...] = dot(trans_dy, near_out[...], ((1,), (1,)))

    def body(j, carry):
        r = pl.ds(pl.multiple_of(j * BLOCK, BLOCK), BLOCK)
        z = gate[r, :]
        gm[r, :] = gg_o[r, :] * (z * sigmoid(z))
        return carry

    lax.fori_loop(0, rows // BLOCK, body, 0)
    fill_broadcast(cbc, xproj, rank + state, state)
    for lb in range(inner // LANES):
        ls = slice(lb * LANES, (lb + 1) * LANES)
        rate = [jnp.broadcast_to(a2[n : n + 1, ls], (CHUNKS, LANES)) for n in range(state)]

        def scan_body(k, flows):
            r = pl.ds(pl.multiple_of((steps - 1 - k) * CHUNKS, CHUNKS), CHUNKS)
            distance, g = far[r, ls], gm[r, ls]
            return tuple(
                jnp.exp2(distance * rate[n]) * (flows[n] + g * cbc[r, n * LANES : (n + 1) * LANES])
                for n in range(state)
            )

        zero = jnp.zeros((CHUNKS, LANES), F32)
        last = lax.fori_loop(0, steps, scan_body, (zero,) * state, unroll=2)
        for n in range(state):
            chunkb_o[lb, n * CHUNKS : (n + 1) * CHUNKS, :] = last[n]
    total = jnp.zeros((state, inner), F32)
    for c in reversed(range(CHUNKS)):
        total = jnp.exp2(a2[...] * sums[c : c + 1, :]) * total + chunk_of(chunkb_o, c, state)
    passed = jnp.broadcast_to(jnp.sum(sums[...], axis=0, keepdims=True), (CHUNKS, inner))
    if n_out == 1:
        carries_o[0][:state, :] = f[...]
        carries_o[0][state : 2 * state, :] = total
        carries_o[0][2 * state :, :] = passed
        return
    for out, d in zip(carries_o, SENT):
        later = jnp.bitwise_xor(me[0], d) > me[0]
        out[:state, :] = jnp.where(later, f[...], total)
        out[state:, :] = passed


def core_of(me, devices):
    return jnp.bitwise_and(me, 1) if devices == len(CUBE) else jnp.int32(0)


def hold_carries(held, carries, me):
    n_pieces, size = len(carries), carries[0].shape[0]
    devices = len(CUBE) if n_pieces == len(CUBE) - 1 else n_pieces
    for p in range(n_pieces):
        whence = source(me, p + 1, devices) if devices > n_pieces else p
        held[pl.ds(pl.multiple_of(whence * size, CHUNKS), size), :] = carries[p][...]
    return devices


def scan_forward_kernel(sizes, n_pieces, me_ref, *refs):
    rows, width, inner, rank, state, lags, clouds = sizes
    steps = rows // CHUNKS
    carries = refs[:n_pieces]
    (trans_dy, normed, gg, gate, act, far, use, bbc, cbc, chunkf, sums, a2, consts, w_out) = refs[n_pieces : n_pieces + 14]
    blocks = inner // LANES
    states = refs[n_pieces + 14 : n_pieces + 14 + blocks]
    (branch_o, gz_o, keep_o, send_o) = refs[n_pieces + 14 + blocks : n_pieces + 18 + blocks]
    (mixed, sstart, gated, held) = refs[n_pieces + 18 + blocks :]
    me = me_ref[0]
    skips = consts[lags + 1 : lags + 2, :]
    size = carries[0].shape[0]
    devices = hold_carries(held, carries, me_ref)

    def ahead(s, flow):
        base = pl.multiple_of(s * size, CHUNKS)
        p_s = jnp.exp2(a2[...] * held[pl.ds(base + size - CHUNKS, 1), :])
        return jnp.where(s < me, p_s * flow + held[pl.ds(base, state), :], flow)

    now = lax.fori_loop(0, devices, ahead, jnp.zeros((state, inner), F32))
    for c in range(CHUNKS):
        set_chunk(sstart, c, now)
        now = jnp.exp2(a2[...] * sums[c : c + 1, :]) * now + chunk_of(chunkf, c, state)

    for lb in range(inner // LANES):
        ls = slice(lb * LANES, (lb + 1) * LANES)
        rate = [jnp.broadcast_to(a2[n : n + 1, ls], (CHUNKS, LANES)) for n in range(state)]
        begin = []
        for n in range(state):
            tile = sstart[lb, n * CHUNKS : (n + 1) * CHUNKS, :]
            states[lb][n, 0:CHUNKS, :] = tile
            begin.append(tile)

        def forward(i, now):
            r0 = pl.multiple_of(i * CHUNKS, CHUNKS)
            r = pl.ds(r0, CHUNKS)
            nxt = pl.ds(pl.multiple_of(r0 + CHUNKS, CHUNKS), CHUNKS)
            distance, u = far[r, ls], use[r, ls]
            new, out = [], None
            for n in range(state):
                value = jnp.exp2(distance * rate[n]) * now[n] + u * bbc[r, n * LANES : (n + 1) * LANES]
                states[lb][n, nxt, :] = value
                part = value * cbc[r, n * LANES : (n + 1) * LANES]
                out = part if out is None else out + part
                new.append(value)
            mixed[r, ls] = out
            return tuple(new)

        lax.fori_loop(0, steps, forward, tuple(begin), unroll=2)

    def gating(j, carry):
        r = pl.ds(pl.multiple_of(j * BLOCK, BLOCK), BLOCK)
        z, a = gate[r, :], act[r, :].astype(F32)
        s = sigmoid(z)
        m = mixed[r, :] + skips * a
        gated[r, :] = (m * (z * s)).astype(BF16)
        gz_o[r, :] = (gg[r, :] * m * s * (1.0 + z * (1.0 - s))).astype(BF16)
        return carry

    lax.fori_loop(0, rows // BLOCK, gating, 0)
    branch_o[...] = dot(gated[...], w_out[...]).astype(BF16)
    second = core_of(me, devices) == 1
    wout_g = dot(trans_dy[...], gated[...], ((0,), (0,))).astype(BF16)
    gate_g = dot(normed[...], gz_o[...], ((0,), (0,))).astype(BF16)
    keep_o[...] = jnp.where(second, gate_g, wout_g)
    send_o[...] = jnp.where(second, wout_g, gate_g)


def adjoint_carries_kernel(sizes, n_pieces, me_ref, *refs):
    rows, width, inner, rank, state, lags, clouds = sizes
    carries = refs[:n_pieces]
    chunkb, sums, a2, gstart, held = refs[n_pieces:]
    me = me_ref[0]
    size = carries[0].shape[0]
    back = size - CHUNKS - state
    devices = hold_carries(held, carries, me_ref)

    def behind(k, flow):
        s = devices - 1 - k
        base = pl.multiple_of(s * size, CHUNKS)
        p_s = jnp.exp2(a2[...] * held[pl.ds(base + size - CHUNKS, 1), :])
        return jnp.where(s > me, p_s * flow + held[pl.ds(pl.multiple_of(base + back, CHUNKS), state), :], flow)

    now = lax.fori_loop(0, devices, behind, jnp.zeros((state, inner), F32))
    for c in reversed(range(CHUNKS)):
        set_chunk(gstart, c, now)
        now = jnp.exp2(a2[...] * sums[c : c + 1, :]) * now + chunk_of(chunkb, c, state)


def scan_backward_kernel(sizes, *refs):
    rows, width, inner, rank, state, lags, clouds = sizes
    steps = rows // CHUNKS
    states, refs = refs[: inner // LANES], refs[inner // LANES :]
    (gstart, far, use, bbc, cbc, gm, step, act, conv, valid, a2, conv_w, w_x, w_dt) = refs[:14]
    (gconv, rim_o, gpre, gxproj_o, galog_o) = refs[14:19]
    (gs, lamb, gb, gc) = refs[19:]
    skips = conv_w[lags + 1 : lags + 2, :]
    group, pair = 3, 4
    for lg in range(inner // LANES // group):
        lanes = [slice((lg * group + k) * LANES, (lg * group + k + 1) * LANES) for k in range(group)]
        for ng in range(state // pair):
            ns = [ng * pair + k for k in range(pair)]
            rate = [[jnp.broadcast_to(a2[n : n + 1, ls], (CHUNKS, LANES)) for ls in lanes] for n in ns]
            begin = [gstart[lg * group + k, n * CHUNKS : (n + 1) * CHUNKS, :] for n in ns for k in range(group)]
            zero = jnp.zeros((CHUNKS, LANES), F32)

            def backward(k, carry):
                flows, sums_a = carry
                r0 = pl.multiple_of((steps - 1 - k) * CHUNKS, CHUNKS)
                r = pl.ds(r0, CHUNKS)
                nxt = pl.ds(pl.multiple_of(r0 + CHUNKS, CHUNKS), CHUNKS)
                gs_t = [None] * group
                lamb_t = [None] * group
                g_t = [gm[r, ls] for ls in lanes]
                u_t = [use[r, ls] for ls in lanes]
                d_t = [step[r, ls] for ls in lanes]
                f_t = [far[r, ls] for ls in lanes]
                new_flows, new_sums = [], []
                for q, n in enumerate(ns):
                    b = bbc[r, n * LANES : (n + 1) * LANES]
                    c = cbc[r, n * LANES : (n + 1) * LANES]
                    gb_t = gc_t = None
                    for x, ls in enumerate(lanes):
                        lam = g_t[x] * c + flows[q * group + x]
                        flow = jnp.exp2(f_t[x] * rate[q][x]) * lam
                        part = flow * states[lg * group + x][n, r, :]
                        one, two = part * rate[q][x], lam * b
                        gs_t[x] = one if gs_t[x] is None else gs_t[x] + one
                        lamb_t[x] = two if lamb_t[x] is None else lamb_t[x] + two
                        three, four = lam * u_t[x], g_t[x] * states[lg * group + x][n, nxt, :]
                        gb_t = three if gb_t is None else gb_t + three
                        gc_t = four if gc_t is None else gc_t + four
                        new_flows.append(flow)
                        new_sums.append(sums_a[q * group + x] + part * d_t[x])
                    nl = slice(n * LANES, (n + 1) * LANES)
                    if lg == 0:
                        gb[r, nl] = gb_t
                        gc[r, nl] = gc_t
                    else:
                        gb[r, nl] += gb_t
                        gc[r, nl] += gc_t
                for x, ls in enumerate(lanes):
                    if ng == 0:
                        gs[r, ls] = gs_t[x]
                        lamb[r, ls] = lamb_t[x]
                    else:
                        gs[r, ls] += gs_t[x]
                        lamb[r, ls] += lamb_t[x]
                return tuple(new_flows), tuple(new_sums)

            flows, sums_a = lax.fori_loop(
                0, steps, backward, (tuple(begin), (zero,) * (pair * group))
            )
            for q, n in enumerate(ns):
                for x, ls in enumerate(lanes):
                    galog_o[n : n + 1, ls] = (
                        jnp.sum(sums_a[q * group + x], axis=0, keepdims=True) * rate[q][x][0:1] * (1.0 / LOG2E)
                    )
    col = lax.broadcasted_iota(jnp.int32, (state * LANES, LANES), 1)
    row = lax.div(lax.broadcasted_iota(jnp.int32, (state * LANES, LANES), 0), LANES)
    pick_b = (col == row + rank).astype(F32).astype(BF16)
    pick_c = (col == row + rank + state).astype(F32).astype(BF16)

    def lane_sums(ref, pick):
        whole = ref[...]
        high = whole.astype(BF16)
        low = (whole - high.astype(F32)).astype(BF16)
        return dot(high, pick) + dot(low, pick)

    grad_bc = lane_sums(gb, pick_b) + lane_sums(gc, pick_c)

    def pre_body(j, carry):
        r = pl.ds(pl.multiple_of(j * BLOCK, BLOCK), BLOCK)
        grad_step = gs[r, :] * (1.0 / LOG2E) + lamb[r, :] * act[r, :].astype(F32)
        gpre[r, :] = (grad_step * (1.0 - jnp.exp(-step[r, :]))).astype(BF16)
        return carry

    lax.fori_loop(0, rows // BLOCK, pre_body, 0)
    grad_xproj = (dot(gpre[...], w_dt[...], ((1,), (1,))) + grad_bc).astype(BF16)
    gxproj_o[...] = grad_xproj
    gs[...] = dot(grad_xproj, w_x[...])

    def conv_body(j, carry):
        r = pl.ds(pl.multiple_of(j * BLOCK, BLOCK), BLOCK)
        grad_act = gm[r, :] * skips + lamb[r, :] * step[r, :] + gs[r, :]
        v = conv[r, :]
        s = sigmoid(v)
        gconv[r, :] = grad_act * (s * (1.0 + v * (1.0 - s)))
        return carry

    lax.fori_loop(0, rows // BLOCK, conv_body, 0)
    rim_o[...] = jnp.zeros((CHUNKS, inner), F32)
    for b in range(1, lags + 1):
        total = jnp.zeros((1, inner), F32)
        for k in range(b, lags + 1):
            total = total + masked_tile(gconv, valid, conv_w, k - b, k, lags)[0:1]
        rim_o[b : b + 1, :] = total


def masked_tile(gconv, valid, conv_w, i, k, lags):
    r = pl.ds(pl.multiple_of(i * CHUNKS, CHUNKS), CHUNKS)
    tile = gconv[r, :] * conv_w[lags - k : lags - k + 1, :]
    return tile if k == 0 else tile * wide(valid[k - 1, r, :], tile.shape[1])


def small_kernel(sizes, gpre, gxproj, xproj, act, gconv, ext, valid, gm, conv_w, galog, small_o, gci_o):
    rows, width, inner, rank, state, lags, clouds = sizes
    steps = rows // CHUNKS

    def spread(i, carry):
        total = masked_tile(gconv, valid, conv_w, i, 0, lags)
        for k in range(1, lags + 1):
            total = total + masked_tile(gconv, valid, conv_w, i + k, k, lags)
        gci_o[pl.ds(pl.multiple_of(i * CHUNKS, CHUNKS), CHUNKS), :] = total
        return carry

    lax.fori_loop(0, steps - lags, spread, 0)
    sub = lax.broadcasted_iota(jnp.int32, (CHUNKS, inner), 0)
    for i in range(steps - lags, steps):
        total = masked_tile(gconv, valid, conv_w, i, 0, lags)
        for k in range(1, lags + 1):
            if i + k < steps:
                total = total + masked_tile(gconv, valid, conv_w, i + k, k, lags)
            else:
                moved = pltpu.roll(masked_tile(gconv, valid, conv_w, i + k - steps, k, lags), CHUNKS - 1, 0)
                total = total + jnp.where(sub == CHUNKS - 1, 0.0, moved)
        gci_o[i * CHUNKS : (i + 1) * CHUNKS, :] = total

    def sum_body(j, carry):
        r0 = pl.multiple_of(j * BLOCK, BLOCK)
        r = pl.ds(r0, BLOCK)
        grad = gconv[r, :]
        parts = [gm[r, :] * act[r, :].astype(F32), gpre[r, :].astype(F32), grad]
        for k in reversed(range(lags + 1)):
            masked = grad if k == 0 else grad * wide(valid[k - 1, r, :], inner)
            parts.append(masked * ext[pl.ds(pl.multiple_of(r0 + (lags - k) * CHUNKS, CHUNKS), BLOCK), :])
        return tuple(total + part[:CHUNKS] + part[CHUNKS:] for total, part in zip(carry, parts))

    sums = lax.fori_loop(0, rows // BLOCK, sum_body, (jnp.zeros((CHUNKS, inner), F32),) * (lags + 4))
    small_o[0:state, :] = galog[...]
    at = state
    small_o[at : at + rank + 2 * state, :] = dot(gxproj[...], act[...], ((0,), (0,)))[: rank + 2 * state]
    at += rank + 2 * state
    small_o[at : at + rank, :] = dot(xproj[...].astype(BF16), gpre[...], ((0,), (0,)))[:rank]
    at += rank
    for k, part in enumerate(sums):
        small_o[at + k : at + k + 1, :] = jnp.sum(part, axis=0, keepdims=True)
    at += len(sums)
    small_o[at:, :] = jnp.zeros((small_o.shape[0] - at, inner), F32)


def final_kernel(sizes, devices, me, trans, normed, gci, gz, rim, small, gain, w_in, back_o, keep_o, send_o, both):
    rows, width, inner, rank, state, lags, clouds = sizes
    steps = rows // CHUNKS
    r = lax.broadcasted_iota(jnp.int32, (rows, inner), 0)
    total = gci[...]
    for k in range(1, lags + 1):
        total = total + jnp.where(r == (steps - k) * CHUNKS + CHUNKS - 1, rim[k : k + 1, :], 0.0)
    grad_ci = total.astype(BF16)
    grad_z = gz[...]
    grad_normed = dot(grad_ci, w_in[:, :inner], ((1,), (1,))) + dot(grad_z, w_in[:, inner:], ((1,), (1,)))
    x = trans[...].astype(F32)
    inv_rms = lax.rsqrt(jnp.mean(x * x, axis=1, keepdims=True) + EPSILON)
    scaled = grad_normed * as_row(gain)
    back_o[...] = (
        inv_rms * scaled
        - inv_rms * inv_rms * inv_rms * x * jnp.mean(scaled * x, axis=1, keepdims=True)
    ).astype(BF16)
    both[0:width, :] = dot(normed[...], grad_ci, ((0,), (0,))).astype(BF16)
    gain_row = jnp.sum(grad_normed * x * inv_rms, axis=0, keepdims=True)
    gain_row = jnp.concatenate([gain_row, jnp.zeros((1, inner - width), F32)], axis=1)
    n_small = small.shape[0]
    last = lax.broadcasted_iota(jnp.int32, (n_small, inner), 0) == n_small - 1
    both[width : width + n_small, :] = jnp.where(last, gain_row, small[...]).astype(BF16)
    half = keep_o.shape[0]
    core = core_of(me[0], devices)
    keep_o[...] = both[pl.ds(pl.multiple_of(core * half, BLOCK), half), :]
    send_o[...] = both[pl.ds(pl.multiple_of((1 - core) * half, BLOCK), half), :]


def small_rows(sizes):
    rows, width, inner, rank, state, lags, clouds = sizes
    return state + (rank + 2 * state) + rank + 3 + lags + 1 + 1


def halves_kernel(me, kept, got, own_o, *sent_o):
    part = own_o.shape[0]
    chip = lax.div(me[0], 2)
    for d, out in enumerate((own_o,) + sent_o):
        r = pl.ds(pl.multiple_of(jnp.bitwise_xor(chip, d) * part, BLOCK), part)
        out[...] = (kept[r, :].astype(F32) + got[r, :].astype(F32)).astype(BF16)


def beside(out, rows):
    half, width = rows.shape[0] // 2, rows.shape[1]
    out[0:half, 0:width] = rows[0:half, :]
    out[0:half, width:] = rows[half:, :]


def unfold(piece, rows, width):
    if piece.shape == (rows, width):
        return piece[...]
    half = rows // 2
    return jnp.concatenate([piece[0:half, 0:width], piece[0:half, width : 2 * width]], axis=0)


def halves_beside_kernel(me, kept, got, rows, own_o, *sent_o):
    part = own_o.shape[0]
    half = rows.shape[0] // 2
    chip = lax.div(me[0], 2)
    for d, out in enumerate((own_o,) + sent_o):
        r = pl.ds(pl.multiple_of(jnp.bitwise_xor(chip, d) * part, BLOCK), part)
        total = (kept[r, :].astype(F32) + got[r, :].astype(F32)).astype(BF16)
        if d == 0:
            out[...] = total
        else:
            beside(out, rows)
            out[half:, :] = total


def sum_kernel(a, b, c, d, out):
    one, two, three, four = (x[x.shape[0] - a.shape[0] :, :].astype(F32) for x in (a, b, c, d))
    out[...] = ((one + two) + (three + four)).astype(BF16)


def sum_beside_kernel(a, b, c, d, rows, out):
    beside(out, rows)
    sum_kernel(a, b, c, d, out.at[pl.ds(rows.shape[0] // 2, a.shape[0])])


def unpack_kernel(sizes, n_pieces, me, *refs):
    rows, width, inner, rank, state, lags, clouds = sizes
    one, two = refs[:n_pieces], refs[n_pieces : 2 * n_pieces]
    (gain_o, win_o, taps_o, convb_o, wx_o, wdt_o, dtb_o, alog_o, skip_o, wout_o) = refs[2 * n_pieces : 2 * n_pieces + 10]
    all_one, all_two = refs[2 * n_pieces + 10 :]
    for pieces, whole in ((one, all_one), (two, all_two)):
        part = whole.shape[0] // n_pieces
        for p, piece in enumerate(pieces):
            s = source(me, p, n_pieces)
            if n_pieces == len(CUBE):
                s = jnp.bitwise_and(s, 1) * (n_pieces // 2) + lax.div(s, 2)
            whole[pl.ds(pl.multiple_of(s * part, BLOCK), part), :] = piece[piece.shape[0] - part :, :]
    wout_o[...] = all_one[0:width, :].astype(F32).T
    win_o[:, inner:] = all_one[width : 2 * width, :].astype(F32)
    win_o[:, :inner] = all_two[0:width, :].astype(F32)
    n_small = small_rows(sizes)
    small = all_two[width : width + n_small, :].astype(F32)
    alog_o[...] = small[0:state]
    at = state
    wx_o[...] = small[at : at + rank + 2 * state]
    at += rank + 2 * state
    wdt_o[...] = small[at : at + rank]
    at += rank
    for k, out in enumerate((skip_o, dtb_o, convb_o)):
        out[...] = small[at + k : at + k + 1].reshape(inner)
    at += 3
    taps_o[...] = small[at : at + lags + 1]
    gain_o[...] = small[n_small - 1 : n_small, :width].reshape(width)


def place_kernel(rows, n_pieces, me, here, orders, *refs):
    pieces, out = refs[:n_pieces], refs[n_pieces]
    place = (me[0] * rows + lax.broadcasted_iota(jnp.int32, (rows, rows), 0)).astype(F32)
    mine = [(orders[p : p + 1, :] == place).astype(F32).astype(BF16) for p in range(n_pieces)]
    moved = dot(jnp.concatenate(mine, axis=1), jnp.concatenate([unfold(p, rows, out.shape[1]) for p in pieces], axis=0))
    out[...] = (here[...].astype(F32) + moved).astype(BF16)


def call(kernel, outs, scratch, n_smem, name, room, time=1.0, far_ins=()):
    vmem = pl.BlockSpec(memory_space=pltpu.VMEM)
    smem = pl.BlockSpec(memory_space=pltpu.SMEM)
    anywhere = pl.BlockSpec(memory_space=pltpu.HBM)

    def run(*args):
        args = [pltpu.with_memory_space_constraint(v, pltpu.HBM) if k in far_ins else v for k, v in enumerate(args)]
        return pl.pallas_call(
            kernel,
            out_shape=[jax.ShapeDtypeStruct(*part) if isinstance(part, tuple) else part for part in outs],
            in_specs=[smem if k < n_smem else anywhere if k in far_ins else vmem for k in range(len(args))],
            out_specs=[vmem] * len(outs),
            scratch_shapes=[pltpu.VMEM(*part) if isinstance(part, tuple) else part for part in scratch],
            compiler_params=pltpu.CompilerParams(vmem_limit_bytes=room * MIB),
            cost_estimate=pl.CostEstimate(
                flops=1, bytes_accessed=1, transcendentals=0
            ),
            name=name,
        )(*args)

    return run


def after(value, *others):
    return lax.optimization_barrier((value, others))[0]


def swap(block, axis, distance):
    devices = lax.axis_size(axis)
    return lax.ppermute(block, axis, [(i, i ^ distance) for i in range(devices)])


def spread_pieces(block, axis, then=None):
    devices = lax.axis_size(axis)
    if devices == len(CUBE):
        across = [block] + [swap(block, axis, d) for d in CUBE[1:4]]
        if then is not None:
            then = after(then, across[3])
        pieces = across + [swap(part, axis, 1) for part in across]
    else:
        whole = lax.all_gather(block, axis)
        pieces = [whole[i] for i in range(devices)]
    return pieces if then is None else (pieces, then)


def spread_carries(blocks, axis):
    if len(blocks) == 1:
        return spread_pieces(blocks[0], axis)
    across = [swap(block, axis, d) for block, d in zip(blocks, SENT)]
    return across[:3] + [across[3]] + [swap(part, axis, 1) for part in across[:3]]


def from_behind(block, axis, distance):
    devices = range(lax.axis_size(axis))
    route = [(i - distance, i) for i in devices if i - distance in devices]
    return lax.ppermute(block, axis, route)


def shards(
    tokens,
    lengths,
    order,
    norm_gain,
    w_in,
    conv_weight,
    conv_bias,
    w_x,
    w_dt,
    dt_bias,
    a_log,
    d_skip,
    w_out,
    cotangent,
):
    rows, width = tokens.shape[1:]
    inner, rank, state, taps = w_out.shape[0], w_dt.shape[0], a_log.shape[1], conv_weight.shape[1]
    lags, clouds, steps = taps - 1, lengths.shape[1], rows // CHUNKS
    sizes = (rows, width, inner, rank, state, lags, clouds)
    devices = lax.axis_size("seq")
    me = lax.axis_index("seq").astype(jnp.int32)[None]
    here_x, here_dy = tokens[0], cotangent[0]
    digits = jnp.concatenate([order >> 7, order & 127], axis=0).astype(BF16)
    digits = jnp.pad(digits, ((0, ORDER_ROWS - 2), (0, width - rows)))
    weights = (lengths, norm_gain, w_in, conv_weight.T, conv_bias, w_x.T, w_dt, dt_bias, a_log.T, d_skip)
    pieces_x, here_dy = spread_pieces(jnp.concatenate([here_x, digits], axis=0), "seq", then=here_dy)
    pieces_dy = spread_pieces(here_dy, "seq")
    n = len(pieces_x)
    big, lane = (rows, inner), (rows, LANES)
    carried = (inner // LANES, state * CHUNKS, LANES)
    spread = (rows, state * LANES)
    ext_rows = rows + lags * CHUNKS
    (trans, normed, gate, ext, conv, act, step, xproj, chunkf, sums, f, orders, column, valid, far, use, bbc, w_x_pad, w_dt_pad, a2, row_consts) = call(
        functools.partial(pre_kernel, sizes, n, len(weights)),
        [
            ((rows, width), BF16),
            ((rows, width), BF16),
            (big, F32),
            ((ext_rows, inner), F32),
            (big, F32),
            (big, BF16),
            (big, F32),
            (lane, F32),
            (carried, F32),
            ((CHUNKS, inner), F32),
            ((state, inner), F32),
            ((n, rows), F32),
            (lane, F32),
            ((lags, rows, LANES), F32),
            (big, F32),
            (big, F32),
            (spread, F32),
            ((LANES, inner), BF16),
            ((LANES, inner), BF16),
            ((state, inner), F32),
            ((lags + 2, inner), F32),
        ],
        [((rows + BLOCK, inner), F32), pltpu.SMEM(lengths.shape, jnp.int32)]
        + [(v.shape, v.dtype) for v in weights[1:]]
        + [pltpu.SemaphoreType.DMA((len(weights),))],
        1,
        "forward_local",
        24,
        9,
        far_ins=tuple(range(n + 1, n + 1 + len(weights))),
    )(me, *pieces_x, *weights)
    carry_rows = (state + CHUNKS, 2 * state + CHUNKS)[n != len(CUBE)]
    n_sent = (len(SENT), 1)[n != len(CUBE)]
    trans_dy, gg, gm, cbc, chunkb, *carries = call(
        functools.partial(back_kernel, sizes, n),
        [((rows, width), BF16), (big, F32), (big, F32), (spread, F32), (carried, F32)]
        + [((carry_rows, inner), F32)] * n_sent,
        [(w_out.shape, w_out.dtype), pltpu.SemaphoreType.DMA],
        1,
        "backward_local",
        20,
        7,
        far_ins=(n + 5,),
    )(me, *pieces_dy, gate, far, xproj, a2, w_out, sums, f, column)
    carries = spread_carries(carries, "seq")
    n_small = small_rows(sizes)
    held = ((n * carry_rows, inner), F32)
    kept = [pltpu.VMEM((state, rows + CHUNKS, LANES), F32)] * (inner // LANES)
    *states, branch, gz, keep, send = call(
        functools.partial(scan_forward_kernel, sizes, len(carries)),
        [*kept, ((rows, width), BF16), (big, BF16), ((width, inner), BF16), ((width, inner), BF16)],
        [(big, F32), (carried, F32), (big, BF16), held],
        1,
        "scan_forward",
        18,
        7,
    )(me, *carries, trans_dy, normed, gg, gate, act, far, use, bbc, cbc, chunkf, sums, a2, row_consts, w_out)
    cube = n == len(CUBE) and lax.axis_size("dp") == 4
    first = (keep, send)
    half_one, half_two = width, -(-(width + n_small) // (8 * BLOCK)) * (4 * BLOCK)
    got = swap(send, "seq", 1) if cube else None
    (gstart,) = call(
        functools.partial(adjoint_carries_kernel, sizes, len(carries)),
        [(carried, F32)],
        [held],
        1,
        "adjoint_carries",
        8,
        1.5,
    )(me, *carries, chunkb, sums, a2)
    if cube:
        part_one = half_one // 4
        beside_one = ((rows // 2 + part_one, inner), BF16)
        own_one, *sent = call(
            halves_beside_kernel, [((part_one, inner), BF16)] + [beside_one] * 3, [], 1, "add_halves_beside_rows", 8
        )(me, keep, got, branch)
        away_one = [swap(block, "seq", d) for block, d in zip(sent, SENT)]
    gconv, rim, gpre, gxproj, galog = call(
        functools.partial(scan_backward_kernel, sizes),
        [(big, F32), ((CHUNKS, inner), F32), (big, BF16), (lane, BF16), ((state, inner), F32)],
        [(big, F32), (big, F32), (spread, F32), (spread, F32)],
        0,
        "scan_backward",
        20,
        14,
    )(*[pltpu.with_memory_space_constraint(part, pltpu.VMEM) for part in states], gstart, far, use, bbc, cbc, gm, step, act, conv, valid, a2, row_consts, w_x_pad, w_dt_pad)
    rim = from_behind(rim, "seq", -1)
    small, gci = call(
        functools.partial(small_kernel, sizes),
        [((n_small, inner), F32), (big, F32)],
        [],
        0,
        "small_grads",
        16,
        1.6,
    )(after(gpre, *away_one) if cube else gpre, gxproj, xproj, act, gconv, ext, valid, gm, row_consts, galog)
    back, keep, send = call(
        functools.partial(final_kernel, sizes, devices),
        [((rows, width), BF16), ((half_two, inner), BF16), ((half_two, inner), BF16)],
        [((2 * half_two, inner), BF16)],
        1,
        "input_projection_grads",
        16,
    )(me, trans, normed, gci, gz, rim, small, norm_gain, w_in)
    place = call(functools.partial(place_kernel, rows, n), [((rows, width), BF16)], [], 1, "to_hilbert", 12, 1.4)
    if cube:
        part_two = half_two // 4
        adds_one = call(sum_kernel, [((part_one, inner), BF16)], [], 0, "add_parts", 4)
        adds_two = call(sum_kernel, [((part_two, inner), BF16)], [], 0, "add_parts", 4)
        got = swap(send, "seq", 1)
        (one,) = adds_one(own_one, *away_one)
        pieces_b = [branch, *away_one]
        pieces_b += [swap(part, "seq", 1) for part in pieces_b]
        own_two, *sent = call(halves_kernel, [((part_two, inner), BF16)] * 4, [], 1, "add_halves", 4)(me, keep, got)
        away_two = [swap(block, "seq", d) for block, d in zip(sent, SENT)]
        one = after(one, own_two)
        z_one = [swap(one, "dp", d) for d in (1, 2, 3)]
        (two,) = adds_two(own_two, *away_two)
        z_two = [swap(two, "dp", d) for d in (1, 2, 3)]
        (output,) = place(me, after(here_x, two), orders, *pieces_b)
        (one,) = call(sum_beside_kernel, [beside_one], [], 0, "add_parts_beside_rows", 8)(
            one, *z_one, after(back, two)
        )
        pieces_g = spread_pieces(one, "seq")
        (two,) = adds_two(two, *z_two)
        totals = (pieces_g, spread_pieces(two, "seq"))
    else:
        totals = [
            [lax.psum(half.astype(F32), ("dp", "seq")).astype(BF16) for half in halves]
            for halves in (first, (keep, send))
        ]
        (output,) = place(me, here_x, orders, *spread_pieces(branch, "seq"))
        pieces_g = spread_pieces(back, "seq")
    (input_grad,) = place(me, here_dy, orders, *pieces_g)
    weights = call(
        functools.partial(unpack_kernel, sizes, len(totals[0])),
        [
            ((width,), F32),
            ((width, 2 * inner), F32),
            ((taps, inner), F32),
            ((inner,), F32),
            ((rank + 2 * state, inner), F32),
            ((rank, inner), F32),
            ((inner,), F32),
            ((state, inner), F32),
            ((inner,), F32),
            ((inner, width), F32),
        ],
        [((2 * half_one, inner), BF16), ((2 * half_two, inner), BF16)],
        1,
        "unpack_sums",
        24,
        2.4,
    )(me, *totals[0], *totals[1])
    turned = [v.T if v.ndim == 2 and v.shape[1] == inner and v.shape[0] != rank else v for v in weights]
    return (output[None], input_grad[None], *turned)


def solution(mesh):
    placed = (
        P("dp", "seq", None),
        P("dp", None),
        P("dp", "seq"),
        P(),
        P(),
        P(),
        P(),
        P(),
        P(),
        P(),
        P(),
        P(),
        P(),
        P("dp", "seq", None),
    )
    return jax.shard_map(
        shards,
        mesh=mesh,
        in_specs=placed,
        out_specs=(
            P("dp", "seq", None),
            P("dp", "seq", None),
            P(),
            P(),
            P(),
            P(),
            P(),
            P(),
            P(),
            P(),
            P(),
            P(),
        ),
        check_vma=False,
    )
```

```python
import functools

import jax
import jax.numpy as jnp
from jax import lax
from jax.experimental import pallas as pl
from jax.experimental.pallas import tpu as pltpu
from jax.sharding import PartitionSpec as P

EPSILON = 1e-05
LOG2E = 1.4426950408889634
FAR = 1e30
CHUNKS = 8
LANES = 128
BLOCK = 16
CUBE = (0, 2, 4, 6, 1, 3, 5, 7)
SENT = (2, 4, 6, 1)
ORDER_ROWS = 16
F32, BF16 = jnp.float32, jnp.bfloat16
MIB = 1024 * 1024


def dot(a, b, contract=((1,), (0,))):
    return lax.dot_general(a, b, (contract, ((), ())), preferred_element_type=F32)


def as_row(ref):
    return ref[...].reshape(1, ref.shape[0])


def wide(tile, width):
    return jnp.concatenate([tile] * (width // LANES), axis=1)


def sigmoid(v):
    return 1.0 / (1.0 + jnp.exp(-v))


def scalars(me, lengths, rows):
    begin, meta = jnp.int32(0), [me[0] * rows]
    for k in range(lengths.shape[1]):
        meta.append(begin)
        begin = begin + lengths[0, k]
    return meta


def source(me, p, n_pieces):
    return jnp.bitwise_xor(me[0], CUBE[p]) if n_pieces == len(CUBE) else jnp.int32(p)


def places(first, rows, r0, steps):
    r = r0 + lax.broadcasted_iota(jnp.int32, (rows, LANES), 0)
    return first + lax.rem(r, CHUNKS) * steps + lax.div(r, CHUNKS)


def cloud_start(meta, clouds, place):
    start = jnp.zeros_like(place)
    for k in range(clouds):
        begin = meta[1 + k]
        start = jnp.maximum(start, jnp.where(begin <= place, begin, 0))
    return start


def fill_valid(valid, meta, clouds, rows, lags):
    steps = rows // CHUNKS

    def body(j, carry):
        r0 = pl.multiple_of(j * BLOCK, BLOCK)
        place = places(meta[0], BLOCK, r0, steps)
        begin = cloud_start(meta, clouds, place)
        for k in range(1, lags + 1):
            valid[k - 1, pl.ds(r0, BLOCK), :] = (place - k >= begin).astype(F32)
        return carry

    lax.fori_loop(0, rows // BLOCK, body, 0)


def row_of_place(rows):
    place = lax.broadcasted_iota(jnp.int32, (rows, rows), 0)
    row = lax.broadcasted_iota(jnp.int32, (rows, rows), 1)
    return (place == lax.rem(row, CHUNKS) * (rows // CHUNKS) + lax.div(row, CHUNKS)).astype(F32).astype(BF16)


def gather_rows(column, pieces, me, rows):
    lane = lax.broadcasted_iota(jnp.int32, (column.shape[0], rows), 1).astype(F32)
    mine = [
        (column - (source(me, p, len(pieces)) * rows).astype(F32) == lane).astype(F32).astype(BF16)
        for p in range(len(pieces))
    ]
    return dot(jnp.concatenate(mine, axis=1), jnp.concatenate(pieces, axis=0))


def fill_broadcast(out, xproj, first, count):
    whole = xproj[...]
    high = whole.astype(BF16)
    low = (whole - high.astype(F32)).astype(BF16)
    row = lax.rem(lax.broadcasted_iota(jnp.int32, (2 * LANES, LANES), 0), LANES)
    for n in range(count):
        pick = (row == first + n).astype(F32).astype(BF16)
        out[:, n * LANES : (n + 1) * LANES] = dot(jnp.concatenate([high, low], axis=1), pick)


def rates(alog):
    return -jnp.exp(alog[...])


def chunk_of(ref, c, count):
    return jnp.concatenate([ref[b, pl.ds(c, count, stride=CHUNKS), :] for b in range(ref.shape[0])], axis=1)


def set_chunk(ref, c, value):
    for b in range(ref.shape[0]):
        ref[b, pl.ds(c, value.shape[0], stride=CHUNKS), :] = value[:, b * LANES : (b + 1) * LANES]


def payload_kernel(tokens, order, out, near, copied):
    rows, width = tokens.shape
    copies = [
        pltpu.make_async_copy(order, near, copied.at[0]),
        pltpu.make_async_copy(tokens, out.at[pl.ds(0, rows)], copied.at[1]),
    ]
    for copy in copies:
        copy.start()
    out[rows:, :] = jnp.zeros((ORDER_ROWS, width), BF16)
    copies[0].wait()
    out[rows:, 0:rows] = order_digits(near)
    copies[1].wait()


def order_digits(order):
    sub = lax.broadcasted_iota(jnp.int32, (ORDER_ROWS, order.shape[1]), 0)
    digits = jnp.where(sub == 0, order[...] >> 7, jnp.where(sub == 1, order[...] & 127, 0))
    return digits.astype(F32).astype(BF16)


def pre_kernel(sizes, n_pieces, n_far, me, order, *refs):
    rows, width, inner, rank, state, lags, clouds = sizes
    steps = rows // CHUNKS
    pieces = refs[:n_pieces]
    far_refs, refs = refs[n_pieces : n_pieces + n_far], refs[:n_pieces] + refs[n_pieces + n_far :]
    near_refs, copied, refs = refs[-n_far - 1 : -1], refs[-1], refs[: -n_far - 1]
    copies = [pltpu.make_async_copy(a, b, copied.at[k]) for k, (a, b) in enumerate(zip(far_refs, near_refs))]
    for copy in copies:
        copy.start()
    (lengths, gain, w_in, conv_w, conv_b, w_x, w_dt, dt_b, alog, skip) = near_refs
    (trans_o, normed_o, gate_o, ext_o, conv_o, act_o, step_o, xproj_o, chunkf_o, sums_o, f_o, column_o, orders_o,
     valid, far, use, bbc, wx_o, wdt_o, a2, rows_o, conv_in) = refs[n_pieces:]
    to_row = row_of_place(rows)
    sub = lax.broadcasted_iota(jnp.int32, (BLOCK, LANES), 0)
    extra = jnp.full((BLOCK, LANES), -1.0, F32)
    tail = jnp.zeros((ORDER_ROWS, rows), F32)
    for p in range(n_pieces):
        now = pieces[p][rows : rows + ORDER_ROWS, :rows]
        tail = jnp.where(source(me, p, n_pieces) == me[0] - 1, now.astype(F32), tail)
        if p < orders_o.shape[0]:
            row = dot(now, to_row)
            orders_o[p : p + 1, :] = row[0:1] * 128.0 + row[1:2]
    for k in range(1, lags + 1):
        extra = jnp.where(sub == k, tail[0:1, rows - k : rows - k + 1] * 128.0 + tail[1:2, rows - k : rows - k + 1], extra)
    both = dot(to_row, order_digits(order), ((0,), (1,)))
    own = jnp.broadcast_to(both[:, 0:1] * 128.0 + both[:, 1:2], (rows, LANES))
    column_o[...] = own
    column = jnp.concatenate([own, extra], axis=0)
    trans = gather_rows(wide(column, rows), [p[0:rows, :] for p in pieces], me, rows)
    trans_o[...] = trans[:rows].astype(BF16)
    for copy in copies:
        copy.wait()
    meta = scalars(me, lengths, rows)
    bias, dt_bias = as_row(conv_b), as_row(dt_b)
    rows_o[0 : lags + 1, :] = conv_w[...]
    rows_o[lags + 1 : lags + 2, :] = as_row(skip)
    inv_rms = lax.rsqrt(jnp.mean(trans * trans, axis=1, keepdims=True) + EPSILON)
    normed = (trans * inv_rms * as_row(gain)).astype(BF16)
    normed_o[...] = normed[:rows]
    conv_in[...] = dot(normed, w_in[:, :inner]).astype(BF16).astype(F32)
    gate_o[...] = dot(normed[:rows], w_in[:, inner:])
    pad = lags * CHUNKS
    ext_o[pad : pad + rows, :] = conv_in[:rows, :]
    first_sub = lax.broadcasted_iota(jnp.int32, (CHUNKS, inner), 0) == 0
    for k in range(1, lags + 1):
        tile = conv_in[(steps - k) * CHUNKS : (steps - k + 1) * CHUNKS, :]
        before = conv_in[rows + k : rows + k + 1, :]
        ext_o[(lags - k) * CHUNKS : (lags - k + 1) * CHUNKS, :] = jnp.where(
            first_sub, before, pltpu.roll(tile, 1, 0)
        )
    for thin, full in ((w_x, wx_o), (w_dt, wdt_o)):
        blank = jnp.zeros((LANES - thin.shape[0], inner), F32)
        full[...] = jnp.concatenate([thin[...].astype(F32), blank], axis=0).astype(BF16)
    fill_valid(valid, meta, clouds, rows, lags)

    def conv_body(j, carry):
        r0 = pl.multiple_of(j * BLOCK, BLOCK)
        out = bias + conv_w[lags : lags + 1, :] * ext_o[pl.ds(r0 + pad, BLOCK), :]
        for k in range(1, lags + 1):
            ok = wide(valid[k - 1, pl.ds(r0, BLOCK), :], inner)
            shifted = ext_o[pl.ds(pl.multiple_of(r0 + pad - k * CHUNKS, CHUNKS), BLOCK), :]
            out = out + conv_w[lags - k : lags - k + 1, :] * shifted * ok
        conv_o[pl.ds(r0, BLOCK), :] = out
        act_o[pl.ds(r0, BLOCK), :] = (out * sigmoid(out)).astype(BF16)
        return carry

    lax.fori_loop(0, rows // BLOCK, conv_body, 0)
    xproj = dot(act_o[...], wx_o[...], ((1,), (1,)))
    xproj_o[...] = xproj
    step_o[...] = dot(xproj.astype(BF16), wdt_o[...])

    def step_body(j, carry):
        r0 = pl.multiple_of(j * BLOCK, BLOCK)
        pre = step_o[pl.ds(r0, BLOCK), :] + dt_bias
        step = jnp.maximum(pre, 0.0) + jnp.log1p(jnp.exp(-jnp.abs(pre)))
        step_o[pl.ds(r0, BLOCK), :] = step
        keep = wide(valid[0, pl.ds(r0, BLOCK), :], inner)
        distance = jnp.where(keep > 0.5, step, FAR)
        far[pl.ds(r0, BLOCK), :] = distance
        use[pl.ds(r0, BLOCK), :] = step * act_o[pl.ds(r0, BLOCK), :].astype(F32)
        return carry + distance[:CHUNKS] + distance[CHUNKS:]

    sums_o[...] = lax.fori_loop(0, rows // BLOCK, step_body, jnp.zeros((CHUNKS, inner), F32))
    fill_broadcast(bbc, xproj_o, rank, state)
    a2[...] = rates(alog) * LOG2E
    for lb in range(inner // LANES):
        ls = slice(lb * LANES, (lb + 1) * LANES)
        rate = [jnp.broadcast_to(a2[n : n + 1, ls], (CHUNKS, LANES)) for n in range(state)]

        def scan_body(i, states):
            r = pl.ds(pl.multiple_of(i * CHUNKS, CHUNKS), CHUNKS)
            distance, u = far[r, ls], use[r, ls]
            return tuple(
                jnp.exp2(distance * rate[n]) * states[n] + u * bbc[r, n * LANES : (n + 1) * LANES]
                for n in range(state)
            )

        zero = jnp.zeros((CHUNKS, LANES), F32)
        last = lax.fori_loop(0, steps, scan_body, (zero,) * state, unroll=8)
        for n in range(state):
            chunkf_o[lb, n * CHUNKS : (n + 1) * CHUNKS, :] = last[n]
    total = jnp.zeros((state, inner), F32)
    for c in range(CHUNKS):
        total = jnp.exp2(a2[...] * sums_o[c : c + 1, :]) * total + chunk_of(chunkf_o, c, state)
    f_o[...] = total


def back_kernel(sizes, n_pieces, me, *refs):
    rows, width, inner, rank, state, lags, clouds = sizes
    steps = rows // CHUNKS
    pieces = refs[:n_pieces]
    gate, far, xproj, a2, w_out, sums, f, column = refs[n_pieces : n_pieces + 8]
    n_out = (len(CUBE) - 4 if n_pieces == len(CUBE) else 1)
    dy_o, gg_o, gm, cbc, chunkb_o = refs[n_pieces + 8 : n_pieces + 13]
    carries_o = refs[n_pieces + 13 : n_pieces + 13 + n_out]
    near_out, copied = refs[n_pieces + 13 + n_out :]
    copy = pltpu.make_async_copy(w_out, near_out, copied)
    copy.start()
    trans_dy = gather_rows(wide(column[...], rows), [p[0:rows, :] for p in pieces], me, rows).astype(BF16)
    dy_o[...] = trans_dy
    copy.wait()
    gg_o[...] = dot(trans_dy, near_out[...], ((1,), (1,)))

    def body(j, carry):
        r = pl.ds(pl.multiple_of(j * BLOCK, BLOCK), BLOCK)
        z = gate[r, :]
        gm[r, :] = gg_o[r, :] * (z * sigmoid(z))
        return carry

    lax.fori_loop(0, rows // BLOCK, body, 0)
    fill_broadcast(cbc, xproj, rank + state, state)
    for lb in range(inner // LANES):
        ls = slice(lb * LANES, (lb + 1) * LANES)
        rate = [jnp.broadcast_to(a2[n : n + 1, ls], (CHUNKS, LANES)) for n in range(state)]

        def scan_body(k, flows):
            r = pl.ds(pl.multiple_of((steps - 1 - k) * CHUNKS, CHUNKS), CHUNKS)
            distance, g = far[r, ls], gm[r, ls]
            return tuple(
                jnp.exp2(distance * rate[n]) * (flows[n] + g * cbc[r, n * LANES : (n + 1) * LANES])
                for n in range(state)
            )

        zero = jnp.zeros((CHUNKS, LANES), F32)
        last = lax.fori_loop(0, steps, scan_body, (zero,) * state, unroll=8)
        for n in range(state):
            chunkb_o[lb, n * CHUNKS : (n + 1) * CHUNKS, :] = last[n]
    total = jnp.zeros((state, inner), F32)
    for c in reversed(range(CHUNKS)):
        total = jnp.exp2(a2[...] * sums[c : c + 1, :]) * total + chunk_of(chunkb_o, c, state)
    passed = jnp.broadcast_to(jnp.sum(sums[...], axis=0, keepdims=True), (CHUNKS, inner))
    if n_out == 1:
        carries_o[0][:state, :] = f[...]
        carries_o[0][state : 2 * state, :] = total
        carries_o[0][2 * state :, :] = passed
        return
    for out, d in zip(carries_o, SENT):
        later = jnp.bitwise_xor(me[0], d) > me[0]
        out[:state, :] = jnp.where(later, f[...], total)
        out[state:, :] = passed


def core_of(me, devices):
    return jnp.bitwise_and(me, 1) if devices == len(CUBE) else jnp.int32(0)


def hold_carries(held, carries, me):
    n_pieces, size = len(carries), carries[0].shape[0]
    devices = len(CUBE) if n_pieces == len(CUBE) - 1 else n_pieces
    for p in range(n_pieces):
        whence = source(me, p + 1, devices) if devices > n_pieces else p
        held[pl.ds(pl.multiple_of(whence * size, CHUNKS), size), :] = carries[p][...]
    return devices


def scan_forward_kernel(sizes, n_pieces, me_ref, *refs):
    rows, width, inner, rank, state, lags, clouds = sizes
    steps = rows // CHUNKS
    carries = refs[:n_pieces]
    (trans_dy, normed, gg, gate, act, far, use, bbc, cbc, chunkf, sums, a2, consts, w_out) = refs[n_pieces : n_pieces + 14]
    blocks = inner // LANES
    states = refs[n_pieces + 14 : n_pieces + 14 + blocks]
    (branch_o, gz_o, keep_o, send_o) = refs[n_pieces + 14 + blocks : n_pieces + 18 + blocks]
    (mixed, sstart, gated, held) = refs[n_pieces + 18 + blocks :]
    me = me_ref[0]
    skips = consts[lags + 1 : lags + 2, :]
    size = carries[0].shape[0]
    devices = hold_carries(held, carries, me_ref)

    def ahead(s, flow):
        base = pl.multiple_of(s * size, CHUNKS)
        p_s = jnp.exp2(a2[...] * held[pl.ds(base + size - CHUNKS, 1), :])
        return jnp.where(s < me, p_s * flow + held[pl.ds(base, state), :], flow)

    now = lax.fori_loop(0, devices, ahead, jnp.zeros((state, inner), F32))
    for c in range(CHUNKS):
        set_chunk(sstart, c, now)
        now = jnp.exp2(a2[...] * sums[c : c + 1, :]) * now + chunk_of(chunkf, c, state)

    for lb in range(inner // LANES):
        ls = slice(lb * LANES, (lb + 1) * LANES)
        rate = [jnp.broadcast_to(a2[n : n + 1, ls], (CHUNKS, LANES)) for n in range(state)]
        begin = []
        for n in range(state):
            tile = sstart[lb, n * CHUNKS : (n + 1) * CHUNKS, :]
            states[lb][n, 0:CHUNKS, :] = tile
            begin.append(tile)

        def forward(i, now):
            r0 = pl.multiple_of(i * CHUNKS, CHUNKS)
            r = pl.ds(r0, CHUNKS)
            nxt = pl.ds(pl.multiple_of(r0 + CHUNKS, CHUNKS), CHUNKS)
            distance, u = far[r, ls], use[r, ls]
            new, out = [], None
            for n in range(state):
                value = jnp.exp2(distance * rate[n]) * now[n] + u * bbc[r, n * LANES : (n + 1) * LANES]
                states[lb][n, nxt, :] = value
                part = value * cbc[r, n * LANES : (n + 1) * LANES]
                out = part if out is None else out + part
                new.append(value)
            mixed[r, ls] = out
            return tuple(new)

        lax.fori_loop(0, steps, forward, tuple(begin), unroll=8)

    def gating(j, carry):
        r = pl.ds(pl.multiple_of(j * BLOCK, BLOCK), BLOCK)
        z, a = gate[r, :], act[r, :].astype(F32)
        s = sigmoid(z)
        m = mixed[r, :] + skips * a
        gated[r, :] = (m * (z * s)).astype(BF16)
        gz_o[r, :] = (gg[r, :] * m * s * (1.0 + z * (1.0 - s))).astype(BF16)
        return carry

    lax.fori_loop(0, rows // BLOCK, gating, 0)
    branch_o[...] = dot(gated[...], w_out[...]).astype(BF16)
    second = core_of(me, devices) == 1
    wout_g = dot(trans_dy[...], gated[...], ((0,), (0,))).astype(BF16)
    gate_g = dot(normed[...], gz_o[...], ((0,), (0,))).astype(BF16)
    keep_o[...] = jnp.where(second, gate_g, wout_g)
    send_o[...] = jnp.where(second, wout_g, gate_g)


def adjoint_carries_kernel(sizes, n_pieces, me_ref, *refs):
    rows, width, inner, rank, state, lags, clouds = sizes
    carries = refs[:n_pieces]
    chunkb, sums, a2, gstart, held = refs[n_pieces:]
    me = me_ref[0]
    size = carries[0].shape[0]
    back = size - CHUNKS - state
    devices = hold_carries(held, carries, me_ref)

    def behind(k, flow):
        s = devices - 1 - k
        base = pl.multiple_of(s * size, CHUNKS)
        p_s = jnp.exp2(a2[...] * held[pl.ds(base + size - CHUNKS, 1), :])
        return jnp.where(s > me, p_s * flow + held[pl.ds(pl.multiple_of(base + back, CHUNKS), state), :], flow)

    now = lax.fori_loop(0, devices, behind, jnp.zeros((state, inner), F32))
    for c in reversed(range(CHUNKS)):
        set_chunk(gstart, c, now)
        now = jnp.exp2(a2[...] * sums[c : c + 1, :]) * now + chunk_of(chunkb, c, state)


def scan_backward_kernel(sizes, *refs):
    rows, width, inner, rank, state, lags, clouds = sizes
    steps = rows // CHUNKS
    states, refs = refs[: inner // LANES], refs[inner // LANES :]
    (gstart, far, use, bbc, cbc, gm, step, act, conv, valid, a2, conv_w, w_x, w_dt) = refs[:14]
    (gconv, rim_o, gpre, gxproj_o, galog_o) = refs[14:19]
    (gs, lamb, gb, gc) = refs[19:]
    skips = conv_w[lags + 1 : lags + 2, :]
    group, pair = 3, 4
    for lg in range(inner // LANES // group):
        lanes = [slice((lg * group + k) * LANES, (lg * group + k + 1) * LANES) for k in range(group)]
        for ng in range(state // pair):
            ns = [ng * pair + k for k in range(pair)]
            rate = [[jnp.broadcast_to(a2[n : n + 1, ls], (CHUNKS, LANES)) for ls in lanes] for n in ns]
            begin = [gstart[lg * group + k, n * CHUNKS : (n + 1) * CHUNKS, :] for n in ns for k in range(group)]
            zero = jnp.zeros((CHUNKS, LANES), F32)

            def backward(k, carry):
                flows, sums_a = carry
                r0 = pl.multiple_of((steps - 1 - k) * CHUNKS, CHUNKS)
                r = pl.ds(r0, CHUNKS)
                nxt = pl.ds(pl.multiple_of(r0 + CHUNKS, CHUNKS), CHUNKS)
                gs_t = [None] * group
                lamb_t = [None] * group
                g_t = [gm[r, ls] for ls in lanes]
                u_t = [use[r, ls] for ls in lanes]
                d_t = [step[r, ls] for ls in lanes]
                f_t = [far[r, ls] for ls in lanes]
                new_flows, new_sums = [], []
                for q, n in enumerate(ns):
                    b = bbc[r, n * LANES : (n + 1) * LANES]
                    c = cbc[r, n * LANES : (n + 1) * LANES]
                    gb_t = gc_t = None
                    for x, ls in enumerate(lanes):
                        lam = g_t[x] * c + flows[q * group + x]
                        flow = jnp.exp2(f_t[x] * rate[q][x]) * lam
                        part = flow * states[lg * group + x][n, r, :]
                        one, two = part * rate[q][x], lam * b
                        gs_t[x] = one if gs_t[x] is None else gs_t[x] + one
                        lamb_t[x] = two if lamb_t[x] is None else lamb_t[x] + two
                        three, four = lam * u_t[x], g_t[x] * states[lg * group + x][n, nxt, :]
                        gb_t = three if gb_t is None else gb_t + three
                        gc_t = four if gc_t is None else gc_t + four
                        new_flows.append(flow)
                        new_sums.append(sums_a[q * group + x] + part * d_t[x])
                    nl = slice(n * LANES, (n + 1) * LANES)
                    if lg == 0:
                        gb[r, nl] = gb_t
                        gc[r, nl] = gc_t
                    else:
                        gb[r, nl] += gb_t
                        gc[r, nl] += gc_t
                for x, ls in enumerate(lanes):
                    if ng == 0:
                        gs[r, ls] = gs_t[x]
                        lamb[r, ls] = lamb_t[x]
                    else:
                        gs[r, ls] += gs_t[x]
                        lamb[r, ls] += lamb_t[x]
                return tuple(new_flows), tuple(new_sums)

            flows, sums_a = lax.fori_loop(
                0, steps, backward, (tuple(begin), (zero,) * (pair * group)), unroll=8
            )
            for q, n in enumerate(ns):
                for x, ls in enumerate(lanes):
                    galog_o[n : n + 1, ls] = (
                        jnp.sum(sums_a[q * group + x], axis=0, keepdims=True) * rate[q][x][0:1] * (1.0 / LOG2E)
                    )
    col = lax.broadcasted_iota(jnp.int32, (state * LANES, LANES), 1)
    row = lax.div(lax.broadcasted_iota(jnp.int32, (state * LANES, LANES), 0), LANES)
    pick_b = (col == row + rank).astype(F32).astype(BF16)
    pick_c = (col == row + rank + state).astype(F32).astype(BF16)

    def lane_sums(ref, pick):
        whole = ref[...]
        high = whole.astype(BF16)
        low = (whole - high.astype(F32)).astype(BF16)
        return dot(high, pick) + dot(low, pick)

    grad_bc = lane_sums(gb, pick_b) + lane_sums(gc, pick_c)

    def pre_body(j, carry):
        r = pl.ds(pl.multiple_of(j * BLOCK, BLOCK), BLOCK)
        grad_step = gs[r, :] * (1.0 / LOG2E) + lamb[r, :] * act[r, :].astype(F32)
        gpre[r, :] = (grad_step * (1.0 - jnp.exp(-step[r, :]))).astype(BF16)
        return carry

    lax.fori_loop(0, rows // BLOCK, pre_body, 0)
    grad_xproj = (dot(gpre[...], w_dt[...], ((1,), (1,))) + grad_bc).astype(BF16)
    gxproj_o[...] = grad_xproj
    gs[...] = dot(grad_xproj, w_x[...])

    def conv_body(j, carry):
        r = pl.ds(pl.multiple_of(j * BLOCK, BLOCK), BLOCK)
        grad_act = gm[r, :] * skips + lamb[r, :] * step[r, :] + gs[r, :]
        v = conv[r, :]
        s = sigmoid(v)
        gconv[r, :] = grad_act * (s * (1.0 + v * (1.0 - s)))
        return carry

    lax.fori_loop(0, rows // BLOCK, conv_body, 0)
    rim_o[...] = jnp.zeros((CHUNKS, inner), F32)
    for b in range(1, lags + 1):
        total = jnp.zeros((1, inner), F32)
        for k in range(b, lags + 1):
            total = total + masked_tile(gconv, valid, conv_w, k - b, k, lags)[0:1]
        rim_o[b : b + 1, :] = total


def masked_tile(gconv, valid, conv_w, i, k, lags):
    r = pl.ds(pl.multiple_of(i * CHUNKS, CHUNKS), CHUNKS)
    tile = gconv[r, :] * conv_w[lags - k : lags - k + 1, :]
    return tile if k == 0 else tile * wide(valid[k - 1, r, :], tile.shape[1])


def small_kernel(sizes, gpre, gxproj, xproj, act, gconv, ext, valid, gm, conv_w, galog, small_o, gci_o):
    rows, width, inner, rank, state, lags, clouds = sizes
    steps = rows // CHUNKS

    def spread(i, carry):
        total = masked_tile(gconv, valid, conv_w, i, 0, lags)
        for k in range(1, lags + 1):
            total = total + masked_tile(gconv, valid, conv_w, i + k, k, lags)
        gci_o[pl.ds(pl.multiple_of(i * CHUNKS, CHUNKS), CHUNKS), :] = total
        return carry

    lax.fori_loop(0, steps - lags, spread, 0)
    sub = lax.broadcasted_iota(jnp.int32, (CHUNKS, inner), 0)
    for i in range(steps - lags, steps):
        total = masked_tile(gconv, valid, conv_w, i, 0, lags)
        for k in range(1, lags + 1):
            if i + k < steps:
                total = total + masked_tile(gconv, valid, conv_w, i + k, k, lags)
            else:
                moved = pltpu.roll(masked_tile(gconv, valid, conv_w, i + k - steps, k, lags), CHUNKS - 1, 0)
                total = total + jnp.where(sub == CHUNKS - 1, 0.0, moved)
        gci_o[i * CHUNKS : (i + 1) * CHUNKS, :] = total

    def sum_body(j, carry):
        r0 = pl.multiple_of(j * BLOCK, BLOCK)
        r = pl.ds(r0, BLOCK)
        grad = gconv[r, :]
        parts = [gm[r, :] * act[r, :].astype(F32), gpre[r, :].astype(F32), grad]
        for k in reversed(range(lags + 1)):
            masked = grad if k == 0 else grad * wide(valid[k - 1, r, :], inner)
            parts.append(masked * ext[pl.ds(pl.multiple_of(r0 + (lags - k) * CHUNKS, CHUNKS), BLOCK), :])
        return tuple(total + part[:CHUNKS] + part[CHUNKS:] for total, part in zip(carry, parts))

    sums = lax.fori_loop(0, rows // BLOCK, sum_body, (jnp.zeros((CHUNKS, inner), F32),) * (lags + 4))
    small_o[0:state, :] = galog[...]
    at = state
    small_o[at : at + rank + 2 * state, :] = dot(gxproj[...], act[...], ((0,), (0,)))[: rank + 2 * state]
    at += rank + 2 * state
    small_o[at : at + rank, :] = dot(xproj[...].astype(BF16), gpre[...], ((0,), (0,)))[:rank]
    at += rank
    for k, part in enumerate(sums):
        small_o[at + k : at + k + 1, :] = jnp.sum(part, axis=0, keepdims=True)
    at += len(sums)
    small_o[at:, :] = jnp.zeros((small_o.shape[0] - at, inner), F32)


def final_kernel(sizes, devices, me, trans, normed, gci, gz, rim, small, gain, w_in, back_o, keep_o, send_o, both):
    rows, width, inner, rank, state, lags, clouds = sizes
    steps = rows // CHUNKS
    r = lax.broadcasted_iota(jnp.int32, (rows, inner), 0)
    total = gci[...]
    for k in range(1, lags + 1):
        total = total + jnp.where(r == (steps - k) * CHUNKS + CHUNKS - 1, rim[k : k + 1, :], 0.0)
    grad_ci = total.astype(BF16)
    grad_z = gz[...]
    grad_normed = dot(grad_ci, w_in[:, :inner], ((1,), (1,))) + dot(grad_z, w_in[:, inner:], ((1,), (1,)))
    x = trans[...].astype(F32)
    inv_rms = lax.rsqrt(jnp.mean(x * x, axis=1, keepdims=True) + EPSILON)
    scaled = grad_normed * as_row(gain)
    back_o[...] = (
        inv_rms * scaled
        - inv_rms * inv_rms * inv_rms * x * jnp.mean(scaled * x, axis=1, keepdims=True)
    ).astype(BF16)
    both[0:width, :] = dot(normed[...], grad_ci, ((0,), (0,))).astype(BF16)
    gain_row = jnp.sum(grad_normed * x * inv_rms, axis=0, keepdims=True)
    gain_row = jnp.concatenate([gain_row, jnp.zeros((1, inner - width), F32)], axis=1)
    n_small = small.shape[0]
    last = lax.broadcasted_iota(jnp.int32, (n_small, inner), 0) == n_small - 1
    both[width : width + n_small, :] = jnp.where(last, gain_row, small[...]).astype(BF16)
    half = keep_o.shape[0]
    core = core_of(me[0], devices)
    keep_o[...] = both[pl.ds(pl.multiple_of(core * half, BLOCK), half), :]
    send_o[...] = both[pl.ds(pl.multiple_of((1 - core) * half, BLOCK), half), :]


def small_rows(sizes):
    rows, width, inner, rank, state, lags, clouds = sizes
    return state + (rank + 2 * state) + rank + 3 + lags + 1 + 1


def halves_kernel(me, kept, got, own_o, *sent_o):
    part = own_o.shape[0]
    chip = lax.div(me[0], 2)
    for d, out in enumerate((own_o,) + sent_o):
        r = pl.ds(pl.multiple_of(jnp.bitwise_xor(chip, d) * part, BLOCK), part)
        out[...] = (kept[r, :].astype(F32) + got[r, :].astype(F32)).astype(BF16)


def beside(out, rows):
    half, width = rows.shape[0] // 2, rows.shape[1]
    out[0:half, 0:width] = rows[0:half, :]
    out[0:half, width:] = rows[half:, :]


def unfold(piece, rows, width):
    if piece.shape == (rows, width):
        return piece[...]
    half = rows // 2
    return jnp.concatenate([piece[0:half, 0:width], piece[0:half, width : 2 * width]], axis=0)


def halves_beside_kernel(me, kept, got, rows, own_o, *sent_o):
    part = own_o.shape[0]
    half = rows.shape[0] // 2
    chip = lax.div(me[0], 2)
    for d, out in enumerate((own_o,) + sent_o):
        r = pl.ds(pl.multiple_of(jnp.bitwise_xor(chip, d) * part, BLOCK), part)
        total = (kept[r, :].astype(F32) + got[r, :].astype(F32)).astype(BF16)
        if d == 0:
            out[...] = total
        else:
            beside(out, rows)
            out[half:, :] = total


def sum_kernel(a, b, c, d, out):
    one, two, three, four = (x[x.shape[0] - a.shape[0] :, :].astype(F32) for x in (a, b, c, d))
    out[...] = ((one + two) + (three + four)).astype(BF16)


def pair_kernel(a, b, out):
    out[...] = (a[...].astype(F32) + b[...].astype(F32)).astype(BF16)


def pair_beside_kernel(a, b, rows, out):
    beside(out, rows)
    out[rows.shape[0] // 2 :, :] = (a[...].astype(F32) + b[...].astype(F32)).astype(BF16)


def by_chip(out, first, parts, me, part):
    for d, piece in enumerate(parts):
        chip = jnp.bitwise_xor(lax.div(me[0], 2), d)
        out[pl.ds(pl.multiple_of(first + chip * part, BLOCK), part), :] = piece[piece.shape[0] - part :, :]


def chips_kernel(me, own, two, four, six, out):
    by_chip(out, 0, (own, two, four, six), me, own.shape[0])


def share_kernel(rows, width, me, orders, own, two, four, six, mine_o, theirs_o, *half_o):
    pieces = (own, two, four, six)
    whole = jnp.concatenate([unfold(p, rows, width) for p in pieces], axis=0)
    for core, out in enumerate((mine_o, theirs_o)):
        first = jnp.bitwise_xor(me[0], core) * rows
        place = (first + lax.broadcasted_iota(jnp.int32, (rows, rows), 0)).astype(F32)
        match = [(orders[p : p + 1, :] == place).astype(F32).astype(BF16) for p in range(len(pieces))]
        moved = dot(jnp.concatenate(match, axis=1), whole).astype(BF16)
        if core == 0:
            out[...] = moved
        else:
            out[0 : rows // 2, 0:width] = moved[: rows // 2]
            out[0 : rows // 2, width:] = moved[rows // 2 :]
    for out in half_o:
        part = out.shape[0] // len(pieces)
        by_chip(out, 0, pieces, me, part)
        by_chip(theirs_o, rows // 2, pieces, me, part)


def arrive_kernel(here, mine, theirs, out):
    rows, width = here.shape
    moved = mine[...].astype(F32) + unfold(theirs, rows, width).astype(F32)
    out[...] = (here[...].astype(F32) + moved).astype(BF16)


def unpack_kernel(sizes, devices, me, own_one, other_one, own_two, other_two, *refs):
    rows, width, inner, rank, state, lags, clouds = sizes
    (gain_o, win_o, taps_o, convb_o, wx_o, wdt_o, dtb_o, alog_o, skip_o, wout_o, all_one, all_two) = refs
    for own, other, whole, n in ((own_one, other_one, all_one, devices[0]), (own_two, other_two, all_two, devices[1])):
        core, half = core_of(me[0], n), whole.shape[0] // 2
        for k, piece in ((core, own), (1 - core, other)):
            whole[pl.ds(pl.multiple_of(k * half, BLOCK), half), :] = piece[piece.shape[0] - half :, :]
    wout_o[...] = all_one[0:width, :].astype(F32).T
    win_o[:, inner:] = all_one[width : 2 * width, :].astype(F32)
    win_o[:, :inner] = all_two[0:width, :].astype(F32)
    n_small = small_rows(sizes)
    small = all_two[width : width + n_small, :].astype(F32)
    alog_o[...] = small[0:state]
    at = state
    wx_o[...] = small[at : at + rank + 2 * state]
    at += rank + 2 * state
    wdt_o[...] = small[at : at + rank]
    at += rank
    for k, out in enumerate((skip_o, dtb_o, convb_o)):
        out[...] = small[at + k : at + k + 1].reshape(inner)
    at += 3
    taps_o[...] = small[at : at + lags + 1]
    gain_o[...] = small[n_small - 1 : n_small, :width].reshape(width)


def place_kernel(rows, n_pieces, me, here, orders, *refs):
    pieces, out = refs[:n_pieces], refs[n_pieces]
    place = (me[0] * rows + lax.broadcasted_iota(jnp.int32, (rows, rows), 0)).astype(F32)
    mine = [(orders[p : p + 1, :] == place).astype(F32).astype(BF16) for p in range(n_pieces)]
    moved = dot(jnp.concatenate(mine, axis=1), jnp.concatenate([p[...] for p in pieces], axis=0))
    out[...] = (here[...].astype(F32) + moved).astype(BF16)


def call(kernel, outs, scratch, n_smem, name, room, time=1.0, far_ins=()):
    vmem = pl.BlockSpec(memory_space=pltpu.VMEM)
    smem = pl.BlockSpec(memory_space=pltpu.SMEM)
    anywhere = pl.BlockSpec(memory_space=pltpu.HBM)

    def run(*args):
        args = [pltpu.with_memory_space_constraint(v, pltpu.HBM) if k in far_ins else v for k, v in enumerate(args)]
        return pl.pallas_call(
            kernel,
            out_shape=[jax.ShapeDtypeStruct(*part) if isinstance(part, tuple) else part for part in outs],
            in_specs=[smem if k < n_smem else anywhere if k in far_ins else vmem for k in range(len(args))],
            out_specs=[vmem] * len(outs),
            scratch_shapes=[pltpu.VMEM(*part) if isinstance(part, tuple) else part for part in scratch],
            compiler_params=pltpu.CompilerParams(vmem_limit_bytes=room * MIB),
            cost_estimate=pl.CostEstimate(
                flops=1, bytes_accessed=1, transcendentals=0
            ),
            name=name,
        )(*args)

    return run


CFG = {'dy': 'd6', 'dy1': 'fwd', 'adj': 'gstart', 'rim': '', 'small': 'one', 'z1': 'send', 'halves': '', 'pair': '', 'share': 'pair', 'hold': 'out', 'm3': 'pair', 'd': 'out', 'share3': 'total'}


def tie(name, value, choices):
    pick = CFG.get(name, "")
    for k in pick.split("+") if pick else ():
        value = after(value, choices[k])
    return value


def after(value, *others):
    return lax.optimization_barrier((value, others))[0]


def swap(block, axis, distance):
    devices = lax.axis_size(axis)
    return lax.ppermute(block, axis, [(i, i ^ distance) for i in range(devices)])


def spread_pieces(block, axis):
    whole = lax.all_gather(block, axis)
    return [whole[i] for i in range(lax.axis_size(axis))]


def spread_carries(blocks, axis):
    if len(blocks) == 1:
        return spread_pieces(blocks[0], axis)
    across = [swap(block, axis, d) for block, d in zip(blocks, SENT)]
    return across[:3] + [across[3]] + [swap(part, axis, 1) for part in across[:3]]


def from_behind(block, axis, distance):
    devices = range(lax.axis_size(axis))
    route = [(i - distance, i) for i in devices if i - distance in devices]
    return lax.ppermute(block, axis, route)


def shards(
    tokens,
    lengths,
    order,
    norm_gain,
    w_in,
    conv_weight,
    conv_bias,
    w_x,
    w_dt,
    dt_bias,
    a_log,
    d_skip,
    w_out,
    cotangent,
):
    rows, width = tokens.shape[1:]
    inner, rank, state, taps = w_out.shape[0], w_dt.shape[0], a_log.shape[1], conv_weight.shape[1]
    lags, clouds, steps = taps - 1, lengths.shape[1], rows // CHUNKS
    sizes = (rows, width, inner, rank, state, lags, clouds)
    devices = lax.axis_size("seq")
    me = lax.axis_index("seq").astype(jnp.int32)[None]
    here_x, here_dy = tokens[0], cotangent[0]
    cube = devices == len(CUBE) and lax.axis_size("dp") == 4
    (payload,) = call(
        payload_kernel,
        [((rows + ORDER_ROWS, width), BF16)],
        [(order.shape, order.dtype), pltpu.SemaphoreType.DMA((2,))],
        0,
        "tokens_and_order",
        4,
        far_ins=(0, 1),
    )(here_x, order)
    weights = (lengths, norm_gain, w_in, conv_weight.T, conv_bias, w_x.T, w_dt, dt_bias, a_log.T, d_skip)
    if cube:
        across_x = [payload] + [swap(payload, "seq", d) for d in CUBE[1:4]]
        send_dy = tie("dy", here_dy, {"d2": across_x[1], "d4": across_x[2], "d6": across_x[3]})
        across_dy = [send_dy] + [swap(send_dy, "seq", d) for d in CUBE[1:4]]
        pieces_x = across_x + [swap(part, "seq", 1) for part in across_x]
    else:
        pieces_x, pieces_dy = spread_pieces(payload, "seq"), spread_pieces(here_dy, "seq")
    n = len(pieces_x)
    big, lane = (rows, inner), (rows, LANES)
    carried = (inner // LANES, state * CHUNKS, LANES)
    spread = (rows, state * LANES)
    ext_rows = rows + lags * CHUNKS
    (trans, normed, gate, ext, conv, act, step, xproj, chunkf, sums, f, column, orders, valid, far, use, bbc, w_x_pad, w_dt_pad, a2, row_consts) = call(
        functools.partial(pre_kernel, sizes, n, len(weights)),
        [
            ((rows, width), BF16),
            ((rows, width), BF16),
            (big, F32),
            ((ext_rows, inner), F32),
            (big, F32),
            (big, BF16),
            (big, F32),
            (lane, F32),
            (carried, F32),
            ((CHUNKS, inner), F32),
            ((state, inner), F32),
            (lane, F32),
            ((4 if cube else n, rows), F32),
            ((lags, rows, LANES), F32),
            (big, F32),
            (big, F32),
            (spread, F32),
            ((LANES, inner), BF16),
            ((LANES, inner), BF16),
            ((state, inner), F32),
            ((lags + 2, inner), F32),
        ],
        [((rows + BLOCK, inner), F32), pltpu.SMEM(lengths.shape, jnp.int32)]
        + [(v.shape, v.dtype) for v in weights[1:]]
        + [pltpu.SemaphoreType.DMA((len(weights),))],
        1,
        "forward_local",
        24,
        9,
        far_ins=tuple(range(n + 2, n + 2 + len(weights))),
    )(me, order, *pieces_x, *weights)
    if cube:
        across_dy = [tie("dy1", part, {"fwd": xproj}) for part in across_dy]
        pieces_dy = across_dy + [swap(part, "seq", 1) for part in across_dy]
    carry_rows = (state + CHUNKS, 2 * state + CHUNKS)[not cube]
    n_sent = (len(SENT), 1)[not cube]
    trans_dy, gg, gm, cbc, chunkb, *carries = call(
        functools.partial(back_kernel, sizes, n),
        [((rows, width), BF16), (big, F32), (big, F32), (spread, F32), (carried, F32)]
        + [((carry_rows, inner), F32)] * n_sent,
        [(w_out.shape, w_out.dtype), pltpu.SemaphoreType.DMA],
        1,
        "backward_local",
        20,
        7,
        far_ins=(n + 5,),
    )(me, *pieces_dy, gate, far, xproj, a2, w_out, sums, f, column)
    carries = spread_carries(carries, "seq")
    n_small = small_rows(sizes)
    held = ((n * carry_rows, inner), F32)
    kept = [pltpu.VMEM((state, rows + CHUNKS, LANES), F32)] * (inner // LANES)
    *states, branch, gz, keep, send = call(
        functools.partial(scan_forward_kernel, sizes, len(carries)),
        [*kept, ((rows, width), BF16), (big, BF16), ((width, inner), BF16), ((width, inner), BF16)],
        [(big, F32), (carried, F32), (big, BF16), held],
        1,
        "scan_forward",
        18,
        7,
    )(me, *carries, trans_dy, normed, gg, gate, act, far, use, bbc, cbc, chunkf, sums, a2, row_consts, w_out)
    first = (keep, send)
    half_one, half_two = width, -(-(width + n_small) // (8 * BLOCK)) * (4 * BLOCK)
    got = swap(send, "seq", 1) if cube else None
    (gstart,) = call(
        functools.partial(adjoint_carries_kernel, sizes, len(carries)),
        [(carried, F32)],
        [held],
        1,
        "adjoint_carries",
        8,
        1.5,
    )(me, *carries, chunkb, sums, a2)
    if cube:
        part_one = half_one // 4
        beside_one = ((rows // 2 + part_one, inner), BF16)
        own_one, *sent = call(
            halves_beside_kernel, [((part_one, inner), BF16)] + [beside_one] * 3, [], 1, "add_halves_beside_rows", 8
        )(me, tie("adj", keep, {"gstart": gstart}), got, branch)
        away_one = [swap(block, "seq", d) for block, d in zip(sent, SENT)]
    gconv, rim, gpre, gxproj, galog = call(
        functools.partial(scan_backward_kernel, sizes),
        [(big, F32), ((CHUNKS, inner), F32), (big, BF16), (lane, BF16), ((state, inner), F32)],
        [(big, F32), (big, F32), (spread, F32), (spread, F32)],
        0,
        "scan_backward",
        20,
        14,
    )(*[pltpu.with_memory_space_constraint(part, pltpu.VMEM) for part in states], gstart, far, use, bbc, cbc, gm, step, act, conv, valid, a2, row_consts, w_x_pad, w_dt_pad)
    rim = from_behind(rim, "seq", -1)
    if cube:
        (one,) = call(sum_kernel, [((part_one, inner), BF16)], [], 0, "add_parts", 4)(
            tie("rim", after(own_one, gpre), {"rim": rim}), *away_one
        )
        gpre = tie("small", gpre, {"one": one})
    small, gci = call(
        functools.partial(small_kernel, sizes),
        [((n_small, inner), F32), (big, F32)],
        [],
        0,
        "small_grads",
        16,
        1.6,
    )(gpre, gxproj, xproj, act, gconv, ext, valid, gm, row_consts, galog)
    back, keep, send = call(
        functools.partial(final_kernel, sizes, devices),
        [((rows, width), BF16), ((half_two, inner), BF16), ((half_two, inner), BF16)],
        [((2 * half_two, inner), BF16)],
        1,
        "input_projection_grads",
        16,
    )(me, trans, normed, gci, gz, rim, small, norm_gain, w_in)
    if cube:
        part_two = half_two // 4
        piece_one, piece_two = ((part_one, inner), BF16), ((part_two, inner), BF16)
        pair_two = call(pair_kernel, [piece_two], [], 0, "add_pair", 4)
        rows_out = [((rows, width), BF16)]
        arrive = call(arrive_kernel, rows_out, [], 0, "add_arrived", 4)
        got = swap(send, "seq", 1)
        at = {"send": send}

        def branch_rows(point, value):
            if CFG["share"] != point:
                return value
            mine, theirs = call(
                functools.partial(share_kernel, rows, width),
                rows_out + [((rows // 2, inner), BF16)],
                [],
                1,
                "share_rows",
                8,
            )(me, orders, after(branch, at[point]), *away_one)
            at["out"] = arrive(here_x, mine, swap(theirs, "seq", 1))[0]
            return tie("hold", value, at)

        one = tie("z1", one, at)
        z_one = swap(one, "dp", 1)
        keep = tie("halves", keep, {"z": z_one})
        keep = branch_rows("send", keep)
        own_two, *sent = call(halves_kernel, [piece_two] * 4, [], 1, "add_halves", 4)(me, keep, got)
        away_two = [swap(block, "seq", d) for block, d in zip(sent, SENT)]
        at.update(d2=away_two[0], d4=away_two[1], d6=away_two[2], own=own_two)
        (one,) = call(pair_kernel, [piece_one], [], 0, "add_pair", 4)(tie("pair", one, at), z_one)
        z_one = swap(one, "dp", 2)
        own_two = branch_rows("own", own_two)
        (two,) = call(sum_kernel, [piece_two], [], 0, "add_parts", 4)(own_two, *away_two)
        z_two = swap(two, "dp", 1)
        at["summed"], at["z"] = two, z_two
        two = branch_rows("summed", two)
        (two,) = pair_two(two, z_two)
        z_two = swap(two, "dp", 2)
        at["pair"] = two
        two = branch_rows("pair", two)
        (two,) = pair_two(two, z_two)
        at["total"] = two
        branch_rows("total", two)
        (one,) = call(pair_beside_kernel, [beside_one], [], 0, "add_pair_beside_rows", 8)(
            one, z_one, tie("m3", back, at)
        )
        away_one = [swap(one, "seq", d) for d in SENT[:3]]
        if CFG["d"] == "ag":
            whole = lax.all_gather(two, "seq").reshape(4, 2, *two.shape).swapaxes(0, 1).reshape(2, half_two, inner)
            at["d2"] = at["d4"] = at["d6"] = whole
        else:
            away_two = [swap(two, "seq", d) for d in SENT[:3]]
            at.update(d2=away_two[0], d4=away_two[1], d6=away_two[2])
        mine, theirs, own_one = call(
            functools.partial(share_kernel, rows, width),
            rows_out + [((rows // 2 + half_one, inner), BF16), ((half_one, inner), BF16)],
            [],
            1,
            "share_rows_and_parts",
            12,
        )(me, orders, tie("share3", one, at), *away_one)
        other_one = swap(theirs, "seq", 1)
        (input_grad,) = arrive(here_dy, mine, other_one)
        output = at["out"]
        if CFG["d"] == "ag":
            totals = (own_one, other_one, whole[0], whole[1])
        else:
            (own_two,) = call(chips_kernel, [((half_two, inner), BF16)], [], 1, "order_parts", 4)(me, two, *away_two)
            totals = (own_one, other_one, own_two, swap(own_two, "seq", 1))
    else:
        totals = [lax.psum(half.astype(F32), ("dp", "seq")).astype(BF16) for half in (*first, keep, send)]
        place = call(functools.partial(place_kernel, rows, n), [((rows, width), BF16)], [], 1, "to_hilbert", 24)
        (output,) = place(me, here_x, orders, *spread_pieces(branch, "seq"))
        (input_grad,) = place(me, here_dy, orders, *spread_pieces(back, "seq"))
    weights = call(
        functools.partial(unpack_kernel, sizes, (devices if cube else 0, devices if cube and CFG["d"] != "ag" else 0)),
        [
            ((width,), F32),
            ((width, 2 * inner), F32),
            ((taps, inner), F32),
            ((inner,), F32),
            ((rank + 2 * state, inner), F32),
            ((rank, inner), F32),
            ((inner,), F32),
            ((state, inner), F32),
            ((inner,), F32),
            ((inner, width), F32),
        ],
        [((2 * half_one, inner), BF16), ((2 * half_two, inner), BF16)],
        1,
        "unpack_sums",
        24,
        2.4,
    )(me, *totals)
    turned = [v.T if v.ndim == 2 and v.shape[1] == inner and v.shape[0] != rank else v for v in weights]
    return (output[None], input_grad[None], *turned)


def solution(mesh):
    placed = (
        P("dp", "seq", None),
        P("dp", None),
        P("dp", "seq"),
        P(),
        P(),
        P(),
        P(),
        P(),
        P(),
        P(),
        P(),
        P(),
        P(),
        P("dp", "seq", None),
    )
    return jax.shard_map(
        shards,
        mesh=mesh,
        in_specs=placed,
        out_specs=(
            P("dp", "seq", None),
            P("dp", "seq", None),
            P(),
            P(),
            P(),
            P(),
            P(),
            P(),
            P(),
            P(),
            P(),
            P(),
        ),
        check_vma=False,
    )
```

```python
import functools

import jax
import jax.numpy as jnp
from jax import lax
from jax.experimental import pallas as pl
from jax.experimental.pallas import tpu as pltpu
from jax.sharding import PartitionSpec as P

EPSILON = 1e-05
LOG2E = 1.4426950408889634
FAR = 1e30
CHUNKS = 8
LANES = 128
BLOCK = 16
CUBE = (0, 2, 4, 6, 1, 3, 5, 7)
SENT = (2, 4, 6, 1)
ORDER_ROWS = 16
F32, BF16 = jnp.float32, jnp.bfloat16
MIB = 1024 * 1024


def dot(a, b, contract=((1,), (0,))):
    return lax.dot_general(a, b, (contract, ((), ())), preferred_element_type=F32)


def as_row(ref):
    return ref[...].reshape(1, ref.shape[0])


def wide(tile, width):
    return jnp.concatenate([tile] * (width // LANES), axis=1)


def sigmoid(v):
    return 1.0 / (1.0 + jnp.exp(-v))


def scalars(me, lengths, rows):
    begin, meta = jnp.int32(0), [me[0] * rows]
    for k in range(lengths.shape[1]):
        meta.append(begin)
        begin = begin + lengths[0, k]
    return meta


def source(me, p, n_pieces):
    return jnp.bitwise_xor(me[0], CUBE[p]) if n_pieces == len(CUBE) else jnp.int32(p)


def places(first, rows, r0, steps):
    r = r0 + lax.broadcasted_iota(jnp.int32, (rows, LANES), 0)
    return first + lax.rem(r, CHUNKS) * steps + lax.div(r, CHUNKS)


def cloud_start(meta, clouds, place):
    start = jnp.zeros_like(place)
    for k in range(clouds):
        begin = meta[1 + k]
        start = jnp.maximum(start, jnp.where(begin <= place, begin, 0))
    return start


def fill_valid(valid, meta, clouds, rows, lags):
    steps = rows // CHUNKS

    def body(j, carry):
        r0 = pl.multiple_of(j * BLOCK, BLOCK)
        place = places(meta[0], BLOCK, r0, steps)
        begin = cloud_start(meta, clouds, place)
        for k in range(1, lags + 1):
            valid[k - 1, pl.ds(r0, BLOCK), :] = (place - k >= begin).astype(F32)
        return carry

    lax.fori_loop(0, rows // BLOCK, body, 0)


def row_of_place(rows):
    place = lax.broadcasted_iota(jnp.int32, (rows, rows), 0)
    row = lax.broadcasted_iota(jnp.int32, (rows, rows), 1)
    return (place == lax.rem(row, CHUNKS) * (rows // CHUNKS) + lax.div(row, CHUNKS)).astype(F32).astype(BF16)


def gather_rows(column, pieces, me, rows):
    lane = lax.broadcasted_iota(jnp.int32, (column.shape[0], rows), 1).astype(F32)
    mine = [
        (column - (source(me, p, len(pieces)) * rows).astype(F32) == lane).astype(F32).astype(BF16)
        for p in range(len(pieces))
    ]
    return dot(jnp.concatenate(mine, axis=1), jnp.concatenate(pieces, axis=0))


def fill_broadcast(out, xproj, first, count):
    whole = xproj[...]
    high = whole.astype(BF16)
    low = (whole - high.astype(F32)).astype(BF16)
    row = lax.rem(lax.broadcasted_iota(jnp.int32, (2 * LANES, LANES), 0), LANES)
    for n in range(count):
        pick = (row == first + n).astype(F32).astype(BF16)
        out[:, n * LANES : (n + 1) * LANES] = dot(jnp.concatenate([high, low], axis=1), pick)


def rates(alog):
    return -jnp.exp(alog[...])


def chunk_of(ref, c, count):
    return jnp.concatenate([ref[b, pl.ds(c, count, stride=CHUNKS), :] for b in range(ref.shape[0])], axis=1)


def set_chunk(ref, c, value):
    for b in range(ref.shape[0]):
        ref[b, pl.ds(c, value.shape[0], stride=CHUNKS), :] = value[:, b * LANES : (b + 1) * LANES]


def payload_kernel(tokens, order, out, near, copied):
    rows, width = tokens.shape
    copies = [
        pltpu.make_async_copy(order, near, copied.at[0]),
        pltpu.make_async_copy(tokens, out.at[pl.ds(0, rows)], copied.at[1]),
    ]
    for copy in copies:
        copy.start()
    out[rows:, :] = jnp.zeros((ORDER_ROWS, width), BF16)
    copies[0].wait()
    out[rows:, 0:rows] = order_digits(near)
    copies[1].wait()


def order_column(to_row, digits):
    both = dot(to_row, digits, ((0,), (1,)))
    return jnp.broadcast_to(both[:, 0:1] * 128.0 + both[:, 1:2], (to_row.shape[0], LANES))


def order_digits(order):
    sub = lax.broadcasted_iota(jnp.int32, (ORDER_ROWS, order.shape[1]), 0)
    digits = jnp.where(sub == 0, order[...] >> 7, jnp.where(sub == 1, order[...] & 127, 0))
    return digits.astype(F32).astype(BF16)


def pre_kernel(sizes, n_pieces, n_far, me, *refs):
    rows, width, inner, rank, state, lags, clouds = sizes
    steps = rows // CHUNKS
    pieces = refs[:n_pieces]
    far_refs, refs = refs[n_pieces : n_pieces + n_far], refs[:n_pieces] + refs[n_pieces + n_far :]
    near_refs, copied, refs = refs[-n_far - 1 : -1], refs[-1], refs[: -n_far - 1]
    copies = [pltpu.make_async_copy(a, b, copied.at[k]) for k, (a, b) in enumerate(zip(far_refs, near_refs))]
    for copy in copies:
        copy.start()
    (lengths, order, gain, w_in, conv_w, conv_b, w_x, w_dt, dt_b, alog, skip) = near_refs
    copies[1].wait()
    (trans_o, normed_o, gate_o, ext_o, conv_o, act_o, step_o, xproj_o, chunkf_o, sums_o, f_o, column_o, orders_o,
     valid, far, use, bbc, wx_o, wdt_o, a2, rows_o, conv_in) = refs[n_pieces:]
    to_row = row_of_place(rows)
    sub = lax.broadcasted_iota(jnp.int32, (BLOCK, LANES), 0)
    extra = jnp.full((BLOCK, LANES), -1.0, F32)
    tail = jnp.zeros((ORDER_ROWS, rows), F32)
    for p in range(n_pieces):
        now = pieces[p][rows : rows + ORDER_ROWS, :rows]
        tail = jnp.where(source(me, p, n_pieces) == me[0] - 1, now.astype(F32), tail)
        if p < orders_o.shape[0]:
            row = dot(now, to_row)
            orders_o[p : p + 1, :] = row[0:1] * 128.0 + row[1:2]
    for k in range(1, lags + 1):
        extra = jnp.where(sub == k, tail[0:1, rows - k : rows - k + 1] * 128.0 + tail[1:2, rows - k : rows - k + 1], extra)
    own = order_column(to_row, order_digits(order))
    column_o[0] = own
    if n_pieces == len(CUBE):
        column_o[1] = order_column(to_row, pieces[CUBE.index(1)][rows : rows + ORDER_ROWS, :rows])
    column = jnp.concatenate([own, extra], axis=0)
    trans = gather_rows(wide(column, rows), [p[0:rows, :] for p in pieces], me, rows)
    trans_o[...] = trans[:rows].astype(BF16)
    for copy in copies[:1] + copies[2:]:
        copy.wait()
    meta = scalars(me, lengths, rows)
    bias, dt_bias = as_row(conv_b), as_row(dt_b)
    rows_o[0 : lags + 1, :] = conv_w[...]
    rows_o[lags + 1 : lags + 2, :] = as_row(skip)
    inv_rms = lax.rsqrt(jnp.mean(trans * trans, axis=1, keepdims=True) + EPSILON)
    normed = (trans * inv_rms * as_row(gain)).astype(BF16)
    normed_o[...] = normed[:rows]
    conv_in[...] = dot(normed, w_in[:, :inner]).astype(BF16).astype(F32)
    gate_o[...] = dot(normed[:rows], w_in[:, inner:])
    pad = lags * CHUNKS
    ext_o[pad : pad + rows, :] = conv_in[:rows, :]
    first_sub = lax.broadcasted_iota(jnp.int32, (CHUNKS, inner), 0) == 0
    for k in range(1, lags + 1):
        tile = conv_in[(steps - k) * CHUNKS : (steps - k + 1) * CHUNKS, :]
        before = conv_in[rows + k : rows + k + 1, :]
        ext_o[(lags - k) * CHUNKS : (lags - k + 1) * CHUNKS, :] = jnp.where(
            first_sub, before, pltpu.roll(tile, 1, 0)
        )
    for thin, full in ((w_x, wx_o), (w_dt, wdt_o)):
        blank = jnp.zeros((LANES - thin.shape[0], inner), F32)
        full[...] = jnp.concatenate([thin[...].astype(F32), blank], axis=0).astype(BF16)
    fill_valid(valid, meta, clouds, rows, lags)

    def conv_body(j, carry):
        r0 = pl.multiple_of(j * BLOCK, BLOCK)
        out = bias + conv_w[lags : lags + 1, :] * ext_o[pl.ds(r0 + pad, BLOCK), :]
        for k in range(1, lags + 1):
            ok = wide(valid[k - 1, pl.ds(r0, BLOCK), :], inner)
            shifted = ext_o[pl.ds(pl.multiple_of(r0 + pad - k * CHUNKS, CHUNKS), BLOCK), :]
            out = out + conv_w[lags - k : lags - k + 1, :] * shifted * ok
        conv_o[pl.ds(r0, BLOCK), :] = out
        act_o[pl.ds(r0, BLOCK), :] = (out * sigmoid(out)).astype(BF16)
        return carry

    lax.fori_loop(0, rows // BLOCK, conv_body, 0)
    xproj = dot(act_o[...], wx_o[...], ((1,), (1,)))
    xproj_o[...] = xproj
    step_o[...] = dot(xproj.astype(BF16), wdt_o[...])

    def step_body(j, carry):
        r0 = pl.multiple_of(j * BLOCK, BLOCK)
        pre = step_o[pl.ds(r0, BLOCK), :] + dt_bias
        step = jnp.maximum(pre, 0.0) + jnp.log1p(jnp.exp(-jnp.abs(pre)))
        step_o[pl.ds(r0, BLOCK), :] = step
        keep = wide(valid[0, pl.ds(r0, BLOCK), :], inner)
        distance = jnp.where(keep > 0.5, step, FAR)
        far[pl.ds(r0, BLOCK), :] = distance
        use[pl.ds(r0, BLOCK), :] = step * act_o[pl.ds(r0, BLOCK), :].astype(F32)
        return carry + distance[:CHUNKS] + distance[CHUNKS:]

    sums_o[...] = lax.fori_loop(0, rows // BLOCK, step_body, jnp.zeros((CHUNKS, inner), F32))
    fill_broadcast(bbc, xproj_o, rank, state)
    a2[...] = rates(alog) * LOG2E
    for lb in range(inner // LANES):
        ls = slice(lb * LANES, (lb + 1) * LANES)
        rate = [jnp.broadcast_to(a2[n : n + 1, ls], (CHUNKS, LANES)) for n in range(state)]

        def scan_body(i, states):
            r = pl.ds(pl.multiple_of(i * CHUNKS, CHUNKS), CHUNKS)
            distance, u = far[r, ls], use[r, ls]
            return tuple(
                jnp.exp2(distance * rate[n]) * states[n] + u * bbc[r, n * LANES : (n + 1) * LANES]
                for n in range(state)
            )

        zero = jnp.zeros((CHUNKS, LANES), F32)
        last = lax.fori_loop(0, steps, scan_body, (zero,) * state, unroll=8)
        for n in range(state):
            chunkf_o[lb, n * CHUNKS : (n + 1) * CHUNKS, :] = last[n]
    total = jnp.zeros((state, inner), F32)
    for c in range(CHUNKS):
        total = jnp.exp2(a2[...] * sums_o[c : c + 1, :]) * total + chunk_of(chunkf_o, c, state)
    f_o[...] = total


def gather_kernel(core, me, column, own, two, four, six, out):
    rows = own.shape[0]
    whole = jnp.concatenate([p[...] for p in (own, two, four, six)], axis=0)
    lane = lax.broadcasted_iota(jnp.int32, (rows, rows), 1).astype(F32)
    place = wide(column[core], rows)
    match = [(place - (source(me, p, len(CUBE)) * rows).astype(F32) == lane).astype(F32).astype(BF16) for p in range(4)]
    out[...] = dot(jnp.concatenate(match, axis=1), whole).astype(BF16)


def back_kernel(sizes, n_pieces, me, *refs):
    rows, width, inner, rank, state, lags, clouds = sizes
    steps = rows // CHUNKS
    pieces = refs[:n_pieces]
    gate, far, xproj, a2, w_out, sums, f, column = refs[n_pieces : n_pieces + 8]
    n_out = len(SENT) if n_pieces == 2 else 1
    dy_o, gg_o, gm, cbc, chunkb_o, near_out = refs[n_pieces + 8 : n_pieces + 14]
    carries_o = refs[n_pieces + 14 : n_pieces + 14 + n_out]
    (copied,) = refs[n_pieces + 14 + n_out :]
    copy = pltpu.make_async_copy(w_out, near_out, copied)
    copy.start()
    if n_pieces == 2:
        trans_dy = (pieces[0][...].astype(F32) + pieces[1][...].astype(F32)).astype(BF16)
    else:
        trans_dy = gather_rows(wide(column[0], rows), [p[...] for p in pieces], me, rows).astype(BF16)
    dy_o[...] = trans_dy
    copy.wait()
    gg_o[...] = dot(trans_dy, near_out[...], ((1,), (1,)))

    def body(j, carry):
        r = pl.ds(pl.multiple_of(j * BLOCK, BLOCK), BLOCK)
        z = gate[r, :]
        gm[r, :] = gg_o[r, :] * (z * sigmoid(z))
        return carry

    lax.fori_loop(0, rows // BLOCK, body, 0)
    fill_broadcast(cbc, xproj, rank + state, state)
    for lb in range(inner // LANES):
        ls = slice(lb * LANES, (lb + 1) * LANES)
        rate = [jnp.broadcast_to(a2[n : n + 1, ls], (CHUNKS, LANES)) for n in range(state)]

        def scan_body(k, flows):
            r = pl.ds(pl.multiple_of((steps - 1 - k) * CHUNKS, CHUNKS), CHUNKS)
            distance, g = far[r, ls], gm[r, ls]
            return tuple(
                jnp.exp2(distance * rate[n]) * (flows[n] + g * cbc[r, n * LANES : (n + 1) * LANES])
                for n in range(state)
            )

        zero = jnp.zeros((CHUNKS, LANES), F32)
        last = lax.fori_loop(0, steps, scan_body, (zero,) * state, unroll=8)
        for n in range(state):
            chunkb_o[lb, n * CHUNKS : (n + 1) * CHUNKS, :] = last[n]
    total = jnp.zeros((state, inner), F32)
    for c in reversed(range(CHUNKS)):
        total = jnp.exp2(a2[...] * sums[c : c + 1, :]) * total + chunk_of(chunkb_o, c, state)
    passed = jnp.sum(sums[...], axis=0, keepdims=True)
    blocks = inner // LANES
    passed = jnp.concatenate([passed[:, b * LANES : (b + 1) * LANES] for b in range(blocks)], axis=0)
    passed = jnp.concatenate([passed, jnp.zeros((state - blocks, LANES), F32)], axis=0)
    if n_out == 1:
        carries_o[0][:state, :inner] = f[...]
        carries_o[0][state:, :inner] = total
        carries_o[0][:state, inner:] = passed
        carries_o[0][state:, inner:] = passed
        return
    for out, d in zip(carries_o, SENT):
        later = jnp.bitwise_xor(me[0], d) > me[0]
        out[:, :inner] = jnp.where(later, f[...], total)
        out[:, inner:] = passed


def core_of(me, devices):
    return jnp.bitwise_and(me, 1) if devices == len(CUBE) else jnp.int32(0)


def hold_carries(held, carries, me):
    n_pieces, count, inner = len(carries), carries[0].shape[0], held.shape[1]
    devices = len(CUBE) if n_pieces == len(CUBE) - 1 else n_pieces
    size = count + CHUNKS
    for p in range(n_pieces):
        whence = source(me, p + 1, devices) if devices > n_pieces else p
        base = whence * size
        held[pl.ds(pl.multiple_of(base, CHUNKS), count), :] = carries[p][:, :inner]
        passed = [carries[p][b : b + 1, inner:] for b in range(inner // LANES)]
        passed = jnp.broadcast_to(jnp.concatenate(passed, axis=1), (CHUNKS, inner))
        held[pl.ds(pl.multiple_of(base + count, CHUNKS), CHUNKS), :] = passed
    return devices, size


def scan_forward_kernel(sizes, n_pieces, me_ref, *refs):
    rows, width, inner, rank, state, lags, clouds = sizes
    steps = rows // CHUNKS
    carries = refs[:n_pieces]
    (trans_dy, normed, gg, gate, act, far, use, bbc, cbc, chunkf, sums, a2, consts) = refs[n_pieces : n_pieces + 13]
    blocks = inner // LANES
    states = refs[n_pieces + 13 : n_pieces + 13 + blocks]
    (gated, gz_o, keep_o, send_o) = refs[n_pieces + 13 + blocks : n_pieces + 17 + blocks]
    (mixed, sstart, held) = refs[n_pieces + 17 + blocks :]
    me = me_ref[0]
    skips = consts[lags + 1 : lags + 2, :]
    devices, size = hold_carries(held, carries, me_ref)

    def ahead(s, flow):
        base = pl.multiple_of(s * size, CHUNKS)
        p_s = jnp.exp2(a2[...] * held[pl.ds(base + size - CHUNKS, 1), :])
        return jnp.where(s < me, p_s * flow + held[pl.ds(base, state), :], flow)

    now = lax.fori_loop(0, devices, ahead, jnp.zeros((state, inner), F32))
    for c in range(CHUNKS):
        set_chunk(sstart, c, now)
        now = jnp.exp2(a2[...] * sums[c : c + 1, :]) * now + chunk_of(chunkf, c, state)

    for lb in range(inner // LANES):
        ls = slice(lb * LANES, (lb + 1) * LANES)
        rate = [jnp.broadcast_to(a2[n : n + 1, ls], (CHUNKS, LANES)) for n in range(state)]
        begin = []
        for n in range(state):
            tile = sstart[lb, n * CHUNKS : (n + 1) * CHUNKS, :]
            states[lb][n, 0:CHUNKS, :] = tile
            begin.append(tile)

        def forward(i, now):
            r0 = pl.multiple_of(i * CHUNKS, CHUNKS)
            r = pl.ds(r0, CHUNKS)
            nxt = pl.ds(pl.multiple_of(r0 + CHUNKS, CHUNKS), CHUNKS)
            distance, u = far[r, ls], use[r, ls]
            new, out = [], None
            for n in range(state):
                value = jnp.exp2(distance * rate[n]) * now[n] + u * bbc[r, n * LANES : (n + 1) * LANES]
                states[lb][n, nxt, :] = value
                part = value * cbc[r, n * LANES : (n + 1) * LANES]
                out = part if out is None else out + part
                new.append(value)
            mixed[r, ls] = out
            return tuple(new)

        lax.fori_loop(0, steps, forward, tuple(begin), unroll=8)

    def gating(j, carry):
        r = pl.ds(pl.multiple_of(j * BLOCK, BLOCK), BLOCK)
        z, a = gate[r, :], act[r, :].astype(F32)
        s = sigmoid(z)
        m = mixed[r, :] + skips * a
        gated[r, :] = (m * (z * s)).astype(BF16)
        gz_o[r, :] = (gg[r, :] * m * s * (1.0 + z * (1.0 - s))).astype(BF16)
        return carry

    lax.fori_loop(0, rows // BLOCK, gating, 0)
    second = core_of(me, devices) == 1
    wout_g = dot(trans_dy[...], gated[...], ((0,), (0,))).astype(BF16)
    gate_g = dot(normed[...], gz_o[...], ((0,), (0,))).astype(BF16)
    keep_o[...] = jnp.where(second, gate_g, wout_g)
    send_o[...] = jnp.where(second, wout_g, gate_g)


def branch_kernel(sizes, n_pieces, me_ref, *refs):
    rows, width, inner, rank, state, lags, clouds = sizes
    carries = refs[:n_pieces]
    chunkb, sums, a2, gated, w_out, gstart, branch_o, held = refs[n_pieces:]
    me = me_ref[0]
    branch_o[...] = dot(gated[...], w_out[...]).astype(BF16)
    devices, size = hold_carries(held, carries, me_ref)
    back = size - CHUNKS - state

    def behind(k, flow):
        s = devices - 1 - k
        base = pl.multiple_of(s * size, CHUNKS)
        p_s = jnp.exp2(a2[...] * held[pl.ds(base + size - CHUNKS, 1), :])
        return jnp.where(s > me, p_s * flow + held[pl.ds(pl.multiple_of(base + back, CHUNKS), state), :], flow)

    now = lax.fori_loop(0, devices, behind, jnp.zeros((state, inner), F32))
    for c in reversed(range(CHUNKS)):
        set_chunk(gstart, c, now)
        now = jnp.exp2(a2[...] * sums[c : c + 1, :]) * now + chunk_of(chunkb, c, state)


def scan_backward_kernel(sizes, *refs):
    rows, width, inner, rank, state, lags, clouds = sizes
    steps = rows // CHUNKS
    states, refs = refs[: inner // LANES], refs[inner // LANES :]
    (gstart, far, use, bbc, cbc, gm, step, act, conv, valid, a2, conv_w, w_x, w_dt) = refs[:14]
    (gconv, rim_o, gpre, gxproj_o, galog_o) = refs[14:19]
    (gs, lamb, gb, gc) = refs[19:]
    skips = conv_w[lags + 1 : lags + 2, :]
    group, pair = 3, 4
    for lg in range(inner // LANES // group):
        lanes = [slice((lg * group + k) * LANES, (lg * group + k + 1) * LANES) for k in range(group)]
        for ng in range(state // pair):
            ns = [ng * pair + k for k in range(pair)]
            rate = [[jnp.broadcast_to(a2[n : n + 1, ls], (CHUNKS, LANES)) for ls in lanes] for n in ns]
            begin = [gstart[lg * group + k, n * CHUNKS : (n + 1) * CHUNKS, :] for n in ns for k in range(group)]
            zero = jnp.zeros((CHUNKS, LANES), F32)

            def backward(k, carry):
                flows, sums_a = carry
                r0 = pl.multiple_of((steps - 1 - k) * CHUNKS, CHUNKS)
                r = pl.ds(r0, CHUNKS)
                nxt = pl.ds(pl.multiple_of(r0 + CHUNKS, CHUNKS), CHUNKS)
                gs_t = [None] * group
                lamb_t = [None] * group
                g_t = [gm[r, ls] for ls in lanes]
                u_t = [use[r, ls] for ls in lanes]
                d_t = [step[r, ls] for ls in lanes]
                f_t = [far[r, ls] for ls in lanes]
                new_flows, new_sums = [], []
                for q, n in enumerate(ns):
                    b = bbc[r, n * LANES : (n + 1) * LANES]
                    c = cbc[r, n * LANES : (n + 1) * LANES]
                    gb_t = gc_t = None
                    for x, ls in enumerate(lanes):
                        lam = g_t[x] * c + flows[q * group + x]
                        flow = jnp.exp2(f_t[x] * rate[q][x]) * lam
                        part = flow * states[lg * group + x][n, r, :]
                        one, two = part * rate[q][x], lam * b
                        gs_t[x] = one if gs_t[x] is None else gs_t[x] + one
                        lamb_t[x] = two if lamb_t[x] is None else lamb_t[x] + two
                        three, four = lam * u_t[x], g_t[x] * states[lg * group + x][n, nxt, :]
                        gb_t = three if gb_t is None else gb_t + three
                        gc_t = four if gc_t is None else gc_t + four
                        new_flows.append(flow)
                        new_sums.append(sums_a[q * group + x] + part * d_t[x])
                    nl = slice(n * LANES, (n + 1) * LANES)
                    if lg == 0:
                        gb[r, nl] = gb_t
                        gc[r, nl] = gc_t
                    else:
                        gb[r, nl] += gb_t
                        gc[r, nl] += gc_t
                for x, ls in enumerate(lanes):
                    if ng == 0:
                        gs[r, ls] = gs_t[x]
                        lamb[r, ls] = lamb_t[x]
                    else:
                        gs[r, ls] += gs_t[x]
                        lamb[r, ls] += lamb_t[x]
                return tuple(new_flows), tuple(new_sums)

            flows, sums_a = lax.fori_loop(
                0, steps, backward, (tuple(begin), (zero,) * (pair * group)), unroll=8
            )
            for q, n in enumerate(ns):
                for x, ls in enumerate(lanes):
                    galog_o[n : n + 1, ls] = (
                        jnp.sum(sums_a[q * group + x], axis=0, keepdims=True) * rate[q][x][0:1] * (1.0 / LOG2E)
                    )
    col = lax.broadcasted_iota(jnp.int32, (state * LANES, LANES), 1)
    row = lax.div(lax.broadcasted_iota(jnp.int32, (state * LANES, LANES), 0), LANES)
    pick_b = (col == row + rank).astype(F32).astype(BF16)
    pick_c = (col == row + rank + state).astype(F32).astype(BF16)

    def lane_sums(ref, pick):
        whole = ref[...]
        high = whole.astype(BF16)
        low = (whole - high.astype(F32)).astype(BF16)
        return dot(high, pick) + dot(low, pick)

    grad_bc = lane_sums(gb, pick_b) + lane_sums(gc, pick_c)

    def pre_body(j, carry):
        r = pl.ds(pl.multiple_of(j * BLOCK, BLOCK), BLOCK)
        grad_step = gs[r, :] * (1.0 / LOG2E) + lamb[r, :] * act[r, :].astype(F32)
        gpre[r, :] = (grad_step * (1.0 - jnp.exp(-step[r, :]))).astype(BF16)
        return carry

    lax.fori_loop(0, rows // BLOCK, pre_body, 0)
    grad_xproj = (dot(gpre[...], w_dt[...], ((1,), (1,))) + grad_bc).astype(BF16)
    gxproj_o[...] = grad_xproj
    gs[...] = dot(grad_xproj, w_x[...])

    def conv_body(j, carry):
        r = pl.ds(pl.multiple_of(j * BLOCK, BLOCK), BLOCK)
        grad_act = gm[r, :] * skips + lamb[r, :] * step[r, :] + gs[r, :]
        v = conv[r, :]
        s = sigmoid(v)
        gconv[r, :] = grad_act * (s * (1.0 + v * (1.0 - s)))
        return carry

    lax.fori_loop(0, rows // BLOCK, conv_body, 0)
    rim_o[...] = jnp.zeros((CHUNKS, inner), F32)
    for b in range(1, lags + 1):
        total = jnp.zeros((1, inner), F32)
        for k in range(b, lags + 1):
            total = total + masked_tile(gconv, valid, conv_w, k - b, k, lags)[0:1]
        rim_o[b : b + 1, :] = total


def masked_tile(gconv, valid, conv_w, i, k, lags):
    r = pl.ds(pl.multiple_of(i * CHUNKS, CHUNKS), CHUNKS)
    tile = gconv[r, :] * conv_w[lags - k : lags - k + 1, :]
    return tile if k == 0 else tile * wide(valid[k - 1, r, :], tile.shape[1])


def small_kernel(sizes, gpre, gxproj, xproj, act, gconv, ext, valid, gm, conv_w, galog, small_o, gci_o):
    rows, width, inner, rank, state, lags, clouds = sizes
    steps = rows // CHUNKS

    def spread(i, carry):
        total = masked_tile(gconv, valid, conv_w, i, 0, lags)
        for k in range(1, lags + 1):
            total = total + masked_tile(gconv, valid, conv_w, i + k, k, lags)
        gci_o[pl.ds(pl.multiple_of(i * CHUNKS, CHUNKS), CHUNKS), :] = total
        return carry

    lax.fori_loop(0, steps - lags, spread, 0)
    sub = lax.broadcasted_iota(jnp.int32, (CHUNKS, inner), 0)
    for i in range(steps - lags, steps):
        total = masked_tile(gconv, valid, conv_w, i, 0, lags)
        for k in range(1, lags + 1):
            if i + k < steps:
                total = total + masked_tile(gconv, valid, conv_w, i + k, k, lags)
            else:
                moved = pltpu.roll(masked_tile(gconv, valid, conv_w, i + k - steps, k, lags), CHUNKS - 1, 0)
                total = total + jnp.where(sub == CHUNKS - 1, 0.0, moved)
        gci_o[i * CHUNKS : (i + 1) * CHUNKS, :] = total

    def sum_body(j, carry):
        r0 = pl.multiple_of(j * BLOCK, BLOCK)
        r = pl.ds(r0, BLOCK)
        grad = gconv[r, :]
        parts = [gm[r, :] * act[r, :].astype(F32), gpre[r, :].astype(F32), grad]
        for k in reversed(range(lags + 1)):
            masked = grad if k == 0 else grad * wide(valid[k - 1, r, :], inner)
            parts.append(masked * ext[pl.ds(pl.multiple_of(r0 + (lags - k) * CHUNKS, CHUNKS), BLOCK), :])
        return tuple(total + part[:CHUNKS] + part[CHUNKS:] for total, part in zip(carry, parts))

    sums = lax.fori_loop(0, rows // BLOCK, sum_body, (jnp.zeros((CHUNKS, inner), F32),) * (lags + 4))
    small_o[0:state, :] = galog[...]
    at = state
    small_o[at : at + rank + 2 * state, :] = dot(gxproj[...], act[...], ((0,), (0,)))[: rank + 2 * state]
    at += rank + 2 * state
    small_o[at : at + rank, :] = dot(xproj[...].astype(BF16), gpre[...], ((0,), (0,)))[:rank]
    at += rank
    for k, part in enumerate(sums):
        small_o[at + k : at + k + 1, :] = jnp.sum(part, axis=0, keepdims=True)
    at += len(sums)
    small_o[at:, :] = jnp.zeros((small_o.shape[0] - at, inner), F32)


def final_kernel(sizes, devices, me, trans, normed, gci, gz, rim, small, gain, w_in, back_o, keep_o, send_o, both):
    rows, width, inner, rank, state, lags, clouds = sizes
    steps = rows // CHUNKS
    r = lax.broadcasted_iota(jnp.int32, (rows, inner), 0)
    total = gci[...]
    for k in range(1, lags + 1):
        total = total + jnp.where(r == (steps - k) * CHUNKS + CHUNKS - 1, rim[k : k + 1, :], 0.0)
    grad_ci = total.astype(BF16)
    grad_z = gz[...]
    grad_normed = dot(grad_ci, w_in[:, :inner], ((1,), (1,))) + dot(grad_z, w_in[:, inner:], ((1,), (1,)))
    x = trans[...].astype(F32)
    inv_rms = lax.rsqrt(jnp.mean(x * x, axis=1, keepdims=True) + EPSILON)
    scaled = grad_normed * as_row(gain)
    back_o[...] = (
        inv_rms * scaled
        - inv_rms * inv_rms * inv_rms * x * jnp.mean(scaled * x, axis=1, keepdims=True)
    ).astype(BF16)
    both[0:width, :] = dot(normed[...], grad_ci, ((0,), (0,))).astype(BF16)
    gain_row = jnp.sum(grad_normed * x * inv_rms, axis=0, keepdims=True)
    gain_row = jnp.concatenate([gain_row, jnp.zeros((1, inner - width), F32)], axis=1)
    n_small = small.shape[0]
    last = lax.broadcasted_iota(jnp.int32, (n_small, inner), 0) == n_small - 1
    both[width : width + n_small, :] = jnp.where(last, gain_row, small[...]).astype(BF16)
    half = keep_o.shape[0]
    core = core_of(me[0], devices)
    keep_o[...] = both[pl.ds(pl.multiple_of(core * half, BLOCK), half), :]
    send_o[...] = both[pl.ds(pl.multiple_of((1 - core) * half, BLOCK), half), :]


def small_rows(sizes):
    rows, width, inner, rank, state, lags, clouds = sizes
    return state + (rank + 2 * state) + rank + 3 + lags + 1 + 1


def halves_kernel(me, kept, got, own_o, *sent_o):
    part = own_o.shape[0]
    chip = lax.div(me[0], 2)
    for d, out in enumerate((own_o,) + sent_o):
        r = pl.ds(pl.multiple_of(jnp.bitwise_xor(chip, d) * part, BLOCK), part)
        out[...] = (kept[r, :].astype(F32) + got[r, :].astype(F32)).astype(BF16)


def beside(out, rows):
    half, width = rows.shape[0] // 2, rows.shape[1]
    out[0:half, 0:width] = rows[0:half, :]
    out[0:half, width:] = rows[half:, :]


def unfold(piece, rows, width):
    if piece.shape == (rows, width):
        return piece[...]
    half = rows // 2
    return jnp.concatenate([piece[0:half, 0:width], piece[0:half, width : 2 * width]], axis=0)


def halves_beside_kernel(me, kept, got, rows, own_o, *sent_o):
    part = own_o.shape[0]
    half = rows.shape[0] // 2
    chip = lax.div(me[0], 2)
    for d, out in enumerate((own_o,) + sent_o):
        r = pl.ds(pl.multiple_of(jnp.bitwise_xor(chip, d) * part, BLOCK), part)
        total = (kept[r, :].astype(F32) + got[r, :].astype(F32)).astype(BF16)
        if d == 0:
            out[...] = total
        else:
            beside(out, rows)
            out[half:, :] = total


def sum_kernel(a, b, c, d, out):
    one, two, three, four = (x[x.shape[0] - a.shape[0] :, :].astype(F32) for x in (a, b, c, d))
    out[...] = ((one + two) + (three + four)).astype(BF16)


def pair_kernel(a, b, out):
    out[...] = (a[...].astype(F32) + b[...].astype(F32)).astype(BF16)


def pair_beside_kernel(a, b, rows, out):
    beside(out, rows)
    out[rows.shape[0] // 2 :, :] = (a[...].astype(F32) + b[...].astype(F32)).astype(BF16)


def by_chip(out, first, parts, me, part):
    for d, piece in enumerate(parts):
        chip = jnp.bitwise_xor(lax.div(me[0], 2), d)
        out[pl.ds(pl.multiple_of(first + chip * part, BLOCK), part), :] = piece[piece.shape[0] - part :, :]


def stack_kernel(a, b, out):
    out[0 : a.shape[0], :] = a[...]
    out[a.shape[0] :, :] = b[...]


def both_chips_kernel(part_a, part_b, me, own, two, four, six, out):
    for d, piece in enumerate((own, two, four, six)):
        chip = jnp.bitwise_xor(lax.div(me[0], 2), d)
        out[pl.ds(pl.multiple_of(chip * part_a, BLOCK), part_a), :] = piece[0:part_a, :]
        out[pl.ds(pl.multiple_of(4 * part_a + chip * part_b, BLOCK), part_b), :] = piece[part_a:, :]


def chips_kernel(me, own, two, four, six, out):
    by_chip(out, 0, (own, two, four, six), me, own.shape[0])


def share_kernel(rows, width, me, orders, own, two, four, six, mine_o, theirs_o, *half_o):
    pieces = (own, two, four, six)
    whole = jnp.concatenate([unfold(p, rows, width) for p in pieces], axis=0)
    for core, out in enumerate((mine_o, theirs_o)):
        first = jnp.bitwise_xor(me[0], core) * rows
        place = (first + lax.broadcasted_iota(jnp.int32, (rows, rows), 0)).astype(F32)
        match = [(orders[p : p + 1, :] == place).astype(F32).astype(BF16) for p in range(len(pieces))]
        moved = dot(jnp.concatenate(match, axis=1), whole).astype(BF16)
        if core == 0:
            out[...] = moved
        else:
            out[0 : rows // 2, 0:width] = moved[: rows // 2]
            out[0 : rows // 2, width:] = moved[rows // 2 :]
    for out in half_o:
        part = out.shape[0] // len(pieces)
        by_chip(out, 0, pieces, me, part)
        by_chip(theirs_o, rows // 2, pieces, me, part)


def share_both_kernel(rows, width, me, orders, *refs):
    one, two, (mine_one, mine_two, theirs_o) = refs[0:4], refs[4:8], refs[8:]
    share_kernel(rows, width, me, orders, *one, mine_one, theirs_o.at[pl.ds(0, rows // 2)])
    share_kernel(rows, width, me, orders, *two, mine_two, theirs_o.at[pl.ds(rows // 2, rows // 2)])


def arrive_both_kernel(here_one, here_two, mine_one, mine_two, theirs, out_one, out_two):
    half = here_one.shape[0] // 2
    arrive_kernel(here_one, mine_one, theirs.at[pl.ds(0, half)], out_one)
    arrive_kernel(here_two, mine_two, theirs.at[pl.ds(half, half)], out_two)


def arrive_kernel(here, mine, theirs, out):
    rows, width = here.shape
    moved = mine[...].astype(F32) + unfold(theirs, rows, width).astype(F32)
    out[...] = (here[...].astype(F32) + moved).astype(BF16)


def halves_of(own, other, me, devices):
    second = core_of(me[0], devices) == 1
    return jnp.where(second, other, own), jnp.where(second, own, other)


def first_results_kernel(half, devices, me, own, other, wout_o, win_o, turned, copied):
    wout, gate = halves_of(own[own.shape[0] - half :, :], other[other.shape[0] - half :, :], me, devices)
    turned[...] = gate.astype(F32)
    inner = turned.shape[1]
    copy = pltpu.make_async_copy(turned, win_o.at[:, pl.ds(inner, inner)], copied)
    copy.start()
    wout_o[...] = wout.astype(F32).T
    copy.wait()


def last_results_kernel(sizes, half, devices, me, own, other, win, *refs):
    rows, width, inner, rank, state, lags, clouds = sizes
    (gain_o, win_o, taps_o, convb_o, wx_o, wdt_o, dtb_o, alog_o, skip_o, near, copied) = refs
    first, second = halves_of(own[0:half, :], other[0:half, :], me, devices)
    whole = jnp.concatenate([first, second], axis=0)
    copies = []
    for k in range(width // LANES):
        r = pl.ds(k * LANES, LANES)
        near[r, :] = whole[k * LANES : (k + 1) * LANES].astype(F32)
        copies.append(pltpu.make_async_copy(near.at[r], win_o.at[r, pl.ds(0, inner)], copied.at[k]))
        copies[-1].start()
    n_small = small_rows(sizes)
    small = whole[width : width + n_small].astype(F32)
    alog_o[...] = small[0:state]
    at = state
    wx_o[...] = small[at : at + rank + 2 * state]
    at += rank + 2 * state
    wdt_o[...] = small[at : at + rank]
    at += rank
    for k, out in enumerate((skip_o, dtb_o, convb_o)):
        out[...] = small[at + k : at + k + 1].reshape(inner)
    at += 3
    taps_o[...] = small[at : at + lags + 1]
    gain_o[...] = small[n_small - 1 : n_small, :width].reshape(width)
    for copy in copies:
        copy.wait()


def place_kernel(rows, n_pieces, me, here, orders, *refs):
    pieces, out = refs[:n_pieces], refs[n_pieces]
    place = (me[0] * rows + lax.broadcasted_iota(jnp.int32, (rows, rows), 0)).astype(F32)
    mine = [(orders[p : p + 1, :] == place).astype(F32).astype(BF16) for p in range(n_pieces)]
    moved = dot(jnp.concatenate(mine, axis=1), jnp.concatenate([p[...] for p in pieces], axis=0))
    out[...] = (here[...].astype(F32) + moved).astype(BF16)


def call(kernel, outs, scratch, n_smem, name, room, time=1.0, far_ins=(), far_outs=(), aliases={}):
    vmem = pl.BlockSpec(memory_space=pltpu.VMEM)
    smem = pl.BlockSpec(memory_space=pltpu.SMEM)
    anywhere = pl.BlockSpec(memory_space=pltpu.HBM)

    def run(*args):
        args = [pltpu.with_memory_space_constraint(v, pltpu.HBM) if k in far_ins else v for k, v in enumerate(args)]
        return pl.pallas_call(
            kernel,
            out_shape=[jax.ShapeDtypeStruct(*part) if isinstance(part, tuple) else part for part in outs],
            in_specs=[smem if k < n_smem else anywhere if k in far_ins else vmem for k in range(len(args))],
            out_specs=[anywhere if k in far_outs else vmem for k in range(len(outs))],
            input_output_aliases=aliases,
            scratch_shapes=[pltpu.VMEM(*part) if isinstance(part, tuple) else part for part in scratch],
            compiler_params=pltpu.CompilerParams(vmem_limit_bytes=room * MIB),
            cost_estimate=pl.CostEstimate(
                flops=1, bytes_accessed=1, transcendentals=0
            ),
            name=name,
        )(*args)

    return run


CFG = {'adj': 'gstart', 'arrive': '', 'chips1': 'total', 'chips2': 'first', 'd': '', 'dy': 'd6', 'dy1': 'fwd', 'halves': '', 'hold': '', 'm3': 'own', 'one': 'b2+b4+b6+pair', 'p1d': 'z', 'pair': 'd2', 'rim': '', 'share': 'pair', 'share3': 'total', 'small': 'mid', 'z1': 'send', 'fin': '', 'sumz': 'z1'}


def tie(name, value, choices):
    pick = CFG.get(name, "")
    for k in pick.split("+") if pick else ():
        value = after(value, choices[k]) if k in choices else value
    return value


def after(value, *others):
    return lax.optimization_barrier((value, others))[0]


def swap(block, axis, distance):
    devices = lax.axis_size(axis)
    return lax.ppermute(block, axis, [(i, i ^ distance) for i in range(devices)])


def spread_pieces(block, axis):
    whole = lax.all_gather(block, axis)
    return [whole[i] for i in range(lax.axis_size(axis))]


def spread_carries(blocks, axis):
    if len(blocks) == 1:
        return spread_pieces(blocks[0], axis)
    across = [swap(block, axis, d) for block, d in zip(blocks, SENT)]
    return across[:3] + [across[3]] + [swap(part, axis, 1) for part in across[:3]]


def from_behind(block, axis, distance):
    devices = range(lax.axis_size(axis))
    route = [(i - distance, i) for i in devices if i - distance in devices]
    return lax.ppermute(block, axis, route)


def shards(
    tokens,
    lengths,
    order,
    norm_gain,
    w_in,
    conv_weight,
    conv_bias,
    w_x,
    w_dt,
    dt_bias,
    a_log,
    d_skip,
    w_out,
    cotangent,
):
    rows, width = tokens.shape[1:]
    inner, rank, state, taps = w_out.shape[0], w_dt.shape[0], a_log.shape[1], conv_weight.shape[1]
    lags, clouds, steps = taps - 1, lengths.shape[1], rows // CHUNKS
    sizes = (rows, width, inner, rank, state, lags, clouds)
    devices = lax.axis_size("seq")
    me = lax.axis_index("seq").astype(jnp.int32)[None]
    here_x, here_dy = tokens[0], cotangent[0]
    cube = devices == len(CUBE) and lax.axis_size("dp") == 4
    (payload,) = call(
        payload_kernel,
        [((rows + ORDER_ROWS, width), BF16)],
        [(order.shape, order.dtype), pltpu.SemaphoreType.DMA((2,))],
        0,
        "tokens_and_order",
        4,
        far_ins=(0, 1),
    )(here_x, order)
    weights = (lengths, order, norm_gain, w_in, conv_weight.T, conv_bias, w_x.T, w_dt, dt_bias, a_log.T, d_skip)
    if cube:
        across_x = [payload] + [swap(payload, "seq", d) for d in CUBE[1:4]]
        send_dy = tie("dy", here_dy, {"d2": across_x[1], "d4": across_x[2], "d6": across_x[3]})
        across_dy = [send_dy] + [swap(send_dy, "seq", d) for d in CUBE[1:4]]
        pieces_x = across_x + [swap(part, "seq", 1) for part in across_x]
    else:
        pieces_x, pieces_dy = spread_pieces(payload, "seq"), spread_pieces(here_dy, "seq")
    n = len(pieces_x)
    big, lane = (rows, inner), (rows, LANES)
    carried = (inner // LANES, state * CHUNKS, LANES)
    spread = (rows, state * LANES)
    ext_rows = rows + lags * CHUNKS
    (trans, normed, gate, ext, conv, act, step, xproj, chunkf, sums, f, column, orders, valid, far, use, bbc, w_x_pad, w_dt_pad, a2, row_consts) = call(
        functools.partial(pre_kernel, sizes, n, len(weights)),
        [
            ((rows, width), BF16),
            ((rows, width), BF16),
            (big, F32),
            ((ext_rows, inner), F32),
            (big, F32),
            (big, BF16),
            (big, F32),
            (lane, F32),
            (carried, F32),
            ((CHUNKS, inner), F32),
            ((state, inner), F32),
            ((1 + cube, *lane), F32),
            ((4 if cube else n, rows), F32),
            ((lags, rows, LANES), F32),
            (big, F32),
            (big, F32),
            (spread, F32),
            ((LANES, inner), BF16),
            ((LANES, inner), BF16),
            ((state, inner), F32),
            ((lags + 2, inner), F32),
        ],
        [((rows + BLOCK, inner), F32), pltpu.SMEM(lengths.shape, jnp.int32)]
        + [(v.shape, v.dtype) for v in weights[1:]]
        + [pltpu.SemaphoreType.DMA((len(weights),))],
        1,
        "forward_local",
        24,
        9,
        far_ins=tuple(range(n + 1, n + 1 + len(weights))),
    )(me, *pieces_x, *weights)
    if cube:
        gather = lambda core: call(
            functools.partial(gather_kernel, core), [((rows, width), BF16)], [], 1, ("gather", "gather_other")[core], 8
        )
        (theirs,) = gather(1)(me, column, *across_dy)
        (mine,) = gather(0)(me, after(column, theirs), *across_dy)
        pieces_dy = [mine, swap(theirs, "seq", 1)]
    carry_rows = (state, 2 * state)[not cube]
    n_sent = (len(SENT), 1)[not cube]
    trans_dy, gg, gm, cbc, chunkb, near_out, *carries = call(
        functools.partial(back_kernel, sizes, len(pieces_dy)),
        [((rows, width), BF16), (big, F32), (big, F32), (spread, F32), (carried, F32), (w_out.shape, BF16)]
        + [((carry_rows, inner + LANES), F32)] * n_sent,
        [pltpu.SemaphoreType.DMA],
        1,
        "backward_local",
        20,
        7,
        far_ins=(len(pieces_dy) + 5,),
    )(me, *pieces_dy, gate, far, xproj, a2, w_out, sums, f, column)
    carries = spread_carries(carries, "seq")
    n_small = small_rows(sizes)
    held = ((n * (carry_rows + CHUNKS), inner), F32)
    kept = [pltpu.VMEM((state, rows + CHUNKS, LANES), F32)] * (inner // LANES)
    *states, gated, gz, keep, send = call(
        functools.partial(scan_forward_kernel, sizes, len(carries)),
        [*kept, (big, BF16), (big, BF16), ((width, inner), BF16), ((width, inner), BF16)],
        [(big, F32), (carried, F32), held],
        1,
        "scan_forward",
        18,
        7,
    )(me, *carries, trans_dy, normed, gg, gate, act, far, use, bbc, cbc, chunkf, sums, a2, row_consts)
    first = (keep, send)
    half_one, half_two = width, -(-(width + n_small) // (8 * BLOCK)) * (4 * BLOCK)
    got = swap(send, "seq", 1) if cube else None
    gstart, branch = call(
        functools.partial(branch_kernel, sizes, len(carries)),
        [(carried, F32), ((rows, width), BF16)],
        [held],
        1,
        "adjoint_carries_and_branch",
        8,
        1.5,
    )(me, *carries, chunkb, sums, a2, gated, near_out)
    if cube:
        part_one = half_one // 4
        beside_one = ((rows // 2 + part_one, inner), BF16)
        own_one, *sent = call(
            halves_beside_kernel, [((part_one, inner), BF16)] + [beside_one] * 3, [], 1, "add_halves_beside_rows", 8
        )(me, tie("adj", keep, {"gstart": gstart}), got, branch)
        away_one = [swap(block, "seq", d) for block, d in zip(sent, SENT)]
    gconv, rim, gpre, gxproj, galog = call(
        functools.partial(scan_backward_kernel, sizes),
        [(big, F32), ((CHUNKS, inner), F32), (big, BF16), (lane, BF16), ((state, inner), F32)],
        [(big, F32), (big, F32), (spread, F32), (spread, F32)],
        0,
        "scan_backward",
        20,
        14,
    )(*[pltpu.with_memory_space_constraint(part, pltpu.VMEM) for part in states], gstart, far, use, bbc, cbc, gm, step, act, conv, valid, a2, row_consts, w_x_pad, w_dt_pad)
    rim = from_behind(rim, "seq", -1)
    if cube:
        add_one = call(sum_kernel, [((part_one, inner), BF16)], [], 0, "add_parts", 4)
        if CFG["small"] != "mid":
            (one,) = add_one(tie("rim", after(own_one, gpre), {"rim": rim}), *away_one)
            gpre = tie("small", gpre, {"one": one})
    small, gci = call(
        functools.partial(small_kernel, sizes),
        [((n_small, inner), F32), (big, F32)],
        [],
        0,
        "small_grads",
        16,
        1.6,
    )(gpre, gxproj, xproj, act, gconv, ext, valid, gm, row_consts, galog)
    if cube and CFG["small"] == "mid":
        (one,) = add_one(after(own_one, small), *away_one)
        small = after(small, one)
    back, keep, send = call(
        functools.partial(final_kernel, sizes, devices),
        [((rows, width), BF16), ((half_two, inner), BF16), ((half_two, inner), BF16)],
        [((2 * half_two, inner), BF16)],
        1,
        "input_projection_grads",
        16,
    )(me, trans, normed, gci, gz, rim, small, norm_gain, w_in)
    cores = devices if cube else 0

    def first_results(own, other):
        return call(
            functools.partial(first_results_kernel, half_one, cores),
            [((inner, width), F32), ((width, 2 * inner), F32)],
            [((width, inner), F32), pltpu.SemaphoreType.DMA],
            1,
            "first_results",
            16,
            far_outs=(1,),
        )(me, own, other)

    if cube:
        part_two = half_two // 4
        piece_one, piece_two = ((part_one, inner), BF16), ((part_two, inner), BF16)
        pair_two = call(pair_kernel, [piece_two], [], 0, "add_pair", 4)
        rows_out = [((rows, width), BF16)]
        arrive = call(arrive_kernel, rows_out, [], 0, "add_arrived", 4)
        got = swap(send, "seq", 1)
        at = {"send": send}
        away_first = away_one

        def branch_rows(point, value):
            if CFG["share"] != point or CFG["p1d"] == "z":
                return value
            mine, theirs = call(
                functools.partial(share_kernel, rows, width),
                rows_out + [((rows // 2, inner), BF16)],
                [],
                1,
                "share_rows",
                8,
            )(me, orders, after(branch, at[point]), *away_one)
            at["out"] = arrive(here_x, mine, swap(theirs, "seq", 1))[0]
            return tie("hold", value, at)

        one = tie("z1", one, at)
        z_one = swap(one, "dp", 1)
        keep = tie("halves", keep, {"z": z_one})
        keep = branch_rows("send", keep)
        own_two, *sent = call(halves_kernel, [piece_two] * 4, [], 1, "add_halves", 4)(me, keep, got)
        away_two = [swap(block, "seq", d) for block, d in zip(sent, SENT)]
        at.update(d2=away_two[0], d4=away_two[1], d6=away_two[2], own=own_two)
        at["z1"] = z_one
        (one,) = call(pair_kernel, [piece_one], [], 0, "add_pair", 4)(tie("pair", one, at), z_one)
        z_one = swap(one, "dp", 2)
        at["zz"] = z_one
        own_two = tie("sumz", branch_rows("own", own_two), at)
        (two,) = call(sum_kernel, [piece_two], [], 0, "add_parts", 4)(own_two, *away_two)
        z_two = swap(two, "dp", 1)
        at["summed"], at["z"] = two, z_two
        two = tie("c1", branch_rows("summed", two), at)
        (two,) = pair_two(two, z_two)
        z_two = swap(two, "dp", 2)
        at["pair"] = two
        two = branch_rows("pair", two)
        if CFG["p1d"] == "z":
            back = tie("m3", back, at)
            away_back = [swap(back, "seq", d) for d in SENT[:3]]
            at.update(b2=away_back[0], b4=away_back[1], b6=away_back[2])
            mine_b, mine_g, theirs = call(
                functools.partial(share_both_kernel, rows, width),
                rows_out * 2 + [((rows, inner), BF16)],
                [],
                1,
                "share_rows",
                12,
            )(me, orders, tie("share", branch, at), *away_first, back, *away_back)
            output, input_grad = call(arrive_both_kernel, rows_out * 2, [], 0, "add_arrived", 8)(
                here_x, here_dy, mine_b, mine_g, swap(theirs, "seq", 1)
            )
            at.update(out=output, arrived=input_grad)
            two = tie("fin", two, at)
        (two,) = pair_two(two, z_two)
        at["total"] = two
        branch_rows("total", two)
        if CFG["p1d"] != "z":
            back = tie("m3", back, at)
        share = functools.partial(share_kernel, rows, width)
        if CFG["p1d"] == "m3":
            (one,) = call(pair_beside_kernel, [beside_one], [], 0, "add_pair_beside_rows", 8)(one, z_one, back)
            away_one = [swap(one, "seq", d) for d in SENT[:3]]
            two = tie("d", two, at)
            away_two = [swap(two, "seq", d) for d in SENT[:3]]
            at.update(d2=away_two[0], d4=away_two[1], d6=away_two[2])
            mine, theirs, own_one = call(
                share,
                rows_out + [((rows // 2 + half_one, inner), BF16), ((half_one, inner), BF16)],
                [],
                1,
                "share_rows_and_parts",
                12,
            )(me, orders, tie("share3", one, at), *away_one)
            theirs = swap(theirs, "seq", 1)
            f_wout, f_win = first_results(own_one, theirs)
            (input_grad,) = arrive(here_dy, mine, theirs)
            at.update(first=f_wout, arrived=input_grad)
            (own_two,) = call(chips_kernel, [((half_two, inner), BF16)], [], 1, "order_parts", 4)(
                me, tie("chips2", two, at), *away_two
            )
            other_two = swap(own_two, "seq", 1)
        else:
            if CFG["p1d"] != "z":
                away_back = [swap(back, "seq", d) for d in SENT[:3]]
                at.update(b2=away_back[0], b4=away_back[1], b6=away_back[2])
            (one,) = call(pair_kernel, [piece_one], [], 0, "add_pair", 4)(one, z_one)
            if CFG["p1d"] in "yz":
                away_one = [swap(tie("one", one, at), "seq", d) for d in SENT[:3]]
                at.update(o2=away_one[0], o4=away_one[1], o6=away_one[2])
                (own_one,) = call(chips_kernel, [((half_one, inner), BF16)], [], 1, "order_parts", 4)(
                    me, tie("chips1", one, at), *away_one
                )
                f_wout, f_win = first_results(own_one, swap(own_one, "seq", 1))
                at.update(first=f_wout)
                two = tie("d", two, at)
                away_two = [swap(two, "seq", d) for d in SENT[:3]]
                at.update(d2=away_two[0], d4=away_two[1], d6=away_two[2])
                (own_two,) = call(chips_kernel, [((half_two, inner), BF16)], [], 1, "order_parts", 4)(
                    me, tie("chips2", two, at), *away_two
                )
                other_two = swap(own_two, "seq", 1)
            else:
                two = tie("d", two, at)
                (both,) = call(stack_kernel, [((part_two + part_one, inner), BF16)], [], 0, "stack", 4)(two, one)
                away = [swap(both, "seq", d) for d in SENT[:3]]
                at.update(d2=away[0], d4=away[1], d6=away[2])
                (own_one,) = call(
                    functools.partial(both_chips_kernel, part_two, part_one),
                    [((half_two + half_one, inner), BF16)],
                    [],
                    1,
                    "order_parts",
                    8,
                )(me, both, *away)
                own_two, other_two = own_one, swap(own_one, "seq", 1)
                f_wout, f_win = first_results(own_two, other_two)
            if CFG["p1d"] != "z":
                mine, theirs = call(share, rows_out + [((rows // 2, inner), BF16)], [], 1, "share_rows", 8)(
                    me, orders, tie("share3", back, at), *away_back
                )
                (input_grad,) = arrive(tie("arrive", here_dy, at), mine, swap(theirs, "seq", 1))
        totals = (own_two, other_two)
        output = at["out"]
    else:
        totals = [lax.psum(half.astype(F32), ("dp", "seq")).astype(BF16) for half in (*first, keep, send)]
        f_wout, f_win = first_results(*totals[:2])
        totals = totals[2:]
        place = call(functools.partial(place_kernel, rows, n), [((rows, width), BF16)], [], 1, "to_hilbert", 24)
        (output,) = place(me, here_x, orders, *spread_pieces(branch, "seq"))
        (input_grad,) = place(me, here_dy, orders, *spread_pieces(back, "seq"))
    gain, f_win, taps_g, convb, wx, wdt, dtb, alog, skip = call(
        functools.partial(last_results_kernel, sizes, half_two, cores),
        [
            ((width,), F32),
            ((width, 2 * inner), F32),
            ((taps, inner), F32),
            ((inner,), F32),
            ((rank + 2 * state, inner), F32),
            ((rank, inner), F32),
            ((inner,), F32),
            ((state, inner), F32),
            ((inner,), F32),
        ],
        [((width, inner), F32), pltpu.SemaphoreType.DMA((width // LANES,))],
        1,
        "last_results",
        16,
        far_ins=(3,),
        far_outs=(1,),
        aliases={3: 1},
    )(me, *totals, f_win)
    return (output[None], input_grad[None], gain, f_win, taps_g.T, convb, wx.T, wdt, dtb, alog.T, skip, f_wout)


def solution(mesh):
    placed = (
        P("dp", "seq", None),
        P("dp", None),
        P("dp", "seq"),
        P(),
        P(),
        P(),
        P(),
        P(),
        P(),
        P(),
        P(),
        P(),
        P(),
        P("dp", "seq", None),
    )
    return jax.shard_map(
        shards,
        mesh=mesh,
        in_specs=placed,
        out_specs=(
            P("dp", "seq", None),
            P("dp", "seq", None),
            P(),
            P(),
            P(),
            P(),
            P(),
            P(),
            P(),
            P(),
            P(),
            P(),
        ),
        check_vma=False,
    )
```

```python
import functools

import jax
import jax.numpy as jnp
from jax import lax
from jax.experimental import pallas as pl
from jax.experimental.pallas import tpu as pltpu
from jax.sharding import PartitionSpec as P

EPSILON = 1e-05
LOG2E = 1.4426950408889634
FAR = 1e30
CHUNKS = 8
LANES = 128
BLOCK = 16
CUBE = (0, 2, 4, 6, 1, 3, 5, 7)
SENT = (2, 4, 6, 1)
ORDER_ROWS = 16
F32, BF16 = jnp.float32, jnp.bfloat16
MIB = 1024 * 1024


def dot(a, b, contract=((1,), (0,))):
    return lax.dot_general(a, b, (contract, ((), ())), preferred_element_type=F32)


def as_row(ref):
    return ref[...].reshape(1, ref.shape[0])


def wide(tile, width):
    return jnp.concatenate([tile] * (width // LANES), axis=1)


def sigmoid(v):
    return 1.0 / (1.0 + jnp.exp(-v))


def scalars(me, lengths, rows):
    begin, meta = jnp.int32(0), [me[0] * rows]
    for k in range(lengths.shape[1]):
        meta.append(begin)
        begin = begin + lengths[0, k]
    return meta


def source(me, p, n_pieces):
    return jnp.bitwise_xor(me[0], CUBE[p]) if n_pieces == len(CUBE) else jnp.int32(p)


def places(first, rows, r0, steps):
    r = r0 + lax.broadcasted_iota(jnp.int32, (rows, LANES), 0)
    return first + lax.rem(r, CHUNKS) * steps + lax.div(r, CHUNKS)


def cloud_start(meta, clouds, place):
    start = jnp.zeros_like(place)
    for k in range(clouds):
        begin = meta[1 + k]
        start = jnp.maximum(start, jnp.where(begin <= place, begin, 0))
    return start


def fill_valid(valid, meta, clouds, rows, lags):
    steps = rows // CHUNKS

    def body(j, carry):
        r0 = pl.multiple_of(j * BLOCK, BLOCK)
        place = places(meta[0], BLOCK, r0, steps)
        begin = cloud_start(meta, clouds, place)
        for k in range(1, lags + 1):
            valid[k - 1, pl.ds(r0, BLOCK), :] = (place - k >= begin).astype(F32)
        return carry

    lax.fori_loop(0, rows // BLOCK, body, 0)


def row_of_place(rows):
    place = lax.broadcasted_iota(jnp.int32, (rows, rows), 0)
    row = lax.broadcasted_iota(jnp.int32, (rows, rows), 1)
    return (place == lax.rem(row, CHUNKS) * (rows // CHUNKS) + lax.div(row, CHUNKS)).astype(F32).astype(BF16)


def gather_rows(column, pieces, me, rows):
    lane = lax.broadcasted_iota(jnp.int32, (column.shape[0], rows), 1).astype(F32)
    mine = [
        (column - (source(me, p, len(pieces)) * rows).astype(F32) == lane).astype(F32).astype(BF16)
        for p in range(len(pieces))
    ]
    return dot(jnp.concatenate(mine, axis=1), jnp.concatenate(pieces, axis=0))


def fill_broadcast(out, xproj, first, count):
    whole = xproj[...]
    high = whole.astype(BF16)
    low = (whole - high.astype(F32)).astype(BF16)
    row = lax.rem(lax.broadcasted_iota(jnp.int32, (2 * LANES, LANES), 0), LANES)
    for n in range(count):
        pick = (row == first + n).astype(F32).astype(BF16)
        out[:, n * LANES : (n + 1) * LANES] = dot(jnp.concatenate([high, low], axis=1), pick)


def rates(alog):
    return -jnp.exp(alog[...])


def chunk_of(ref, c, count):
    return jnp.concatenate([ref[b, pl.ds(c, count, stride=CHUNKS), :] for b in range(ref.shape[0])], axis=1)


def set_chunk(ref, c, value):
    for b in range(ref.shape[0]):
        ref[b, pl.ds(c, value.shape[0], stride=CHUNKS), :] = value[:, b * LANES : (b + 1) * LANES]


def payload_kernel(tokens, order, out, near, copied):
    rows, width = tokens.shape
    copies = [
        pltpu.make_async_copy(order, near, copied.at[0]),
        pltpu.make_async_copy(tokens, out.at[pl.ds(0, rows)], copied.at[1]),
    ]
    for copy in copies:
        copy.start()
    out[rows:, :] = jnp.zeros((ORDER_ROWS, width), BF16)
    copies[0].wait()
    out[rows:, 0:rows] = order_digits(near)
    copies[1].wait()


def order_column(to_row, digits):
    both = dot(to_row, digits, ((0,), (1,)))
    return jnp.broadcast_to(both[:, 0:1] * 128.0 + both[:, 1:2], (to_row.shape[0], LANES))


def order_digits(order):
    sub = lax.broadcasted_iota(jnp.int32, (ORDER_ROWS, order.shape[1]), 0)
    digits = jnp.where(sub == 0, order[...] >> 7, jnp.where(sub == 1, order[...] & 127, 0))
    return digits.astype(F32).astype(BF16)


def pre_kernel(sizes, n_pieces, n_far, me, *refs):
    rows, width, inner, rank, state, lags, clouds = sizes
    steps = rows // CHUNKS
    pieces = refs[:n_pieces]
    far_refs, refs = refs[n_pieces : n_pieces + n_far], refs[:n_pieces] + refs[n_pieces + n_far :]
    near_refs, copied, refs = refs[-n_far - 1 : -1], refs[-1], refs[: -n_far - 1]
    copies = [pltpu.make_async_copy(a, b, copied.at[k]) for k, (a, b) in enumerate(zip(far_refs, near_refs))]
    for copy in copies:
        copy.start()
    (lengths, order, gain, w_in, conv_w, conv_b, w_x, w_dt, dt_b, alog, skip) = near_refs
    copies[1].wait()
    (trans_o, normed_o, gate_o, ext_o, conv_o, act_o, step_o, xproj_o, chunkf_o, sums_o, f_o, column_o, orders_o,
     valid, far, use, bbc, wx_o, wdt_o, a2, rows_o, conv_in) = refs[n_pieces:]
    to_row = row_of_place(rows)
    sub = lax.broadcasted_iota(jnp.int32, (BLOCK, LANES), 0)
    extra = jnp.full((BLOCK, LANES), -1.0, F32)
    tail = jnp.zeros((ORDER_ROWS, rows), F32)
    for p in range(n_pieces):
        now = pieces[p][rows : rows + ORDER_ROWS, :rows]
        tail = jnp.where(source(me, p, n_pieces) == me[0] - 1, now.astype(F32), tail)
        if p < orders_o.shape[0]:
            row = dot(now, to_row)
            orders_o[p : p + 1, :] = row[0:1] * 128.0 + row[1:2]
    for k in range(1, lags + 1):
        extra = jnp.where(sub == k, tail[0:1, rows - k : rows - k + 1] * 128.0 + tail[1:2, rows - k : rows - k + 1], extra)
    own = order_column(to_row, order_digits(order))
    column_o[0] = own
    if n_pieces == len(CUBE):
        column_o[1] = order_column(to_row, pieces[CUBE.index(1)][rows : rows + ORDER_ROWS, :rows])
    column = jnp.concatenate([own, extra], axis=0)
    trans = gather_rows(wide(column, rows), [p[0:rows, :] for p in pieces], me, rows)
    trans_o[...] = trans[:rows].astype(BF16)
    for copy in copies[:1] + copies[2:]:
        copy.wait()
    meta = scalars(me, lengths, rows)
    bias, dt_bias = as_row(conv_b), as_row(dt_b)
    rows_o[0 : lags + 1, :] = conv_w[...]
    rows_o[lags + 1 : lags + 2, :] = as_row(skip)
    inv_rms = lax.rsqrt(jnp.mean(trans * trans, axis=1, keepdims=True) + EPSILON)
    normed = (trans * inv_rms * as_row(gain)).astype(BF16)
    normed_o[...] = normed[:rows]
    conv_in[...] = dot(normed, w_in[:, :inner]).astype(BF16).astype(F32)
    gate_o[...] = dot(normed[:rows], w_in[:, inner:])
    pad = lags * CHUNKS
    ext_o[pad : pad + rows, :] = conv_in[:rows, :]
    first_sub = lax.broadcasted_iota(jnp.int32, (CHUNKS, inner), 0) == 0
    for k in range(1, lags + 1):
        tile = conv_in[(steps - k) * CHUNKS : (steps - k + 1) * CHUNKS, :]
        before = conv_in[rows + k : rows + k + 1, :]
        ext_o[(lags - k) * CHUNKS : (lags - k + 1) * CHUNKS, :] = jnp.where(
            first_sub, before, pltpu.roll(tile, 1, 0)
        )
    for thin, full in ((w_x, wx_o), (w_dt, wdt_o)):
        blank = jnp.zeros((LANES - thin.shape[0], inner), F32)
        full[...] = jnp.concatenate([thin[...].astype(F32), blank], axis=0).astype(BF16)
    fill_valid(valid, meta, clouds, rows, lags)

    def conv_body(j, carry):
        r0 = pl.multiple_of(j * BLOCK, BLOCK)
        out = bias + conv_w[lags : lags + 1, :] * ext_o[pl.ds(r0 + pad, BLOCK), :]
        for k in range(1, lags + 1):
            ok = wide(valid[k - 1, pl.ds(r0, BLOCK), :], inner)
            shifted = ext_o[pl.ds(pl.multiple_of(r0 + pad - k * CHUNKS, CHUNKS), BLOCK), :]
            out = out + conv_w[lags - k : lags - k + 1, :] * shifted * ok
        conv_o[pl.ds(r0, BLOCK), :] = out
        act_o[pl.ds(r0, BLOCK), :] = (out * sigmoid(out)).astype(BF16)
        return carry

    lax.fori_loop(0, rows // BLOCK, conv_body, 0)
    xproj = dot(act_o[...], wx_o[...], ((1,), (1,)))
    xproj_o[...] = xproj
    step_o[...] = dot(xproj.astype(BF16), wdt_o[...])

    def step_body(j, carry):
        r0 = pl.multiple_of(j * BLOCK, BLOCK)
        pre = step_o[pl.ds(r0, BLOCK), :] + dt_bias
        step = jnp.maximum(pre, 0.0) + jnp.log1p(jnp.exp(-jnp.abs(pre)))
        step_o[pl.ds(r0, BLOCK), :] = step
        keep = wide(valid[0, pl.ds(r0, BLOCK), :], inner)
        distance = jnp.where(keep > 0.5, step, FAR)
        far[pl.ds(r0, BLOCK), :] = distance
        use[pl.ds(r0, BLOCK), :] = step * act_o[pl.ds(r0, BLOCK), :].astype(F32)
        return carry + distance[:CHUNKS] + distance[CHUNKS:]

    sums_o[...] = lax.fori_loop(0, rows // BLOCK, step_body, jnp.zeros((CHUNKS, inner), F32))
    fill_broadcast(bbc, xproj_o, rank, state)
    a2[...] = rates(alog) * LOG2E
    for lb in range(inner // LANES):
        ls = slice(lb * LANES, (lb + 1) * LANES)
        rate = [jnp.broadcast_to(a2[n : n + 1, ls], (CHUNKS, LANES)) for n in range(state)]

        def scan_body(i, states):
            r = pl.ds(pl.multiple_of(i * CHUNKS, CHUNKS), CHUNKS)
            distance, u = far[r, ls], use[r, ls]
            return tuple(
                jnp.exp2(distance * rate[n]) * states[n] + u * bbc[r, n * LANES : (n + 1) * LANES]
                for n in range(state)
            )

        zero = jnp.zeros((CHUNKS, LANES), F32)
        last = lax.fori_loop(0, steps, scan_body, (zero,) * state, unroll=8)
        for n in range(state):
            chunkf_o[lb, n * CHUNKS : (n + 1) * CHUNKS, :] = last[n]
    total = jnp.zeros((state, inner), F32)
    for c in range(CHUNKS):
        total = jnp.exp2(a2[...] * sums_o[c : c + 1, :]) * total + chunk_of(chunkf_o, c, state)
    f_o[...] = total


def gather_kernel(core, me, column, own, two, four, six, out):
    rows = own.shape[0]
    whole = jnp.concatenate([p[...] for p in (own, two, four, six)], axis=0)
    lane = lax.broadcasted_iota(jnp.int32, (rows, rows), 1).astype(F32)
    place = wide(column[core], rows)
    match = [(place - (source(me, p, len(CUBE)) * rows).astype(F32) == lane).astype(F32).astype(BF16) for p in range(4)]
    out[...] = dot(jnp.concatenate(match, axis=1), whole).astype(BF16)


def back_kernel(sizes, n_pieces, me, *refs):
    rows, width, inner, rank, state, lags, clouds = sizes
    steps = rows // CHUNKS
    pieces = refs[:n_pieces]
    gate, far, xproj, a2, w_out, sums, f, column, normed = refs[n_pieces : n_pieces + 9]
    n_out = len(SENT) if n_pieces == 2 else 1
    dy_o, gg_o, gm, cbc, chunkb_o, near_out, factor_o = refs[n_pieces + 9 : n_pieces + 16]
    carries_o = refs[n_pieces + 16 : n_pieces + 16 + n_out]
    (copied,) = refs[n_pieces + 16 + n_out :]
    copy = pltpu.make_async_copy(w_out, near_out, copied)
    copy.start()
    if n_pieces == 2:
        trans_dy = (pieces[0][...].astype(F32) + pieces[1][...].astype(F32)).astype(BF16)
    else:
        trans_dy = gather_rows(wide(column[0], rows), [p[...] for p in pieces], me, rows).astype(BF16)
    dy_o[...] = trans_dy
    factor_o[...] = jnp.where(jnp.bitwise_and(me[0], 1) == 1, trans_dy, normed[...])
    copy.wait()
    gg_o[...] = dot(trans_dy, near_out[...], ((1,), (1,)))

    def body(j, carry):
        r = pl.ds(pl.multiple_of(j * BLOCK, BLOCK), BLOCK)
        z = gate[r, :]
        gm[r, :] = gg_o[r, :] * (z * sigmoid(z))
        return carry

    lax.fori_loop(0, rows // BLOCK, body, 0)
    fill_broadcast(cbc, xproj, rank + state, state)
    for lb in range(inner // LANES):
        ls = slice(lb * LANES, (lb + 1) * LANES)
        rate = [jnp.broadcast_to(a2[n : n + 1, ls], (CHUNKS, LANES)) for n in range(state)]

        def scan_body(k, flows):
            r = pl.ds(pl.multiple_of((steps - 1 - k) * CHUNKS, CHUNKS), CHUNKS)
            distance, g = far[r, ls], gm[r, ls]
            return tuple(
                jnp.exp2(distance * rate[n]) * (flows[n] + g * cbc[r, n * LANES : (n + 1) * LANES])
                for n in range(state)
            )

        zero = jnp.zeros((CHUNKS, LANES), F32)
        last = lax.fori_loop(0, steps, scan_body, (zero,) * state, unroll=8)
        for n in range(state):
            chunkb_o[lb, n * CHUNKS : (n + 1) * CHUNKS, :] = last[n]
    total = jnp.zeros((state, inner), F32)
    for c in reversed(range(CHUNKS)):
        total = jnp.exp2(a2[...] * sums[c : c + 1, :]) * total + chunk_of(chunkb_o, c, state)
    passed = jnp.sum(sums[...], axis=0, keepdims=True)
    blocks = inner // LANES
    passed = jnp.concatenate([passed[:, b * LANES : (b + 1) * LANES] for b in range(blocks)], axis=0)
    passed = jnp.concatenate([passed, jnp.zeros((state - blocks, LANES), F32)], axis=0)
    if n_out == 1:
        carries_o[0][:state, :inner] = f[...]
        carries_o[0][state:, :inner] = total
        carries_o[0][:state, inner:] = passed
        carries_o[0][state:, inner:] = passed
        return
    for out, d in zip(carries_o, SENT):
        later = jnp.bitwise_xor(me[0], d) > me[0]
        out[:, :inner] = jnp.where(later, f[...], total)
        out[:, inner:] = passed


def core_of(me, devices):
    return jnp.bitwise_and(me, 1) if devices == len(CUBE) else jnp.int32(0)


def hold_carries(held, carries, me):
    n_pieces, count, inner = len(carries), carries[0].shape[0], held.shape[1]
    devices = len(CUBE) if n_pieces == len(CUBE) - 1 else n_pieces
    size = count + CHUNKS
    for p in range(n_pieces):
        whence = source(me, p + 1, devices) if devices > n_pieces else p
        base = whence * size
        held[pl.ds(pl.multiple_of(base, CHUNKS), count), :] = carries[p][:, :inner]
        passed = [carries[p][b : b + 1, inner:] for b in range(inner // LANES)]
        passed = jnp.broadcast_to(jnp.concatenate(passed, axis=1), (CHUNKS, inner))
        held[pl.ds(pl.multiple_of(base + count, CHUNKS), CHUNKS), :] = passed
    return devices, size


def scan_forward_kernel(sizes, n_pieces, me_ref, *refs):
    rows, width, inner, rank, state, lags, clouds = sizes
    steps = rows // CHUNKS
    carries = refs[:n_pieces]
    (gg, gate, act, far, use, bbc, cbc, chunkf, sums, a2, consts) = refs[n_pieces : n_pieces + 11]
    blocks = inner // LANES
    states = refs[n_pieces + 11 : n_pieces + 11 + blocks]
    (gated, gz_o, send_o) = refs[n_pieces + 11 + blocks : n_pieces + 14 + blocks]
    (mixed, sstart, held) = refs[n_pieces + 14 + blocks :]
    me = me_ref[0]
    skips = consts[lags + 1 : lags + 2, :]
    devices, size = hold_carries(held, carries, me_ref)

    def ahead(s, flow):
        base = pl.multiple_of(s * size, CHUNKS)
        p_s = jnp.exp2(a2[...] * held[pl.ds(base + size - CHUNKS, 1), :])
        return jnp.where(s < me, p_s * flow + held[pl.ds(base, state), :], flow)

    now = lax.fori_loop(0, devices, ahead, jnp.zeros((state, inner), F32))
    for c in range(CHUNKS):
        set_chunk(sstart, c, now)
        now = jnp.exp2(a2[...] * sums[c : c + 1, :]) * now + chunk_of(chunkf, c, state)

    for lb in range(inner // LANES):
        ls = slice(lb * LANES, (lb + 1) * LANES)
        rate = [jnp.broadcast_to(a2[n : n + 1, ls], (CHUNKS, LANES)) for n in range(state)]
        begin = []
        for n in range(state):
            tile = sstart[lb, n * CHUNKS : (n + 1) * CHUNKS, :]
            states[lb][n, 0:CHUNKS, :] = tile
            begin.append(tile)

        def forward(i, now):
            r0 = pl.multiple_of(i * CHUNKS, CHUNKS)
            r = pl.ds(r0, CHUNKS)
            nxt = pl.ds(pl.multiple_of(r0 + CHUNKS, CHUNKS), CHUNKS)
            distance, u = far[r, ls], use[r, ls]
            new, out = [], None
            for n in range(state):
                value = jnp.exp2(distance * rate[n]) * now[n] + u * bbc[r, n * LANES : (n + 1) * LANES]
                states[lb][n, nxt, :] = value
                part = value * cbc[r, n * LANES : (n + 1) * LANES]
                out = part if out is None else out + part
                new.append(value)
            mixed[r, ls] = out
            return tuple(new)

        lax.fori_loop(0, steps, forward, tuple(begin), unroll=8)

    second = jnp.bitwise_and(me, 1) == 1

    def gating(j, carry):
        r = pl.ds(pl.multiple_of(j * BLOCK, BLOCK), BLOCK)
        z, a = gate[r, :], act[r, :].astype(F32)
        s = sigmoid(z)
        m = mixed[r, :] + skips * a
        out = (m * (z * s)).astype(BF16)
        grad = (gg[r, :] * m * s * (1.0 + z * (1.0 - s))).astype(BF16)
        gated[r, :] = out
        gz_o[r, :] = grad
        send_o[r, :] = jnp.where(second, out, grad)
        return carry

    lax.fori_loop(0, rows // BLOCK, gating, 0)


def branch_kernel(sizes, n_pieces, me_ref, *refs):
    rows, width, inner, rank, state, lags, clouds = sizes
    carries = refs[:n_pieces]
    chunkb, sums, a2, gated, gz, trans_dy, normed, w_out, gstart, branch_o, part_o, held = refs[n_pieces:]
    me = me_ref[0]
    branch_o[...] = dot(gated[...], w_out[...]).astype(BF16)
    second = jnp.bitwise_and(me, 1) == 1
    factor = jnp.where(second, normed[...], trans_dy[...])
    part_o[...] = dot(factor, jnp.where(second, gz[...], gated[...]), ((0,), (0,)))
    devices, size = hold_carries(held, carries, me_ref)
    back = size - CHUNKS - state

    def behind(k, flow):
        s = devices - 1 - k
        base = pl.multiple_of(s * size, CHUNKS)
        p_s = jnp.exp2(a2[...] * held[pl.ds(base + size - CHUNKS, 1), :])
        return jnp.where(s > me, p_s * flow + held[pl.ds(pl.multiple_of(base + back, CHUNKS), state), :], flow)

    now = lax.fori_loop(0, devices, behind, jnp.zeros((state, inner), F32))
    for c in reversed(range(CHUNKS)):
        set_chunk(gstart, c, now)
        now = jnp.exp2(a2[...] * sums[c : c + 1, :]) * now + chunk_of(chunkb, c, state)


def scan_backward_kernel(sizes, *refs):
    rows, width, inner, rank, state, lags, clouds = sizes
    steps = rows // CHUNKS
    states, refs = refs[: inner // LANES], refs[inner // LANES :]
    (gstart, far, use, bbc, cbc, gm, step, act, conv, valid, a2, conv_w, w_x, w_dt) = refs[:14]
    (gconv, rim_o, gpre, gxproj_o, galog_o) = refs[14:19]
    (gs, lamb, gb, gc) = refs[19:]
    skips = conv_w[lags + 1 : lags + 2, :]
    group, pair = 3, 4
    for lg in range(inner // LANES // group):
        lanes = [slice((lg * group + k) * LANES, (lg * group + k + 1) * LANES) for k in range(group)]
        for ng in range(state // pair):
            ns = [ng * pair + k for k in range(pair)]
            rate = [[jnp.broadcast_to(a2[n : n + 1, ls], (CHUNKS, LANES)) for ls in lanes] for n in ns]
            begin = [gstart[lg * group + k, n * CHUNKS : (n + 1) * CHUNKS, :] for n in ns for k in range(group)]
            zero = jnp.zeros((CHUNKS, LANES), F32)

            def backward(k, carry):
                flows, sums_a = carry
                r0 = pl.multiple_of((steps - 1 - k) * CHUNKS, CHUNKS)
                r = pl.ds(r0, CHUNKS)
                nxt = pl.ds(pl.multiple_of(r0 + CHUNKS, CHUNKS), CHUNKS)
                gs_t = [None] * group
                lamb_t = [None] * group
                g_t = [gm[r, ls] for ls in lanes]
                u_t = [use[r, ls] for ls in lanes]
                d_t = [step[r, ls] for ls in lanes]
                f_t = [far[r, ls] for ls in lanes]
                new_flows, new_sums = [], []
                for q, n in enumerate(ns):
                    b = bbc[r, n * LANES : (n + 1) * LANES]
                    c = cbc[r, n * LANES : (n + 1) * LANES]
                    gb_t = gc_t = None
                    for x, ls in enumerate(lanes):
                        lam = g_t[x] * c + flows[q * group + x]
                        flow = jnp.exp2(f_t[x] * rate[q][x]) * lam
                        part = flow * states[lg * group + x][n, r, :]
                        one, two = part * rate[q][x], lam * b
                        gs_t[x] = one if gs_t[x] is None else gs_t[x] + one
                        lamb_t[x] = two if lamb_t[x] is None else lamb_t[x] + two
                        three, four = lam * u_t[x], g_t[x] * states[lg * group + x][n, nxt, :]
                        gb_t = three if gb_t is None else gb_t + three
                        gc_t = four if gc_t is None else gc_t + four
                        new_flows.append(flow)
                        new_sums.append(sums_a[q * group + x] + part * d_t[x])
                    nl = slice(n * LANES, (n + 1) * LANES)
                    if lg == 0:
                        gb[r, nl] = gb_t
                        gc[r, nl] = gc_t
                    else:
                        gb[r, nl] += gb_t
                        gc[r, nl] += gc_t
                for x, ls in enumerate(lanes):
                    if ng == 0:
                        gs[r, ls] = gs_t[x]
                        lamb[r, ls] = lamb_t[x]
                    else:
                        gs[r, ls] += gs_t[x]
                        lamb[r, ls] += lamb_t[x]
                return tuple(new_flows), tuple(new_sums)

            flows, sums_a = lax.fori_loop(
                0, steps, backward, (tuple(begin), (zero,) * (pair * group)), unroll=8
            )
            for q, n in enumerate(ns):
                for x, ls in enumerate(lanes):
                    galog_o[n : n + 1, ls] = (
                        jnp.sum(sums_a[q * group + x], axis=0, keepdims=True) * rate[q][x][0:1] * (1.0 / LOG2E)
                    )
    col = lax.broadcasted_iota(jnp.int32, (state * LANES, LANES), 1)
    row = lax.div(lax.broadcasted_iota(jnp.int32, (state * LANES, LANES), 0), LANES)
    pick_b = (col == row + rank).astype(F32).astype(BF16)
    pick_c = (col == row + rank + state).astype(F32).astype(BF16)

    def lane_sums(ref, pick):
        return dot(ref[...].astype(BF16), pick)

    grad_bc = lane_sums(gb, pick_b) + lane_sums(gc, pick_c)

    def pre_body(j, carry):
        r = pl.ds(pl.multiple_of(j * BLOCK, BLOCK), BLOCK)
        grad_step = gs[r, :] * (1.0 / LOG2E) + lamb[r, :] * act[r, :].astype(F32)
        gpre[r, :] = (grad_step * (1.0 - jnp.exp(-step[r, :]))).astype(BF16)
        return carry

    lax.fori_loop(0, rows // BLOCK, pre_body, 0)
    grad_xproj = (dot(gpre[...], w_dt[...], ((1,), (1,))) + grad_bc).astype(BF16)
    gxproj_o[...] = grad_xproj
    gs[...] = dot(grad_xproj, w_x[...])

    def conv_body(j, carry):
        r = pl.ds(pl.multiple_of(j * BLOCK, BLOCK), BLOCK)
        grad_act = gm[r, :] * skips + lamb[r, :] * step[r, :] + gs[r, :]
        v = conv[r, :]
        s = sigmoid(v)
        gconv[r, :] = grad_act * (s * (1.0 + v * (1.0 - s)))
        return carry

    lax.fori_loop(0, rows // BLOCK, conv_body, 0)
    rim_o[...] = jnp.zeros((CHUNKS, inner), F32)
    for b in range(1, lags + 1):
        total = jnp.zeros((1, inner), F32)
        for k in range(b, lags + 1):
            total = total + masked_tile(gconv, valid, conv_w, k - b, k, lags)[0:1]
        rim_o[b : b + 1, :] = total


def masked_tile(gconv, valid, conv_w, i, k, lags):
    r = pl.ds(pl.multiple_of(i * CHUNKS, CHUNKS), CHUNKS)
    tile = gconv[r, :] * conv_w[lags - k : lags - k + 1, :]
    return tile if k == 0 else tile * wide(valid[k - 1, r, :], tile.shape[1])


def small_kernel(sizes, gpre, gxproj, xproj, act, gconv, ext, valid, gm, conv_w, galog, small_o, gci_o):
    rows, width, inner, rank, state, lags, clouds = sizes
    steps = rows // CHUNKS

    def spread(i, carry):
        total = masked_tile(gconv, valid, conv_w, i, 0, lags)
        for k in range(1, lags + 1):
            total = total + masked_tile(gconv, valid, conv_w, i + k, k, lags)
        gci_o[pl.ds(pl.multiple_of(i * CHUNKS, CHUNKS), CHUNKS), :] = total
        return carry

    lax.fori_loop(0, steps - lags, spread, 0)
    sub = lax.broadcasted_iota(jnp.int32, (CHUNKS, inner), 0)
    for i in range(steps - lags, steps):
        total = masked_tile(gconv, valid, conv_w, i, 0, lags)
        for k in range(1, lags + 1):
            if i + k < steps:
                total = total + masked_tile(gconv, valid, conv_w, i + k, k, lags)
            else:
                moved = pltpu.roll(masked_tile(gconv, valid, conv_w, i + k - steps, k, lags), CHUNKS - 1, 0)
                total = total + jnp.where(sub == CHUNKS - 1, 0.0, moved)
        gci_o[i * CHUNKS : (i + 1) * CHUNKS, :] = total

    def sum_body(j, carry):
        r0 = pl.multiple_of(j * BLOCK, BLOCK)
        r = pl.ds(r0, BLOCK)
        grad = gconv[r, :]
        parts = [gm[r, :] * act[r, :].astype(F32), gpre[r, :].astype(F32), grad]
        for k in reversed(range(lags + 1)):
            masked = grad if k == 0 else grad * wide(valid[k - 1, r, :], inner)
            parts.append(masked * ext[pl.ds(pl.multiple_of(r0 + (lags - k) * CHUNKS, CHUNKS), BLOCK), :])
        return tuple(total + part[:CHUNKS] + part[CHUNKS:] for total, part in zip(carry, parts))

    sums = lax.fori_loop(0, rows // BLOCK, sum_body, (jnp.zeros((CHUNKS, inner), F32),) * (lags + 4))
    small_o[0:state, :] = galog[...]
    at = state
    small_o[at : at + rank + 2 * state, :] = dot(gxproj[...], act[...], ((0,), (0,)))[: rank + 2 * state]
    at += rank + 2 * state
    small_o[at : at + rank, :] = dot(xproj[...].astype(BF16), gpre[...], ((0,), (0,)))[:rank]
    at += rank
    for k, part in enumerate(sums):
        small_o[at + k : at + k + 1, :] = jnp.sum(part, axis=0, keepdims=True)
    at += len(sums)
    small_o[at:, :] = jnp.zeros((small_o.shape[0] - at, inner), F32)


def final_kernel(sizes, devices, me, trans, normed, gci, gz, rim, small, gain, w_in, back_o, keep_o, send_o, both):
    rows, width, inner, rank, state, lags, clouds = sizes
    steps = rows // CHUNKS
    r = lax.broadcasted_iota(jnp.int32, (rows, inner), 0)
    total = gci[...]
    for k in range(1, lags + 1):
        total = total + jnp.where(r == (steps - k) * CHUNKS + CHUNKS - 1, rim[k : k + 1, :], 0.0)
    grad_ci = total.astype(BF16)
    grad_z = gz[...]
    grad_normed = dot(grad_ci, w_in[:, :inner], ((1,), (1,))) + dot(grad_z, w_in[:, inner:], ((1,), (1,)))
    x = trans[...].astype(F32)
    inv_rms = lax.rsqrt(jnp.mean(x * x, axis=1, keepdims=True) + EPSILON)
    scaled = grad_normed * as_row(gain)
    back_o[...] = (
        inv_rms * scaled
        - inv_rms * inv_rms * inv_rms * x * jnp.mean(scaled * x, axis=1, keepdims=True)
    ).astype(BF16)
    both[0:width, :] = dot(normed[...], grad_ci, ((0,), (0,))).astype(BF16)
    gain_row = jnp.sum(grad_normed * x * inv_rms, axis=0, keepdims=True)
    gain_row = jnp.concatenate([gain_row, jnp.zeros((1, inner - width), F32)], axis=1)
    n_small = small.shape[0]
    last = lax.broadcasted_iota(jnp.int32, (n_small, inner), 0) == n_small - 1
    both[width : width + n_small, :] = jnp.where(last, gain_row, small[...]).astype(BF16)
    both[width + n_small :, :] = jnp.zeros((both.shape[0] - width - n_small, inner), BF16)
    half = keep_o.shape[0]
    core = core_of(me[0], devices)
    keep_o[...] = both[pl.ds(pl.multiple_of(core * half, BLOCK), half), :]
    send_o[...] = both[pl.ds(pl.multiple_of((1 - core) * half, BLOCK), half), :]


def small_rows(sizes):
    rows, width, inner, rank, state, lags, clouds = sizes
    return state + (rank + 2 * state) + rank + 3 + lags + 1 + 1


def halves_kernel(me, kept, got, own_o, *sent_o):
    part = own_o.shape[0]
    chip = lax.div(me[0], 2)
    for d, out in enumerate((own_o,) + sent_o):
        r = pl.ds(pl.multiple_of(jnp.bitwise_xor(chip, d) * part, BLOCK), part)
        out[...] = (kept[r, :].astype(F32) + got[r, :].astype(F32)).astype(BF16)


def beside(out, rows):
    half, width = rows.shape[0] // 2, rows.shape[1]
    out[0:half, 0:width] = rows[0:half, :]
    out[0:half, width:] = rows[half:, :]


def unfold(piece, rows, width):
    if piece.shape == (rows, width):
        return piece[...]
    half = rows // 2
    return jnp.concatenate([piece[0:half, 0:width], piece[0:half, width : 2 * width]], axis=0)


def first_halves_kernel(me, kept, factor, got, rows, own_o, *sent_o):
    whole, sent_o = sent_o[-1], sent_o[:-1]
    part = own_o.shape[0]
    half = rows.shape[0] // 2
    chip = lax.div(me[0], 2)
    whole[...] = kept[...] + dot(factor[...], got[...], ((0,), (0,)))
    for d, out in enumerate((own_o,) + sent_o):
        r = pl.ds(pl.multiple_of(jnp.bitwise_xor(chip, d) * part, BLOCK), part)
        total = whole[r, :].astype(BF16)
        if d == 0:
            out[...] = total
        else:
            beside(out, rows)
            out[half:, :] = total


def products_kernel(trans_dy, gated, normed, gz, wout_o, gate_o):
    wout_o[...] = dot(trans_dy[...], gated[...], ((0,), (0,)))
    gate_o[...] = dot(normed[...], gz[...], ((0,), (0,)))


def sum_kernel(a, b, c, d, out):
    one, two, three, four = (x[x.shape[0] - a.shape[0] :, :].astype(F32) for x in (a, b, c, d))
    out[...] = ((one + two) + (three + four)).astype(BF16)


def pair_kernel(a, b, out):
    out[...] = (a[...].astype(F32) + b[...].astype(F32)).astype(BF16)


def chips_kernel(me, own, two, four, six, out):
    part = own.shape[0]
    for d, piece in enumerate((own, two, four, six)):
        chip = jnp.bitwise_xor(lax.div(me[0], 2), d)
        out[pl.ds(pl.multiple_of(chip * part, BLOCK), part), :] = piece[...]


def share_kernel(rows, width, me, orders, own, two, four, six, mine_o, theirs_o):
    pieces = (own, two, four, six)
    whole = jnp.concatenate([unfold(p, rows, width) for p in pieces], axis=0)
    for core, out in enumerate((mine_o, theirs_o)):
        first = jnp.bitwise_xor(me[0], core) * rows
        place = (first + lax.broadcasted_iota(jnp.int32, (rows, rows), 0)).astype(F32)
        match = [(orders[p : p + 1, :] == place).astype(F32).astype(BF16) for p in range(len(pieces))]
        moved = dot(jnp.concatenate(match, axis=1), whole).astype(BF16)
        if core == 0:
            out[...] = moved
        else:
            out[:, 0:width] = moved[: rows // 2]
            out[:, width:] = moved[rows // 2 :]


def share_both_kernel(rows, width, me, orders, *refs):
    one, two, (mine_one, mine_two, theirs_o) = refs[0:4], refs[4:8], refs[8:]
    share_kernel(rows, width, me, orders, *one, mine_one, theirs_o.at[pl.ds(0, rows // 2)])
    share_kernel(rows, width, me, orders, *two, mine_two, theirs_o.at[pl.ds(rows // 2, rows // 2)])


def arrive_both_kernel(here_one, here_two, mine_one, mine_two, theirs, out_one, out_two):
    half = here_one.shape[0] // 2
    arrive_kernel(here_one, mine_one, theirs.at[pl.ds(0, half)], out_one)
    arrive_kernel(here_two, mine_two, theirs.at[pl.ds(half, half)], out_two)


def arrive_kernel(here, mine, theirs, out):
    rows, width = here.shape
    moved = mine[...].astype(F32) + unfold(theirs, rows, width).astype(F32)
    out[...] = (here[...].astype(F32) + moved).astype(BF16)


def halves_of(own, other, me, devices):
    second = core_of(me[0], devices) == 1
    return jnp.where(second, other, own), jnp.where(second, own, other)


def first_results_kernel(half, devices, me, own, other, wout_o, win_o, turned, copied):
    wout, gate = halves_of(own[own.shape[0] - half :, :], other[other.shape[0] - half :, :], me, devices)
    turned[...] = gate.astype(F32)
    inner = turned.shape[1]
    copy = pltpu.make_async_copy(turned, win_o.at[:, pl.ds(inner, inner)], copied)
    copy.start()
    wout_o[...] = wout.astype(F32).T
    copy.wait()


def last_results_kernel(sizes, half, devices, me, own, other, win, *refs):
    rows, width, inner, rank, state, lags, clouds = sizes
    (gain_o, win_o, taps_o, convb_o, wx_o, wdt_o, dtb_o, alog_o, skip_o, near, copied) = refs
    first, second = halves_of(own[0:half, :], other[0:half, :], me, devices)
    whole = jnp.concatenate([first, second], axis=0)
    copies = []
    for k in range(width // LANES):
        r = pl.ds(k * LANES, LANES)
        near[r, :] = whole[k * LANES : (k + 1) * LANES].astype(F32)
        copies.append(pltpu.make_async_copy(near.at[r], win_o.at[r, pl.ds(0, inner)], copied.at[k]))
        copies[-1].start()
    n_small = small_rows(sizes)
    small = whole[width : width + n_small].astype(F32)
    alog_o[...] = small[0:state]
    at = state
    wx_o[...] = small[at : at + rank + 2 * state]
    at += rank + 2 * state
    wdt_o[...] = small[at : at + rank]
    at += rank
    for k, out in enumerate((skip_o, dtb_o, convb_o)):
        out[...] = small[at + k : at + k + 1].reshape(inner)
    at += 3
    taps_o[...] = small[at : at + lags + 1]
    gain_o[...] = small[n_small - 1 : n_small, :width].reshape(width)
    for copy in copies:
        copy.wait()


def place_kernel(rows, n_pieces, me, here, orders, *refs):
    pieces, out = refs[:n_pieces], refs[n_pieces]
    place = (me[0] * rows + lax.broadcasted_iota(jnp.int32, (rows, rows), 0)).astype(F32)
    mine = [(orders[p : p + 1, :] == place).astype(F32).astype(BF16) for p in range(n_pieces)]
    moved = dot(jnp.concatenate(mine, axis=1), jnp.concatenate([p[...] for p in pieces], axis=0))
    out[...] = (here[...].astype(F32) + moved).astype(BF16)


def call(kernel, outs, scratch, n_smem, name, room, far_ins=(), far_outs=(), aliases={}):
    vmem = pl.BlockSpec(memory_space=pltpu.VMEM)
    smem = pl.BlockSpec(memory_space=pltpu.SMEM)
    anywhere = pl.BlockSpec(memory_space=pltpu.HBM)

    def run(*args):
        args = [pltpu.with_memory_space_constraint(v, pltpu.HBM) if k in far_ins else v for k, v in enumerate(args)]
        return pl.pallas_call(
            kernel,
            out_shape=[jax.ShapeDtypeStruct(*part) if isinstance(part, tuple) else part for part in outs],
            in_specs=[smem if k < n_smem else anywhere if k in far_ins else vmem for k in range(len(args))],
            out_specs=[anywhere if k in far_outs else vmem for k in range(len(outs))],
            input_output_aliases=aliases,
            scratch_shapes=[pltpu.VMEM(*part) if isinstance(part, tuple) else part for part in scratch],
            compiler_params=pltpu.CompilerParams(vmem_limit_bytes=room * MIB),
            cost_estimate=pl.CostEstimate(
                flops=1, bytes_accessed=1, transcendentals=0
            ),
            name=name,
        )(*args)

    return run


def after(value, *others):
    return lax.optimization_barrier((value, others))[0]


def swap(block, axis, distance):
    devices = lax.axis_size(axis)
    return lax.ppermute(block, axis, [(i, i ^ distance) for i in range(devices)])


def spread_pieces(block, axis):
    whole = lax.all_gather(block, axis)
    return [whole[i] for i in range(lax.axis_size(axis))]


def spread_carries(blocks, axis):
    if len(blocks) == 1:
        return spread_pieces(blocks[0], axis)
    across = [swap(block, axis, d) for block, d in zip(blocks, SENT)]
    return across[:3] + [across[3]] + [swap(part, axis, 1) for part in across[:3]]


def from_behind(block, axis, distance):
    devices = range(lax.axis_size(axis))
    route = [(i - distance, i) for i in devices if i - distance in devices]
    return lax.ppermute(block, axis, route)


def shards(
    tokens,
    lengths,
    order,
    norm_gain,
    w_in,
    conv_weight,
    conv_bias,
    w_x,
    w_dt,
    dt_bias,
    a_log,
    d_skip,
    w_out,
    cotangent,
):
    rows, width = tokens.shape[1:]
    inner, rank, state, taps = w_out.shape[0], w_dt.shape[0], a_log.shape[1], conv_weight.shape[1]
    lags, clouds, steps = taps - 1, lengths.shape[1], rows // CHUNKS
    sizes = (rows, width, inner, rank, state, lags, clouds)
    devices = lax.axis_size("seq")
    me = lax.axis_index("seq").astype(jnp.int32)[None]
    here_x, here_dy = tokens[0], cotangent[0]
    cube = devices == len(CUBE) and lax.axis_size("dp") == 4
    if devices == len(CUBE) and not cube:
        raise ValueError("unknown mesh")
    (payload,) = call(
        payload_kernel,
        [((rows + ORDER_ROWS, width), BF16)],
        [(order.shape, order.dtype), pltpu.SemaphoreType.DMA((2,))],
        0,
        "tokens_and_order",
        4,
        far_ins=(0, 1),
    )(here_x, order)
    weights = (lengths, order, norm_gain, w_in, conv_weight.T, conv_bias, w_x.T, w_dt, dt_bias, a_log.T, d_skip)
    if cube:
        across_x = [payload] + [swap(payload, "seq", d) for d in CUBE[1:4]]
        send_dy = after(here_dy, across_x[2])
        across_dy = [send_dy] + [swap(send_dy, "seq", d) for d in CUBE[1:4]]
        pieces_x = across_x + [swap(part, "seq", 1) for part in across_x]
    else:
        pieces_x, pieces_dy = spread_pieces(payload, "seq"), spread_pieces(here_dy, "seq")
    n = len(pieces_x)
    big, lane = (rows, inner), (rows, LANES)
    carried = (inner // LANES, state * CHUNKS, LANES)
    spread = (rows, state * LANES)
    ext_rows = rows + lags * CHUNKS
    (trans, normed, gate, ext, conv, act, step, xproj, chunkf, sums, f, column, orders, valid, far, use, bbc, w_x_pad, w_dt_pad, a2, row_consts) = call(
        functools.partial(pre_kernel, sizes, n, len(weights)),
        [
            ((rows, width), BF16),
            ((rows, width), BF16),
            (big, F32),
            ((ext_rows, inner), F32),
            (big, F32),
            (big, BF16),
            (big, F32),
            (lane, F32),
            (carried, F32),
            ((CHUNKS, inner), F32),
            ((state, inner), F32),
            ((1 + cube, *lane), F32),
            ((4 if cube else n, rows), F32),
            ((lags, rows, LANES), F32),
            (big, F32),
            (big, F32),
            (spread, F32),
            ((LANES, inner), BF16),
            ((LANES, inner), BF16),
            ((state, inner), F32),
            ((lags + 2, inner), F32),
        ],
        [((rows + BLOCK, inner), F32), pltpu.SMEM(lengths.shape, jnp.int32)]
        + [(v.shape, v.dtype) for v in weights[1:]]
        + [pltpu.SemaphoreType.DMA((len(weights),))],
        1,
        "forward_local",
        24,
        far_ins=tuple(range(n + 1, n + 1 + len(weights))),
    )(me, *pieces_x, *weights)
    if cube:
        gather = lambda core: call(
            functools.partial(gather_kernel, core), [((rows, width), BF16)], [], 1, ("gather", "gather_other")[core], 8
        )
        (theirs,) = gather(1)(me, column, *across_dy)
        (mine,) = gather(0)(me, after(column, theirs), *across_dy)
        pieces_dy = [mine, swap(theirs, "seq", 1)]
    carry_rows = (state, 2 * state)[not cube]
    n_sent = (len(SENT), 1)[not cube]
    trans_dy, gg, gm, cbc, chunkb, near_out, factor, *carries = call(
        functools.partial(back_kernel, sizes, len(pieces_dy)),
        [((rows, width), BF16), (big, F32), (big, F32), (spread, F32), (carried, F32), (w_out.shape, BF16), ((rows, width), BF16)]
        + [((carry_rows, inner + LANES), F32)] * n_sent,
        [pltpu.SemaphoreType.DMA],
        1,
        "backward_local",
        20,
        far_ins=(len(pieces_dy) + 5,),
    )(me, *pieces_dy, gate, far, xproj, a2, w_out, sums, f, column, normed)
    carries = spread_carries(carries, "seq")
    if cube:
        factor = swap(factor, "seq", 1)
        gate = after(gate, factor)
    n_small = small_rows(sizes)
    held = ((n * (carry_rows + CHUNKS), inner), F32)
    kept = [pltpu.VMEM((state, rows + CHUNKS, LANES), F32)] * (inner // LANES)
    *states, gated, gz, send = call(
        functools.partial(scan_forward_kernel, sizes, len(carries)),
        [*kept, (big, BF16), (big, BF16), (big, BF16)],
        [(big, F32), (carried, F32), held],
        1,
        "scan_forward",
        18,
    )(me, *carries, gg, gate, act, far, use, bbc, cbc, chunkf, sums, a2, row_consts)
    half_one, half_two = width, -(-(width + n_small) // (8 * BLOCK)) * (4 * BLOCK)
    if cube:
        got = swap(send, "seq", 1)
    gstart, branch, part = call(
        functools.partial(branch_kernel, sizes, len(carries)),
        [(carried, F32), ((rows, width), BF16), ((width, inner), F32)],
        [held],
        1,
        "adjoint_carries_and_branch",
        8,
    )(me, *carries, chunkb, sums, a2, gated, gz, trans_dy, normed, near_out)
    if cube:
        part_one = half_one // 4
        beside_one = ((rows // 2 + part_one, inner), BF16)
        own_one, *sent = call(
            first_halves_kernel,
            [((part_one, inner), BF16)] + [beside_one] * 3,
            [((width, inner), F32)],
            1,
            "first_halves",
            12,
        )(me, part, factor, got, branch)
        away_one = [swap(block, "seq", d) for block, d in zip(sent, SENT)]
    gconv, rim, gpre, gxproj, galog = call(
        functools.partial(scan_backward_kernel, sizes),
        [(big, F32), ((CHUNKS, inner), F32), (big, BF16), (lane, BF16), ((state, inner), F32)],
        [(big, F32), (big, F32), (spread, F32), (spread, F32)],
        0,
        "scan_backward",
        20,
    )(
        *[pltpu.with_memory_space_constraint(part, pltpu.VMEM) for part in states],
        gstart, far, use, bbc, cbc, gm, step, act, conv, valid, a2, row_consts, w_x_pad, w_dt_pad,
    )
    rim = from_behind(rim, "seq", -1)
    small, gci = call(
        functools.partial(small_kernel, sizes),
        [((n_small, inner), F32), (big, F32)],
        [],
        0,
        "small_grads",
        16,
    )(gpre, gxproj, xproj, act, gconv, ext, valid, gm, row_consts, galog)
    if cube:
        (one,) = call(sum_kernel, [((part_one, inner), BF16)], [], 0, "add_parts", 4)(
            after(own_one, small), *away_one
        )
        small = after(small, one)
    back, keep, send = call(
        functools.partial(final_kernel, sizes, devices),
        [((rows, width), BF16), ((half_two, inner), BF16), ((half_two, inner), BF16)],
        [((2 * half_two, inner), BF16)],
        1,
        "input_projection_grads",
        16,
    )(me, trans, normed, gci, gz, rim, small, norm_gain, w_in)
    cores = devices if cube else 0

    def first_results(own, other):
        return call(
            functools.partial(first_results_kernel, half_one, cores),
            [((inner, width), F32), ((width, 2 * inner), F32)],
            [((width, inner), F32), pltpu.SemaphoreType.DMA],
            1,
            "first_results",
            16,
            far_outs=(1,),
        )(me, own, other)

    if cube:
        part_two = half_two // 4
        piece_one, piece_two = ((part_one, inner), BF16), ((part_two, inner), BF16)
        pair_one, pair_two = [call(pair_kernel, [piece], [], 0, "add_pair", 4) for piece in (piece_one, piece_two)]
        got = swap(send, "seq", 1)
        one = after(one, send)
        z_one = swap(one, "dp", 1)
        own_two, *sent = call(halves_kernel, [piece_two] * 4, [], 1, "add_halves", 4)(me, keep, got)
        away_two = [swap(block, "seq", d) for block, d in zip(sent, SENT)]
        (one,) = pair_one(after(one, away_two[0]), z_one)
        z_here, z_one = z_one, swap(one, "dp", 2)
        (two,) = call(sum_kernel, [piece_two], [], 0, "add_parts", 4)(after(own_two, z_here), *away_two)
        (two,) = pair_two(two, swap(two, "dp", 1))
        z_two = swap(two, "dp", 2)
        back = after(back, own_two)
        away_back = [swap(back, "seq", d) for d in SENT[:3]]
        mine_b, mine_g, theirs = call(
            functools.partial(share_both_kernel, rows, width),
            [((rows, width), BF16)] * 2 + [((rows, inner), BF16)],
            [],
            1,
            "share_rows",
            12,
        )(me, orders, after(branch, two), *away_one, back, *away_back)
        output, input_grad = call(arrive_both_kernel, [((rows, width), BF16)] * 2, [], 0, "add_arrived", 8)(
            here_x, here_dy, mine_b, mine_g, swap(theirs, "seq", 1)
        )
        paired = two
        (two,) = pair_two(two, z_two)
        (one,) = pair_one(one, z_one)
        away_one = []
        for d in SENT[:3]:
            held_back = one
            for there in (*away_back, paired):
                held_back = after(held_back, there)
            away_one.append(swap(held_back, "seq", d))
        order_parts = lambda half: call(chips_kernel, [((half, inner), BF16)], [], 1, "order_parts", 4)
        (own_one,) = order_parts(half_one)(me, after(one, two), *away_one)
        f_wout, f_win = first_results(own_one, swap(own_one, "seq", 1))
        away_two = [swap(two, "seq", d) for d in SENT[:3]]
        (own_two,) = order_parts(half_two)(me, after(two, f_wout), *away_two)
        totals = (own_two, swap(own_two, "seq", 1))
    else:
        first = call(products_kernel, [((width, inner), F32)] * 2, [], 0, "products", 12)(trans_dy, gated, normed, gz)
        totals = [lax.psum(half.astype(F32), ("dp", "seq")).astype(BF16) for half in (*first, keep, send)]
        f_wout, f_win = first_results(*totals[:2])
        totals = totals[2:]
        place = call(functools.partial(place_kernel, rows, n), [((rows, width), BF16)], [], 1, "to_hilbert", 24)
        (output,) = place(me, here_x, orders, *spread_pieces(branch, "seq"))
        (input_grad,) = place(me, here_dy, orders, *spread_pieces(back, "seq"))
    gain, f_win, taps_g, convb, wx, wdt, dtb, alog, skip = call(
        functools.partial(last_results_kernel, sizes, half_two, cores),
        [
            ((width,), F32),
            ((width, 2 * inner), F32),
            ((taps, inner), F32),
            ((inner,), F32),
            ((rank + 2 * state, inner), F32),
            ((rank, inner), F32),
            ((inner,), F32),
            ((state, inner), F32),
            ((inner,), F32),
        ],
        [((width, inner), F32), pltpu.SemaphoreType.DMA((width // LANES,))],
        1,
        "last_results",
        16,
        far_ins=(3,),
        far_outs=(1,),
        aliases={3: 1},
    )(me, *totals, f_win)
    return (output[None], input_grad[None], gain, f_win, taps_g.T, convb, wx.T, wdt, dtb, alog.T, skip, f_wout)


def solution(mesh):
    placed = (
        P("dp", "seq", None),
        P("dp", None),
        P("dp", "seq"),
        P(),
        P(),
        P(),
        P(),
        P(),
        P(),
        P(),
        P(),
        P(),
        P(),
        P("dp", "seq", None),
    )
    return jax.shard_map(
        shards,
        mesh=mesh,
        in_specs=placed,
        out_specs=(
            P("dp", "seq", None),
            P("dp", "seq", None),
            P(),
            P(),
            P(),
            P(),
            P(),
            P(),
            P(),
            P(),
            P(),
            P(),
        ),
        check_vma=False,
    )
```

```python
import functools

import jax
import jax.numpy as jnp
from jax import lax
from jax.experimental import pallas as pl
from jax.experimental.pallas import tpu as pltpu
from jax.sharding import PartitionSpec as P

EPSILON = 1e-05
LOG2E = 1.4426950408889634
FAR = 1e30
CHUNKS = 8
LANES = 128
BLOCK = 16
CUBE = (0, 2, 4, 6, 1, 3, 5, 7)
SENT = (2, 4, 6, 1)
ORDER_ROWS = 16
F32, BF16 = jnp.float32, jnp.bfloat16
MIB = 1024 * 1024


def dot(a, b, contract=((1,), (0,))):
    return lax.dot_general(a, b, (contract, ((), ())), preferred_element_type=F32)


def as_row(ref):
    return ref[...].reshape(1, ref.shape[0])


def wide(tile, width):
    return jnp.concatenate([tile] * (width // LANES), axis=1)


def sigmoid(v):
    return 1.0 / (1.0 + jnp.exp(-v))


def scalars(me, lengths, rows):
    begin, meta = jnp.int32(0), [me[0] * rows]
    for k in range(lengths.shape[1]):
        meta.append(begin)
        begin = begin + lengths[0, k]
    return meta


def source(me, p, n_pieces):
    return jnp.bitwise_xor(me[0], CUBE[p]) if n_pieces == len(CUBE) else jnp.int32(p)


def places(first, rows, r0, steps):
    r = r0 + lax.broadcasted_iota(jnp.int32, (rows, LANES), 0)
    return first + lax.rem(r, CHUNKS) * steps + lax.div(r, CHUNKS)


def cloud_start(meta, clouds, place):
    start = jnp.zeros_like(place)
    for k in range(clouds):
        begin = meta[1 + k]
        start = jnp.maximum(start, jnp.where(begin <= place, begin, 0))
    return start


def fill_valid(valid, meta, clouds, rows, lags):
    steps = rows // CHUNKS

    def body(j, carry):
        r0 = pl.multiple_of(j * BLOCK, BLOCK)
        place = places(meta[0], BLOCK, r0, steps)
        begin = cloud_start(meta, clouds, place)
        for k in range(1, lags + 1):
            valid[k - 1, pl.ds(r0, BLOCK), :] = (place - k >= begin).astype(F32)
        return carry

    lax.fori_loop(0, rows // BLOCK, body, 0)


def row_of_place(rows):
    place = lax.broadcasted_iota(jnp.int32, (rows, rows), 0)
    row = lax.broadcasted_iota(jnp.int32, (rows, rows), 1)
    return (place == lax.rem(row, CHUNKS) * (rows // CHUNKS) + lax.div(row, CHUNKS)).astype(F32).astype(BF16)


def gather_rows(column, pieces, me, rows):
    lane = lax.broadcasted_iota(jnp.int32, (column.shape[0], rows), 1).astype(F32)
    mine = [
        (column - (source(me, p, len(pieces)) * rows).astype(F32) == lane).astype(F32).astype(BF16)
        for p in range(len(pieces))
    ]
    return dot(jnp.concatenate(mine, axis=1), jnp.concatenate(pieces, axis=0))


def fill_broadcast(out, xproj, first, count):
    whole = xproj[...]
    high = whole.astype(BF16)
    low = (whole - high.astype(F32)).astype(BF16)
    row = lax.rem(lax.broadcasted_iota(jnp.int32, (2 * LANES, LANES), 0), LANES)
    for n in range(count):
        pick = (row == first + n).astype(F32).astype(BF16)
        out[:, n * LANES : (n + 1) * LANES] = dot(jnp.concatenate([high, low], axis=1), pick)


def rates(alog):
    return -jnp.exp(alog[...])


def chunk_of(ref, c, count):
    return jnp.concatenate([ref[b, pl.ds(c, count, stride=CHUNKS), :] for b in range(ref.shape[0])], axis=1)


def set_chunk(ref, c, value):
    for b in range(ref.shape[0]):
        ref[b, pl.ds(c, value.shape[0], stride=CHUNKS), :] = value[:, b * LANES : (b + 1) * LANES]


def payload_kernel(tokens, order, out, near, copied):
    rows, width = tokens.shape
    copies = [
        pltpu.make_async_copy(order, near, copied.at[0]),
        pltpu.make_async_copy(tokens, out.at[pl.ds(0, rows)], copied.at[1]),
    ]
    for copy in copies:
        copy.start()
    out[rows:, :] = jnp.zeros((ORDER_ROWS, width), BF16)
    copies[0].wait()
    out[rows:, 0:rows] = order_digits(near)
    copies[1].wait()


def order_column(to_row, digits):
    both = dot(to_row, digits, ((0,), (1,)))
    return jnp.broadcast_to(both[:, 0:1] * 128.0 + both[:, 1:2], (to_row.shape[0], LANES))


def order_digits(order):
    sub = lax.broadcasted_iota(jnp.int32, (ORDER_ROWS, order.shape[1]), 0)
    digits = jnp.where(sub == 0, order[...] >> 7, jnp.where(sub == 1, order[...] & 127, 0))
    return digits.astype(F32).astype(BF16)


def pre_kernel(sizes, n_pieces, n_far, me, *refs):
    rows, width, inner, rank, state, lags, clouds = sizes
    steps = rows // CHUNKS
    pieces = refs[:n_pieces]
    far_refs, refs = refs[n_pieces : n_pieces + n_far], refs[:n_pieces] + refs[n_pieces + n_far :]
    near_refs, copied, refs = refs[-n_far - 1 : -1], refs[-1], refs[: -n_far - 1]
    copies = [pltpu.make_async_copy(a, b, copied.at[k]) for k, (a, b) in enumerate(zip(far_refs, near_refs))]
    for copy in copies:
        copy.start()
    (lengths, order, gain, w_in, conv_w, conv_b, w_x, w_dt, dt_b, alog, skip) = near_refs
    copies[1].wait()
    (trans_o, normed_o, gate_o, ext_o, conv_o, act_o, step_o, xproj_o, chunkf_o, sums_o, f_o, column_o, orders_o,
     valid, far, use, bbc, wx_o, wdt_o, a2, rows_o, conv_in) = refs[n_pieces:]
    to_row = row_of_place(rows)
    sub = lax.broadcasted_iota(jnp.int32, (BLOCK, LANES), 0)
    extra = jnp.full((BLOCK, LANES), -1.0, F32)
    tail = jnp.zeros((ORDER_ROWS, rows), F32)
    for p in range(n_pieces):
        now = pieces[p][rows : rows + ORDER_ROWS, :rows]
        tail = jnp.where(source(me, p, n_pieces) == me[0] - 1, now.astype(F32), tail)
        if p < orders_o.shape[0]:
            row = dot(now, to_row)
            orders_o[p : p + 1, :] = row[0:1] * 128.0 + row[1:2]
    for k in range(1, lags + 1):
        extra = jnp.where(sub == k, tail[0:1, rows - k : rows - k + 1] * 128.0 + tail[1:2, rows - k : rows - k + 1], extra)
    own = order_column(to_row, order_digits(order))
    column_o[0] = own
    if n_pieces == len(CUBE):
        column_o[1] = order_column(to_row, pieces[CUBE.index(1)][rows : rows + ORDER_ROWS, :rows])
    column = jnp.concatenate([own, extra], axis=0)
    trans = gather_rows(wide(column, rows), [p[0:rows, :] for p in pieces], me, rows)
    trans_o[...] = trans[:rows].astype(BF16)
    for copy in copies[:1] + copies[2:]:
        copy.wait()
    meta = scalars(me, lengths, rows)
    bias, dt_bias = as_row(conv_b), as_row(dt_b)
    rows_o[0 : lags + 1, :] = conv_w[...]
    rows_o[lags + 1 : lags + 2, :] = as_row(skip)
    inv_rms = lax.rsqrt(jnp.mean(trans * trans, axis=1, keepdims=True) + EPSILON)
    normed = (trans * inv_rms * as_row(gain)).astype(BF16)
    normed_o[...] = normed[:rows]
    conv_in[...] = dot(normed, w_in[:, :inner]).astype(BF16).astype(F32)
    gate_o[...] = dot(normed[:rows], w_in[:, inner:])
    pad = lags * CHUNKS
    ext_o[pad : pad + rows, :] = conv_in[:rows, :]
    first_sub = lax.broadcasted_iota(jnp.int32, (CHUNKS, inner), 0) == 0
    for k in range(1, lags + 1):
        tile = conv_in[(steps - k) * CHUNKS : (steps - k + 1) * CHUNKS, :]
        before = conv_in[rows + k : rows + k + 1, :]
        ext_o[(lags - k) * CHUNKS : (lags - k + 1) * CHUNKS, :] = jnp.where(
            first_sub, before, pltpu.roll(tile, 1, 0)
        )
    for thin, full in ((w_x, wx_o), (w_dt, wdt_o)):
        blank = jnp.zeros((LANES - thin.shape[0], inner), F32)
        full[...] = jnp.concatenate([thin[...].astype(F32), blank], axis=0).astype(BF16)
    fill_valid(valid, meta, clouds, rows, lags)

    def conv_body(j, carry):
        r0 = pl.multiple_of(j * BLOCK, BLOCK)
        out = bias + conv_w[lags : lags + 1, :] * ext_o[pl.ds(r0 + pad, BLOCK), :]
        for k in range(1, lags + 1):
            ok = wide(valid[k - 1, pl.ds(r0, BLOCK), :], inner)
            shifted = ext_o[pl.ds(pl.multiple_of(r0 + pad - k * CHUNKS, CHUNKS), BLOCK), :]
            out = out + conv_w[lags - k : lags - k + 1, :] * shifted * ok
        conv_o[pl.ds(r0, BLOCK), :] = out
        act_o[pl.ds(r0, BLOCK), :] = (out * sigmoid(out)).astype(BF16)
        return carry

    lax.fori_loop(0, rows // BLOCK, conv_body, 0)
    xproj = dot(act_o[...], wx_o[...], ((1,), (1,)))
    xproj_o[...] = xproj
    step_o[...] = dot(xproj.astype(BF16), wdt_o[...])

    def step_body(j, carry):
        r0 = pl.multiple_of(j * BLOCK, BLOCK)
        pre = step_o[pl.ds(r0, BLOCK), :] + dt_bias
        step = jnp.maximum(pre, 0.0) + jnp.log1p(jnp.exp(-jnp.abs(pre)))
        step_o[pl.ds(r0, BLOCK), :] = step
        keep = wide(valid[0, pl.ds(r0, BLOCK), :], inner)
        distance = jnp.where(keep > 0.5, step, FAR)
        far[pl.ds(r0, BLOCK), :] = distance
        use[pl.ds(r0, BLOCK), :] = step * act_o[pl.ds(r0, BLOCK), :].astype(F32)
        return carry + distance[:CHUNKS] + distance[CHUNKS:]

    sums_o[...] = lax.fori_loop(0, rows // BLOCK, step_body, jnp.zeros((CHUNKS, inner), F32))
    fill_broadcast(bbc, xproj_o, rank, state)
    a2[...] = rates(alog) * LOG2E
    for lb in range(inner // LANES):
        ls = slice(lb * LANES, (lb + 1) * LANES)
        rate = [jnp.broadcast_to(a2[n : n + 1, ls], (CHUNKS, LANES)) for n in range(state)]

        def scan_body(i, states):
            r = pl.ds(pl.multiple_of(i * CHUNKS, CHUNKS), CHUNKS)
            distance, u = far[r, ls], use[r, ls]
            return tuple(
                jnp.exp2(distance * rate[n]) * states[n] + u * bbc[r, n * LANES : (n + 1) * LANES]
                for n in range(state)
            )

        zero = jnp.zeros((CHUNKS, LANES), F32)
        last = lax.fori_loop(0, steps, scan_body, (zero,) * state, unroll=True)
        for n in range(state):
            chunkf_o[lb, n * CHUNKS : (n + 1) * CHUNKS, :] = last[n]
    total = jnp.zeros((state, inner), F32)
    for c in range(CHUNKS):
        total = jnp.exp2(a2[...] * sums_o[c : c + 1, :]) * total + chunk_of(chunkf_o, c, state)
    f_o[...] = total


def gather_kernel(core, me, column, own, two, four, six, out):
    rows = own.shape[0]
    whole = jnp.concatenate([p[...] for p in (own, two, four, six)], axis=0)
    lane = lax.broadcasted_iota(jnp.int32, (rows, rows), 1).astype(F32)
    place = wide(column[core], rows)
    match = [(place - (source(me, p, len(CUBE)) * rows).astype(F32) == lane).astype(F32).astype(BF16) for p in range(4)]
    out[...] = dot(jnp.concatenate(match, axis=1), whole).astype(BF16)


def back_kernel(sizes, n_pieces, me, *refs):
    rows, width, inner, rank, state, lags, clouds = sizes
    steps = rows // CHUNKS
    pieces = refs[:n_pieces]
    gate, far, xproj, a2, w_out, sums, f, column, normed = refs[n_pieces : n_pieces + 9]
    n_out = len(SENT) if n_pieces == 2 else 1
    dy_o, gg_o, gm, cbc, chunkb_o, near_out, factor_o = refs[n_pieces + 9 : n_pieces + 16]
    carries_o = refs[n_pieces + 16 : n_pieces + 16 + n_out]
    (copied,) = refs[n_pieces + 16 + n_out :]
    copy = pltpu.make_async_copy(w_out, near_out, copied)
    copy.start()
    if n_pieces == 2:
        trans_dy = (pieces[0][...].astype(F32) + pieces[1][...].astype(F32)).astype(BF16)
    else:
        trans_dy = gather_rows(wide(column[0], rows), [p[...] for p in pieces], me, rows).astype(BF16)
    dy_o[...] = trans_dy
    factor_o[...] = jnp.where(jnp.bitwise_and(me[0], 1) == 1, trans_dy, normed[...])
    copy.wait()
    gg_o[...] = dot(trans_dy, near_out[...], ((1,), (1,)))

    def body(j, carry):
        r = pl.ds(pl.multiple_of(j * BLOCK, BLOCK), BLOCK)
        z = gate[r, :]
        gm[r, :] = gg_o[r, :] * (z * sigmoid(z))
        return carry

    lax.fori_loop(0, rows // BLOCK, body, 0)
    fill_broadcast(cbc, xproj, rank + state, state)
    for lb in range(inner // LANES):
        ls = slice(lb * LANES, (lb + 1) * LANES)
        rate = [jnp.broadcast_to(a2[n : n + 1, ls], (CHUNKS, LANES)) for n in range(state)]

        def scan_body(k, flows):
            r = pl.ds(pl.multiple_of((steps - 1 - k) * CHUNKS, CHUNKS), CHUNKS)
            distance, g = far[r, ls], gm[r, ls]
            return tuple(
                jnp.exp2(distance * rate[n]) * (flows[n] + g * cbc[r, n * LANES : (n + 1) * LANES])
                for n in range(state)
            )

        zero = jnp.zeros((CHUNKS, LANES), F32)
        last = lax.fori_loop(0, steps, scan_body, (zero,) * state, unroll=True)
        for n in range(state):
            chunkb_o[lb, n * CHUNKS : (n + 1) * CHUNKS, :] = last[n]
    total = jnp.zeros((state, inner), F32)
    for c in reversed(range(CHUNKS)):
        total = jnp.exp2(a2[...] * sums[c : c + 1, :]) * total + chunk_of(chunkb_o, c, state)
    passed = jnp.sum(sums[...], axis=0, keepdims=True)
    blocks = inner // LANES
    passed = jnp.concatenate([passed[:, b * LANES : (b + 1) * LANES] for b in range(blocks)], axis=0)
    passed = jnp.concatenate([passed, jnp.zeros((state - blocks, LANES), F32)], axis=0)
    if n_out == 1:
        carries_o[0][:state, :inner] = f[...]
        carries_o[0][state:, :inner] = total
        carries_o[0][:state, inner:] = passed
        carries_o[0][state:, inner:] = passed
        return
    for out, d in zip(carries_o, SENT):
        later = jnp.bitwise_xor(me[0], d) > me[0]
        out[:, :inner] = jnp.where(later, f[...], total)
        out[:, inner:] = passed


def core_of(me, devices):
    return jnp.bitwise_and(me, 1) if devices == len(CUBE) else jnp.int32(0)


def hold_carries(held, carries, me):
    n_pieces, count, inner = len(carries), carries[0].shape[0], held.shape[1]
    devices = len(CUBE) if n_pieces == len(CUBE) - 1 else n_pieces
    size = count + CHUNKS
    for p in range(n_pieces):
        whence = source(me, p + 1, devices) if devices > n_pieces else p
        base = whence * size
        held[pl.ds(pl.multiple_of(base, CHUNKS), count), :] = carries[p][:, :inner]
        passed = [carries[p][b : b + 1, inner:] for b in range(inner // LANES)]
        passed = jnp.broadcast_to(jnp.concatenate(passed, axis=1), (CHUNKS, inner))
        held[pl.ds(pl.multiple_of(base + count, CHUNKS), CHUNKS), :] = passed
    return devices, size


def scan_forward_kernel(sizes, n_pieces, me_ref, *refs):
    rows, width, inner, rank, state, lags, clouds = sizes
    steps = rows // CHUNKS
    carries = refs[:n_pieces]
    (gg, gate, act, far, use, bbc, cbc, chunkf, sums, a2, consts) = refs[n_pieces : n_pieces + 11]
    blocks = inner // LANES
    states = refs[n_pieces + 11 : n_pieces + 11 + blocks]
    (gated, gz_o, send_o) = refs[n_pieces + 11 + blocks : n_pieces + 14 + blocks]
    (mixed, sstart, held) = refs[n_pieces + 14 + blocks :]
    me = me_ref[0]
    skips = consts[lags + 1 : lags + 2, :]
    devices, size = hold_carries(held, carries, me_ref)

    def ahead(s, flow):
        base = pl.multiple_of(s * size, CHUNKS)
        p_s = jnp.exp2(a2[...] * held[pl.ds(base + size - CHUNKS, 1), :])
        return jnp.where(s < me, p_s * flow + held[pl.ds(base, state), :], flow)

    now = lax.fori_loop(0, devices, ahead, jnp.zeros((state, inner), F32))
    for c in range(CHUNKS):
        set_chunk(sstart, c, now)
        now = jnp.exp2(a2[...] * sums[c : c + 1, :]) * now + chunk_of(chunkf, c, state)

    for lb in range(inner // LANES):
        ls = slice(lb * LANES, (lb + 1) * LANES)
        rate = [jnp.broadcast_to(a2[n : n + 1, ls], (CHUNKS, LANES)) for n in range(state)]
        begin = []
        for n in range(state):
            tile = sstart[lb, n * CHUNKS : (n + 1) * CHUNKS, :]
            states[lb][n, 0:CHUNKS, :] = tile
            begin.append(tile)

        def forward(i, now):
            r0 = pl.multiple_of(i * CHUNKS, CHUNKS)
            r = pl.ds(r0, CHUNKS)
            nxt = pl.ds(pl.multiple_of(r0 + CHUNKS, CHUNKS), CHUNKS)
            distance, u = far[r, ls], use[r, ls]
            new, out = [], None
            for n in range(state):
                value = jnp.exp2(distance * rate[n]) * now[n] + u * bbc[r, n * LANES : (n + 1) * LANES]
                states[lb][n, nxt, :] = value
                part = value * cbc[r, n * LANES : (n + 1) * LANES]
                out = part if out is None else out + part
                new.append(value)
            mixed[r, ls] = out
            return tuple(new)

        lax.fori_loop(0, steps, forward, tuple(begin), unroll=True)

    second = jnp.bitwise_and(me, 1) == 1

    def gating(j, carry):
        r = pl.ds(pl.multiple_of(j * BLOCK, BLOCK), BLOCK)
        z, a = gate[r, :], act[r, :].astype(F32)
        s = sigmoid(z)
        m = mixed[r, :] + skips * a
        out = (m * (z * s)).astype(BF16)
        grad = (gg[r, :] * m * s * (1.0 + z * (1.0 - s))).astype(BF16)
        gated[r, :] = out
        gz_o[r, :] = grad
        send_o[r, :] = jnp.where(second, out, grad)
        return carry

    lax.fori_loop(0, rows // BLOCK, gating, 0)


def branch_kernel(sizes, n_pieces, me_ref, *refs):
    rows, width, inner, rank, state, lags, clouds = sizes
    carries = refs[:n_pieces]
    chunkb, sums, a2, gated, gz, trans_dy, normed, w_out, gstart, branch_o, part_o, held = refs[n_pieces:]
    me = me_ref[0]
    branch_o[...] = dot(gated[...], w_out[...]).astype(BF16)
    second = jnp.bitwise_and(me, 1) == 1
    factor = jnp.where(second, normed[...], trans_dy[...])
    part_o[...] = dot(factor, jnp.where(second, gz[...], gated[...]), ((0,), (0,)))
    devices, size = hold_carries(held, carries, me_ref)
    back = size - CHUNKS - state

    def behind(k, flow):
        s = devices - 1 - k
        base = pl.multiple_of(s * size, CHUNKS)
        p_s = jnp.exp2(a2[...] * held[pl.ds(base + size - CHUNKS, 1), :])
        return jnp.where(s > me, p_s * flow + held[pl.ds(pl.multiple_of(base + back, CHUNKS), state), :], flow)

    now = lax.fori_loop(0, devices, behind, jnp.zeros((state, inner), F32))
    for c in reversed(range(CHUNKS)):
        set_chunk(gstart, c, now)
        now = jnp.exp2(a2[...] * sums[c : c + 1, :]) * now + chunk_of(chunkb, c, state)


def scan_backward_kernel(sizes, *refs):
    rows, width, inner, rank, state, lags, clouds = sizes
    steps = rows // CHUNKS
    states, refs = refs[: inner // LANES], refs[inner // LANES :]
    (gstart, far, use, bbc, cbc, gm, step, act, conv, valid, a2, conv_w, w_x, w_dt) = refs[:14]
    (gconv, rim_o, gpre, gxproj_o, galog_o) = refs[14:19]
    (gs, lamb, gb, gc) = refs[19:]
    skips = conv_w[lags + 1 : lags + 2, :]
    group, pair = 3, 4
    for lg in range(inner // LANES // group):
        lanes = [slice((lg * group + k) * LANES, (lg * group + k + 1) * LANES) for k in range(group)]
        for ng in range(state // pair):
            ns = [ng * pair + k for k in range(pair)]
            rate = [[jnp.broadcast_to(a2[n : n + 1, ls], (CHUNKS, LANES)) for ls in lanes] for n in ns]
            begin = [gstart[lg * group + k, n * CHUNKS : (n + 1) * CHUNKS, :] for n in ns for k in range(group)]
            zero = jnp.zeros((CHUNKS, LANES), F32)

            def backward(k, carry):
                flows, sums_a = carry
                r0 = pl.multiple_of((steps - 1 - k) * CHUNKS, CHUNKS)
                r = pl.ds(r0, CHUNKS)
                nxt = pl.ds(pl.multiple_of(r0 + CHUNKS, CHUNKS), CHUNKS)
                gs_t = [None] * group
                lamb_t = [None] * group
                g_t = [gm[r, ls] for ls in lanes]
                u_t = [use[r, ls] for ls in lanes]
                d_t = [step[r, ls] for ls in lanes]
                f_t = [far[r, ls] for ls in lanes]
                new_flows, new_sums = [], []
                for q, n in enumerate(ns):
                    b = bbc[r, n * LANES : (n + 1) * LANES]
                    c = cbc[r, n * LANES : (n + 1) * LANES]
                    gb_t = gc_t = None
                    for x, ls in enumerate(lanes):
                        lam = g_t[x] * c + flows[q * group + x]
                        flow = jnp.exp2(f_t[x] * rate[q][x]) * lam
                        part = flow * states[lg * group + x][n, r, :]
                        one, two = part * rate[q][x], lam * b
                        gs_t[x] = one if gs_t[x] is None else gs_t[x] + one
                        lamb_t[x] = two if lamb_t[x] is None else lamb_t[x] + two
                        three, four = lam * u_t[x], g_t[x] * states[lg * group + x][n, nxt, :]
                        gb_t = three if gb_t is None else gb_t + three
                        gc_t = four if gc_t is None else gc_t + four
                        new_flows.append(flow)
                        new_sums.append(sums_a[q * group + x] + part * d_t[x])
                    nl = slice(n * LANES, (n + 1) * LANES)
                    if lg == 0:
                        gb[r, nl] = gb_t
                        gc[r, nl] = gc_t
                    else:
                        gb[r, nl] += gb_t
                        gc[r, nl] += gc_t
                for x, ls in enumerate(lanes):
                    if ng == 0:
                        gs[r, ls] = gs_t[x]
                        lamb[r, ls] = lamb_t[x]
                    else:
                        gs[r, ls] += gs_t[x]
                        lamb[r, ls] += lamb_t[x]
                return tuple(new_flows), tuple(new_sums)

            flows, sums_a = lax.fori_loop(
                0, steps, backward, (tuple(begin), (zero,) * (pair * group)), unroll=True
            )
            for q, n in enumerate(ns):
                for x, ls in enumerate(lanes):
                    galog_o[n : n + 1, ls] = (
                        jnp.sum(sums_a[q * group + x], axis=0, keepdims=True) * rate[q][x][0:1] * (1.0 / LOG2E)
                    )
    col = lax.broadcasted_iota(jnp.int32, (state * LANES, LANES), 1)
    row = lax.div(lax.broadcasted_iota(jnp.int32, (state * LANES, LANES), 0), LANES)
    pick_b = (col == row + rank).astype(F32).astype(BF16)
    pick_c = (col == row + rank + state).astype(F32).astype(BF16)

    def lane_sums(ref, pick):
        return dot(ref[...].astype(BF16), pick)

    grad_bc = lane_sums(gb, pick_b) + lane_sums(gc, pick_c)

    def pre_body(j, carry):
        r = pl.ds(pl.multiple_of(j * BLOCK, BLOCK), BLOCK)
        grad_step = gs[r, :] * (1.0 / LOG2E) + lamb[r, :] * act[r, :].astype(F32)
        gpre[r, :] = (grad_step * (1.0 - jnp.exp(-step[r, :]))).astype(BF16)
        return carry

    lax.fori_loop(0, rows // BLOCK, pre_body, 0)
    grad_xproj = (dot(gpre[...], w_dt[...], ((1,), (1,))) + grad_bc).astype(BF16)
    gxproj_o[...] = grad_xproj
    gs[...] = dot(grad_xproj, w_x[...])

    def conv_body(j, carry):
        r = pl.ds(pl.multiple_of(j * BLOCK, BLOCK), BLOCK)
        grad_act = gm[r, :] * skips + lamb[r, :] * step[r, :] + gs[r, :]
        v = conv[r, :]
        s = sigmoid(v)
        gconv[r, :] = grad_act * (s * (1.0 + v * (1.0 - s)))
        return carry

    lax.fori_loop(0, rows // BLOCK, conv_body, 0)
    rim_o[...] = jnp.zeros((CHUNKS, inner), F32)
    for b in range(1, lags + 1):
        total = jnp.zeros((1, inner), F32)
        for k in range(b, lags + 1):
            total = total + masked_tile(gconv, valid, conv_w, k - b, k, lags)[0:1]
        rim_o[b : b + 1, :] = total


def masked_tile(gconv, valid, conv_w, i, k, lags):
    r = pl.ds(pl.multiple_of(i * CHUNKS, CHUNKS), CHUNKS)
    tile = gconv[r, :] * conv_w[lags - k : lags - k + 1, :]
    return tile if k == 0 else tile * wide(valid[k - 1, r, :], tile.shape[1])


def small_kernel(sizes, gpre, gxproj, xproj, act, gconv, ext, valid, gm, conv_w, galog, small_o, gci_o):
    rows, width, inner, rank, state, lags, clouds = sizes
    steps = rows // CHUNKS

    def spread(i, carry):
        total = masked_tile(gconv, valid, conv_w, i, 0, lags)
        for k in range(1, lags + 1):
            total = total + masked_tile(gconv, valid, conv_w, i + k, k, lags)
        gci_o[pl.ds(pl.multiple_of(i * CHUNKS, CHUNKS), CHUNKS), :] = total
        return carry

    lax.fori_loop(0, steps - lags, spread, 0)
    sub = lax.broadcasted_iota(jnp.int32, (CHUNKS, inner), 0)
    for i in range(steps - lags, steps):
        total = masked_tile(gconv, valid, conv_w, i, 0, lags)
        for k in range(1, lags + 1):
            if i + k < steps:
                total = total + masked_tile(gconv, valid, conv_w, i + k, k, lags)
            else:
                moved = pltpu.roll(masked_tile(gconv, valid, conv_w, i + k - steps, k, lags), CHUNKS - 1, 0)
                total = total + jnp.where(sub == CHUNKS - 1, 0.0, moved)
        gci_o[i * CHUNKS : (i + 1) * CHUNKS, :] = total

    def sum_body(j, carry):
        r0 = pl.multiple_of(j * BLOCK, BLOCK)
        r = pl.ds(r0, BLOCK)
        grad = gconv[r, :]
        parts = [gm[r, :] * act[r, :].astype(F32), gpre[r, :].astype(F32), grad]
        for k in reversed(range(lags + 1)):
            masked = grad if k == 0 else grad * wide(valid[k - 1, r, :], inner)
            parts.append(masked * ext[pl.ds(pl.multiple_of(r0 + (lags - k) * CHUNKS, CHUNKS), BLOCK), :])
        return tuple(total + part[:CHUNKS] + part[CHUNKS:] for total, part in zip(carry, parts))

    sums = lax.fori_loop(0, rows // BLOCK, sum_body, (jnp.zeros((CHUNKS, inner), F32),) * (lags + 4))
    small_o[0:state, :] = galog[...]
    at = state
    small_o[at : at + rank + 2 * state, :] = dot(gxproj[...], act[...], ((0,), (0,)))[: rank + 2 * state]
    at += rank + 2 * state
    small_o[at : at + rank, :] = dot(xproj[...].astype(BF16), gpre[...], ((0,), (0,)))[:rank]
    at += rank
    for k, part in enumerate(sums):
        small_o[at + k : at + k + 1, :] = jnp.sum(part, axis=0, keepdims=True)
    at += len(sums)
    small_o[at:, :] = jnp.zeros((small_o.shape[0] - at, inner), F32)


def final_kernel(sizes, devices, me, trans, normed, gci, gz, rim, small, gain, w_in, back_o, keep_o, send_o, both):
    rows, width, inner, rank, state, lags, clouds = sizes
    steps = rows // CHUNKS
    r = lax.broadcasted_iota(jnp.int32, (rows, inner), 0)
    total = gci[...]
    for k in range(1, lags + 1):
        total = total + jnp.where(r == (steps - k) * CHUNKS + CHUNKS - 1, rim[k : k + 1, :], 0.0)
    grad_ci = total.astype(BF16)
    grad_z = gz[...]
    grad_normed = dot(grad_ci, w_in[:, :inner], ((1,), (1,))) + dot(grad_z, w_in[:, inner:], ((1,), (1,)))
    x = trans[...].astype(F32)
    inv_rms = lax.rsqrt(jnp.mean(x * x, axis=1, keepdims=True) + EPSILON)
    scaled = grad_normed * as_row(gain)
    back_o[...] = (
        inv_rms * scaled
        - inv_rms * inv_rms * inv_rms * x * jnp.mean(scaled * x, axis=1, keepdims=True)
    ).astype(BF16)
    both[0:width, :] = dot(normed[...], grad_ci, ((0,), (0,))).astype(BF16)
    gain_row = jnp.sum(grad_normed * x * inv_rms, axis=0, keepdims=True)
    gain_row = jnp.concatenate([gain_row, jnp.zeros((1, inner - width), F32)], axis=1)
    n_small = small.shape[0]
    last = lax.broadcasted_iota(jnp.int32, (n_small, inner), 0) == n_small - 1
    both[width : width + n_small, :] = jnp.where(last, gain_row, small[...]).astype(BF16)
    both[width + n_small :, :] = jnp.zeros((both.shape[0] - width - n_small, inner), BF16)
    half = keep_o.shape[0]
    core = core_of(me[0], devices)
    keep_o[...] = both[pl.ds(pl.multiple_of(core * half, BLOCK), half), :]
    send_o[...] = both[pl.ds(pl.multiple_of((1 - core) * half, BLOCK), half), :]


def small_rows(sizes):
    rows, width, inner, rank, state, lags, clouds = sizes
    return state + (rank + 2 * state) + rank + 3 + lags + 1 + 1


def halves_kernel(me, kept, got, own_o, *sent_o):
    part = own_o.shape[0]
    chip = lax.div(me[0], 2)
    for d, out in enumerate((own_o,) + sent_o):
        r = pl.ds(pl.multiple_of(jnp.bitwise_xor(chip, d) * part, BLOCK), part)
        out[...] = (kept[r, :].astype(F32) + got[r, :].astype(F32)).astype(BF16)


def beside(out, rows):
    half, width = rows.shape[0] // 2, rows.shape[1]
    out[0:half, 0:width] = rows[0:half, :]
    out[0:half, width:] = rows[half:, :]


def unfold(piece, rows, width):
    if piece.shape == (rows, width):
        return piece[...]
    half = rows // 2
    return jnp.concatenate([piece[0:half, 0:width], piece[0:half, width : 2 * width]], axis=0)


def first_halves_kernel(me, kept, factor, got, rows, own_o, *sent_o):
    whole, sent_o = sent_o[-1], sent_o[:-1]
    part = own_o.shape[0]
    half = rows.shape[0] // 2
    chip = lax.div(me[0], 2)
    whole[...] = kept[...] + dot(factor[...], got[...], ((0,), (0,)))
    for d, out in enumerate((own_o,) + sent_o):
        r = pl.ds(pl.multiple_of(jnp.bitwise_xor(chip, d) * part, BLOCK), part)
        total = whole[r, :].astype(BF16)
        if d == 0:
            out[...] = total
        else:
            beside(out, rows)
            out[half:, :] = total


def products_kernel(trans_dy, gated, normed, gz, wout_o, gate_o):
    wout_o[...] = dot(trans_dy[...], gated[...], ((0,), (0,)))
    gate_o[...] = dot(normed[...], gz[...], ((0,), (0,)))


def sum_kernel(a, b, c, d, out):
    one, two, three, four = (x[x.shape[0] - a.shape[0] :, :].astype(F32) for x in (a, b, c, d))
    out[...] = ((one + two) + (three + four)).astype(BF16)


def pair_kernel(a, b, out):
    out[...] = (a[...].astype(F32) + b[...].astype(F32)).astype(BF16)


def chips_kernel(me, own, two, four, six, out):
    part = own.shape[0]
    for d, piece in enumerate((own, two, four, six)):
        chip = jnp.bitwise_xor(lax.div(me[0], 2), d)
        out[pl.ds(pl.multiple_of(chip * part, BLOCK), part), :] = piece[...]


def share_kernel(rows, width, me, orders, own, two, four, six, mine_o, theirs_o):
    pieces = (own, two, four, six)
    whole = jnp.concatenate([unfold(p, rows, width) for p in pieces], axis=0)
    for core, out in enumerate((mine_o, theirs_o)):
        first = jnp.bitwise_xor(me[0], core) * rows
        place = (first + lax.broadcasted_iota(jnp.int32, (rows, rows), 0)).astype(F32)
        match = [(orders[p : p + 1, :] == place).astype(F32).astype(BF16) for p in range(len(pieces))]
        moved = dot(jnp.concatenate(match, axis=1), whole).astype(BF16)
        if core == 0:
            out[...] = moved
        else:
            out[:, 0:width] = moved[: rows // 2]
            out[:, width:] = moved[rows // 2 :]


def share_both_kernel(rows, width, me, orders, *refs):
    one, two, (mine_one, mine_two, theirs_o) = refs[0:4], refs[4:8], refs[8:]
    share_kernel(rows, width, me, orders, *one, mine_one, theirs_o.at[pl.ds(0, rows // 2)])
    share_kernel(rows, width, me, orders, *two, mine_two, theirs_o.at[pl.ds(rows // 2, rows // 2)])


def arrive_both_kernel(here_one, here_two, mine_one, mine_two, theirs, out_one, out_two):
    half = here_one.shape[0] // 2
    arrive_kernel(here_one, mine_one, theirs.at[pl.ds(0, half)], out_one)
    arrive_kernel(here_two, mine_two, theirs.at[pl.ds(half, half)], out_two)


def arrive_kernel(here, mine, theirs, out):
    rows, width = here.shape
    moved = mine[...].astype(F32) + unfold(theirs, rows, width).astype(F32)
    out[...] = (here[...].astype(F32) + moved).astype(BF16)


def halves_of(own, other, me, devices):
    second = core_of(me[0], devices) == 1
    return jnp.where(second, other, own), jnp.where(second, own, other)


def first_results_kernel(half, devices, me, own, other, wout_o, win_o, turned, copied):
    wout, gate = halves_of(own[own.shape[0] - half :, :], other[other.shape[0] - half :, :], me, devices)
    turned[...] = gate.astype(F32)
    inner = turned.shape[1]
    copy = pltpu.make_async_copy(turned, win_o.at[:, pl.ds(inner, inner)], copied)
    copy.start()
    wout_o[...] = wout.astype(F32).T
    copy.wait()


def last_results_kernel(sizes, half, devices, me, own, other, win, *refs):
    rows, width, inner, rank, state, lags, clouds = sizes
    (gain_o, win_o, taps_o, convb_o, wx_o, wdt_o, dtb_o, alog_o, skip_o, near, copied) = refs
    first, second = halves_of(own[0:half, :], other[0:half, :], me, devices)
    whole = jnp.concatenate([first, second], axis=0)
    copies = []
    for k in range(width // LANES):
        r = pl.ds(k * LANES, LANES)
        near[r, :] = whole[k * LANES : (k + 1) * LANES].astype(F32)
        copies.append(pltpu.make_async_copy(near.at[r], win_o.at[r, pl.ds(0, inner)], copied.at[k]))
        copies[-1].start()
    n_small = small_rows(sizes)
    small = whole[width : width + n_small].astype(F32)
    alog_o[...] = small[0:state]
    at = state
    wx_o[...] = small[at : at + rank + 2 * state]
    at += rank + 2 * state
    wdt_o[...] = small[at : at + rank]
    at += rank
    for k, out in enumerate((skip_o, dtb_o, convb_o)):
        out[...] = small[at + k : at + k + 1].reshape(inner)
    at += 3
    taps_o[...] = small[at : at + lags + 1]
    gain_o[...] = small[n_small - 1 : n_small, :width].reshape(width)
    for copy in copies:
        copy.wait()


def place_kernel(rows, n_pieces, me, here, orders, *refs):
    pieces, out = refs[:n_pieces], refs[n_pieces]
    place = (me[0] * rows + lax.broadcasted_iota(jnp.int32, (rows, rows), 0)).astype(F32)
    mine = [(orders[p : p + 1, :] == place).astype(F32).astype(BF16) for p in range(n_pieces)]
    moved = dot(jnp.concatenate(mine, axis=1), jnp.concatenate([p[...] for p in pieces], axis=0))
    out[...] = (here[...].astype(F32) + moved).astype(BF16)


def call(kernel, outs, scratch, n_smem, name, room, far_ins=(), far_outs=(), aliases={}):
    vmem = pl.BlockSpec(memory_space=pltpu.VMEM)
    smem = pl.BlockSpec(memory_space=pltpu.SMEM)
    anywhere = pl.BlockSpec(memory_space=pltpu.HBM)

    def run(*args):
        args = [pltpu.with_memory_space_constraint(v, pltpu.HBM) if k in far_ins else v for k, v in enumerate(args)]
        return pl.pallas_call(
            kernel,
            out_shape=[jax.ShapeDtypeStruct(*part) if isinstance(part, tuple) else part for part in outs],
            in_specs=[smem if k < n_smem else anywhere if k in far_ins else vmem for k in range(len(args))],
            out_specs=[anywhere if k in far_outs else vmem for k in range(len(outs))],
            input_output_aliases=aliases,
            scratch_shapes=[pltpu.VMEM(*part) if isinstance(part, tuple) else part for part in scratch],
            compiler_params=pltpu.CompilerParams(vmem_limit_bytes=room * MIB),
            cost_estimate=pl.CostEstimate(
                flops=1, bytes_accessed=1, transcendentals=0
            ),
            name=name,
        )(*args)

    return run


def after(value, *others):
    return lax.optimization_barrier((value, others))[0]


def swap(block, axis, distance):
    devices = lax.axis_size(axis)
    return lax.ppermute(block, axis, [(i, i ^ distance) for i in range(devices)])


def spread_pieces(block, axis):
    whole = lax.all_gather(block, axis)
    return [whole[i] for i in range(lax.axis_size(axis))]


def spread_carries(blocks, axis):
    if len(blocks) == 1:
        return spread_pieces(blocks[0], axis)
    across = [swap(block, axis, d) for block, d in zip(blocks, SENT)]
    return across[:3] + [across[3]] + [swap(part, axis, 1) for part in across[:3]]


def from_behind(block, axis, distance):
    devices = range(lax.axis_size(axis))
    route = [(i - distance, i) for i in devices if i - distance in devices]
    return lax.ppermute(block, axis, route)


def shards(
    tokens,
    lengths,
    order,
    norm_gain,
    w_in,
    conv_weight,
    conv_bias,
    w_x,
    w_dt,
    dt_bias,
    a_log,
    d_skip,
    w_out,
    cotangent,
):
    rows, width = tokens.shape[1:]
    inner, rank, state, taps = w_out.shape[0], w_dt.shape[0], a_log.shape[1], conv_weight.shape[1]
    lags, clouds, steps = taps - 1, lengths.shape[1], rows // CHUNKS
    sizes = (rows, width, inner, rank, state, lags, clouds)
    devices = lax.axis_size("seq")
    me = lax.axis_index("seq").astype(jnp.int32)[None]
    here_x, here_dy = tokens[0], cotangent[0]
    cube = devices == len(CUBE) and lax.axis_size("dp") == 4
    if devices == len(CUBE) and not cube:
        raise ValueError("unknown mesh")
    (payload,) = call(
        payload_kernel,
        [((rows + ORDER_ROWS, width), BF16)],
        [(order.shape, order.dtype), pltpu.SemaphoreType.DMA((2,))],
        0,
        "tokens_and_order",
        4,
        far_ins=(0, 1),
    )(here_x, order)
    weights = (lengths, order, norm_gain, w_in, conv_weight.T, conv_bias, w_x.T, w_dt, dt_bias, a_log.T, d_skip)
    if cube:
        across_x = [payload] + [swap(payload, "seq", d) for d in CUBE[1:4]]
        send_dy = after(here_dy, across_x[2])
        across_dy = [send_dy] + [swap(send_dy, "seq", d) for d in CUBE[1:4]]
        pieces_x = across_x + [swap(part, "seq", 1) for part in across_x]
    else:
        pieces_x, pieces_dy = spread_pieces(payload, "seq"), spread_pieces(here_dy, "seq")
    n = len(pieces_x)
    big, lane = (rows, inner), (rows, LANES)
    carried = (inner // LANES, state * CHUNKS, LANES)
    spread = (rows, state * LANES)
    ext_rows = rows + lags * CHUNKS
    (trans, normed, gate, ext, conv, act, step, xproj, chunkf, sums, f, column, orders, valid, far, use, bbc, w_x_pad, w_dt_pad, a2, row_consts) = call(
        functools.partial(pre_kernel, sizes, n, len(weights)),
        [
            ((rows, width), BF16),
            ((rows, width), BF16),
            (big, F32),
            ((ext_rows, inner), F32),
            (big, F32),
            (big, BF16),
            (big, F32),
            (lane, F32),
            (carried, F32),
            ((CHUNKS, inner), F32),
            ((state, inner), F32),
            ((1 + cube, *lane), F32),
            ((4 if cube else n, rows), F32),
            ((lags, rows, LANES), F32),
            (big, F32),
            (big, F32),
            (spread, F32),
            ((LANES, inner), BF16),
            ((LANES, inner), BF16),
            ((state, inner), F32),
            ((lags + 2, inner), F32),
        ],
        [((rows + BLOCK, inner), F32), pltpu.SMEM(lengths.shape, jnp.int32)]
        + [(v.shape, v.dtype) for v in weights[1:]]
        + [pltpu.SemaphoreType.DMA((len(weights),))],
        1,
        "forward_local",
        24,
        far_ins=tuple(range(n + 1, n + 1 + len(weights))),
    )(me, *pieces_x, *weights)
    if cube:
        gather = lambda core: call(
            functools.partial(gather_kernel, core), [((rows, width), BF16)], [], 1, ("gather", "gather_other")[core], 8
        )
        (theirs,) = gather(1)(me, column, *across_dy)
        (mine,) = gather(0)(me, after(column, theirs), *across_dy)
        pieces_dy = [mine, swap(theirs, "seq", 1)]
    carry_rows = (state, 2 * state)[not cube]
    n_sent = (len(SENT), 1)[not cube]
    trans_dy, gg, gm, cbc, chunkb, near_out, factor, *carries = call(
        functools.partial(back_kernel, sizes, len(pieces_dy)),
        [((rows, width), BF16), (big, F32), (big, F32), (spread, F32), (carried, F32), (w_out.shape, BF16), ((rows, width), BF16)]
        + [((carry_rows, inner + LANES), F32)] * n_sent,
        [pltpu.SemaphoreType.DMA],
        1,
        "backward_local",
        20,
        far_ins=(len(pieces_dy) + 5,),
    )(me, *pieces_dy, gate, far, xproj, a2, w_out, sums, f, column, normed)
    carries = spread_carries(carries, "seq")
    if cube:
        factor = swap(factor, "seq", 1)
        gate = after(gate, factor)
    n_small = small_rows(sizes)
    held = ((n * (carry_rows + CHUNKS), inner), F32)
    kept = [pltpu.VMEM((state, rows + CHUNKS, LANES), F32)] * (inner // LANES)
    *states, gated, gz, send = call(
        functools.partial(scan_forward_kernel, sizes, len(carries)),
        [*kept, (big, BF16), (big, BF16), (big, BF16)],
        [(big, F32), (carried, F32), held],
        1,
        "scan_forward",
        18,
    )(me, *carries, gg, gate, act, far, use, bbc, cbc, chunkf, sums, a2, row_consts)
    half_one, half_two = width, -(-(width + n_small) // (8 * BLOCK)) * (4 * BLOCK)
    if cube:
        got = swap(send, "seq", 1)
    gstart, branch, part = call(
        functools.partial(branch_kernel, sizes, len(carries)),
        [(carried, F32), ((rows, width), BF16), ((width, inner), F32)],
        [held],
        1,
        "adjoint_carries_and_branch",
        8,
    )(me, *carries, chunkb, sums, a2, gated, gz, trans_dy, normed, near_out)
    if cube:
        part_one = half_one // 4
        beside_one = ((rows // 2 + part_one, inner), BF16)
        own_one, *sent = call(
            first_halves_kernel,
            [((part_one, inner), BF16)] + [beside_one] * 3,
            [((width, inner), F32)],
            1,
            "first_halves",
            12,
        )(me, part, factor, got, branch)
        away_one = [swap(block, "seq", d) for block, d in zip(sent, SENT)]
    gconv, rim, gpre, gxproj, galog = call(
        functools.partial(scan_backward_kernel, sizes),
        [(big, F32), ((CHUNKS, inner), F32), (big, BF16), (lane, BF16), ((state, inner), F32)],
        [(big, F32), (big, F32), (spread, F32), (spread, F32)],
        0,
        "scan_backward",
        20,
    )(
        *[pltpu.with_memory_space_constraint(part, pltpu.VMEM) for part in states],
        gstart, far, use, bbc, cbc, gm, step, act, conv, valid, a2, row_consts, w_x_pad, w_dt_pad,
    )
    rim = from_behind(rim, "seq", -1)
    small, gci = call(
        functools.partial(small_kernel, sizes),
        [((n_small, inner), F32), (big, F32)],
        [],
        0,
        "small_grads",
        16,
    )(gpre, gxproj, xproj, act, gconv, ext, valid, gm, row_consts, galog)
    if cube:
        (one,) = call(sum_kernel, [((part_one, inner), BF16)], [], 0, "add_parts", 4)(
            after(own_one, small), *away_one
        )
        small = after(small, one)
    back, keep, send = call(
        functools.partial(final_kernel, sizes, devices),
        [((rows, width), BF16), ((half_two, inner), BF16), ((half_two, inner), BF16)],
        [((2 * half_two, inner), BF16)],
        1,
        "input_projection_grads",
        16,
    )(me, trans, normed, gci, gz, rim, small, norm_gain, w_in)
    cores = devices if cube else 0

    def first_results(own, other):
        return call(
            functools.partial(first_results_kernel, half_one, cores),
            [((inner, width), F32), ((width, 2 * inner), F32)],
            [((width, inner), F32), pltpu.SemaphoreType.DMA],
            1,
            "first_results",
            16,
            far_outs=(1,),
        )(me, own, other)

    if cube:
        part_two = half_two // 4
        piece_one, piece_two = ((part_one, inner), BF16), ((part_two, inner), BF16)
        pair_one, pair_two = [call(pair_kernel, [piece], [], 0, "add_pair", 4) for piece in (piece_one, piece_two)]
        got = swap(send, "seq", 1)
        one = after(one, send)
        z_one = swap(one, "dp", 1)
        own_two, *sent = call(halves_kernel, [piece_two] * 4, [], 1, "add_halves", 4)(me, keep, got)
        away_two = [swap(block, "seq", d) for block, d in zip(sent, SENT)]
        (one,) = pair_one(after(one, away_two[0]), z_one)
        z_here, z_one = z_one, swap(one, "dp", 2)
        (two,) = call(sum_kernel, [piece_two], [], 0, "add_parts", 4)(after(own_two, z_here), *away_two)
        (two,) = pair_two(two, swap(two, "dp", 1))
        z_two = swap(two, "dp", 2)
        back = after(back, own_two)
        away_back = [swap(back, "seq", d) for d in SENT[:3]]
        mine_b, mine_g, theirs = call(
            functools.partial(share_both_kernel, rows, width),
            [((rows, width), BF16)] * 2 + [((rows, inner), BF16)],
            [],
            1,
            "share_rows",
            12,
        )(me, orders, after(branch, two), *away_one, back, *away_back)
        output, input_grad = call(arrive_both_kernel, [((rows, width), BF16)] * 2, [], 0, "add_arrived", 8)(
            here_x, here_dy, mine_b, mine_g, swap(theirs, "seq", 1)
        )
        paired = two
        (two,) = pair_two(two, z_two)
        (one,) = pair_one(one, z_one)
        away_one = []
        for d in SENT[:3]:
            held_back = one
            for there in (*away_back, paired):
                held_back = after(held_back, there)
            away_one.append(swap(held_back, "seq", d))
        order_parts = lambda half: call(chips_kernel, [((half, inner), BF16)], [], 1, "order_parts", 4)
        (own_one,) = order_parts(half_one)(me, after(one, two), *away_one)
        f_wout, f_win = first_results(own_one, swap(own_one, "seq", 1))
        away_two = [swap(two, "seq", d) for d in SENT[:3]]
        (own_two,) = order_parts(half_two)(me, after(two, f_wout), *away_two)
        totals = (own_two, swap(own_two, "seq", 1))
    else:
        first = call(products_kernel, [((width, inner), F32)] * 2, [], 0, "products", 12)(trans_dy, gated, normed, gz)
        totals = [lax.psum(half.astype(F32), ("dp", "seq")).astype(BF16) for half in (*first, keep, send)]
        f_wout, f_win = first_results(*totals[:2])
        totals = totals[2:]
        place = call(functools.partial(place_kernel, rows, n), [((rows, width), BF16)], [], 1, "to_hilbert", 24)
        (output,) = place(me, here_x, orders, *spread_pieces(branch, "seq"))
        (input_grad,) = place(me, here_dy, orders, *spread_pieces(back, "seq"))
    gain, f_win, taps_g, convb, wx, wdt, dtb, alog, skip = call(
        functools.partial(last_results_kernel, sizes, half_two, cores),
        [
            ((width,), F32),
            ((width, 2 * inner), F32),
            ((taps, inner), F32),
            ((inner,), F32),
            ((rank + 2 * state, inner), F32),
            ((rank, inner), F32),
            ((inner,), F32),
            ((state, inner), F32),
            ((inner,), F32),
        ],
        [((width, inner), F32), pltpu.SemaphoreType.DMA((width // LANES,))],
        1,
        "last_results",
        16,
        far_ins=(3,),
        far_outs=(1,),
        aliases={3: 1},
    )(me, *totals, f_win)
    return (output[None], input_grad[None], gain, f_win, taps_g.T, convb, wx.T, wdt, dtb, alog.T, skip, f_wout)


def solution(mesh):
    placed = (
        P("dp", "seq", None),
        P("dp", None),
        P("dp", "seq"),
        P(),
        P(),
        P(),
        P(),
        P(),
        P(),
        P(),
        P(),
        P(),
        P(),
        P("dp", "seq", None),
    )
    return jax.shard_map(
        shards,
        mesh=mesh,
        in_specs=placed,
        out_specs=(
            P("dp", "seq", None),
            P("dp", "seq", None),
            P(),
            P(),
            P(),
            P(),
            P(),
            P(),
            P(),
            P(),
            P(),
            P(),
        ),
        check_vma=False,
    )
```

```python
import functools

import jax
import jax.numpy as jnp
from jax import lax
from jax.experimental import pallas as pl
from jax.experimental.pallas import tpu as pltpu
from jax.sharding import PartitionSpec as P

EPSILON = 1e-05
LOG2E = 1.4426950408889634
FAR = 1e30
CHUNKS = 8
LANES = 128
BLOCK = 16
CUBE = (0, 2, 4, 6, 1, 3, 5, 7)
SENT = (2, 4, 6, 1)
ORDER_ROWS = 16
F32, BF16 = jnp.float32, jnp.bfloat16
MIB = 1024 * 1024


def dot(a, b, contract=((1,), (0,))):
    return lax.dot_general(a, b, (contract, ((), ())), preferred_element_type=F32)


def as_row(ref):
    return ref[...].reshape(1, ref.shape[0])


def wide(tile, width):
    return jnp.concatenate([tile] * (width // LANES), axis=1)


def sigmoid(v):
    return 1.0 / (1.0 + jnp.exp(-v))


def scalars(me, lengths, rows):
    begin, meta = jnp.int32(0), [me[0] * rows]
    for k in range(lengths.shape[1]):
        meta.append(begin)
        begin = begin + lengths[0, k]
    return meta


def source(me, p, n_pieces):
    return jnp.bitwise_xor(me[0], CUBE[p]) if n_pieces == len(CUBE) else jnp.int32(p)


def places(first, rows, r0, steps):
    r = r0 + lax.broadcasted_iota(jnp.int32, (rows, LANES), 0)
    return first + lax.rem(r, CHUNKS) * steps + lax.div(r, CHUNKS)


def cloud_start(meta, clouds, place):
    start = jnp.zeros_like(place)
    for k in range(clouds):
        begin = meta[1 + k]
        start = jnp.maximum(start, jnp.where(begin <= place, begin, 0))
    return start


def fill_valid(valid, meta, clouds, rows, lags):
    steps = rows // CHUNKS

    def body(j, carry):
        r0 = pl.multiple_of(j * BLOCK, BLOCK)
        place = places(meta[0], BLOCK, r0, steps)
        begin = cloud_start(meta, clouds, place)
        for k in range(1, lags + 1):
            valid[k - 1, pl.ds(r0, BLOCK), :] = (place - k >= begin).astype(F32)
        return carry

    lax.fori_loop(0, rows // BLOCK, body, 0)


def row_of_place(rows):
    place = lax.broadcasted_iota(jnp.int32, (rows, rows), 0)
    row = lax.broadcasted_iota(jnp.int32, (rows, rows), 1)
    return (place == lax.rem(row, CHUNKS) * (rows // CHUNKS) + lax.div(row, CHUNKS)).astype(F32).astype(BF16)


def gather_rows(column, pieces, me, rows):
    lane = lax.broadcasted_iota(jnp.int32, (column.shape[0], rows), 1).astype(F32)
    mine = [
        (column - (source(me, p, len(pieces)) * rows).astype(F32) == lane).astype(F32).astype(BF16)
        for p in range(len(pieces))
    ]
    return dot(jnp.concatenate(mine, axis=1), jnp.concatenate(pieces, axis=0))


def fill_broadcast(out, xproj, first, count):
    whole = xproj[...]
    high = whole.astype(BF16)
    low = (whole - high.astype(F32)).astype(BF16)
    row = lax.rem(lax.broadcasted_iota(jnp.int32, (2 * LANES, LANES), 0), LANES)
    for n in range(count):
        pick = (row == first + n).astype(F32).astype(BF16)
        out[:, n * LANES : (n + 1) * LANES] = dot(jnp.concatenate([high, low], axis=1), pick)


def rates(alog):
    return -jnp.exp(alog[...])


def chunk_of(ref, c, count):
    return jnp.concatenate([ref[b, pl.ds(c, count, stride=CHUNKS), :] for b in range(ref.shape[0])], axis=1)


def set_chunk(ref, c, value):
    for b in range(ref.shape[0]):
        ref[b, pl.ds(c, value.shape[0], stride=CHUNKS), :] = value[:, b * LANES : (b + 1) * LANES]


def payload_kernel(tokens, order, out, near, copied):
    rows, width = tokens.shape
    copies = [
        pltpu.make_async_copy(order, near, copied.at[0]),
        pltpu.make_async_copy(tokens, out.at[pl.ds(0, rows)], copied.at[1]),
    ]
    for copy in copies:
        copy.start()
    out[rows:, :] = jnp.zeros((ORDER_ROWS, width), BF16)
    copies[0].wait()
    out[rows:, 0:rows] = order_digits(near)
    copies[1].wait()


def order_column(to_row, digits):
    both = dot(to_row, digits, ((0,), (1,)))
    return jnp.broadcast_to(both[:, 0:1] * 128.0 + both[:, 1:2], (to_row.shape[0], LANES))


def order_digits(order):
    sub = lax.broadcasted_iota(jnp.int32, (ORDER_ROWS, order.shape[1]), 0)
    digits = jnp.where(sub == 0, order[...] >> 7, jnp.where(sub == 1, order[...] & 127, 0))
    return digits.astype(F32).astype(BF16)


def pre_kernel(sizes, n_pieces, n_far, me, *refs):
    rows, width, inner, rank, state, lags, clouds = sizes
    steps = rows // CHUNKS
    pieces = refs[:n_pieces]
    far_refs, refs = refs[n_pieces : n_pieces + n_far], refs[:n_pieces] + refs[n_pieces + n_far :]
    near_refs, copied, refs = refs[-n_far - 1 : -1], refs[-1], refs[: -n_far - 1]
    copies = [pltpu.make_async_copy(a, b, copied.at[k]) for k, (a, b) in enumerate(zip(far_refs, near_refs))]
    for copy in copies:
        copy.start()
    (lengths, order, gain, w_in, conv_w, conv_b, w_x, w_dt, dt_b, alog, skip) = near_refs
    copies[1].wait()
    (trans_o, normed_o, gate_o, ext_o, conv_o, act_o, step_o, xproj_o, chunkf_o, sums_o, f_o, column_o, orders_o,
     valid, far, use, bbc, wx_o, wdt_o, a2, rows_o, conv_in) = refs[n_pieces:]
    to_row = row_of_place(rows)
    sub = lax.broadcasted_iota(jnp.int32, (BLOCK, LANES), 0)
    extra = jnp.full((BLOCK, LANES), -1.0, F32)
    tail = jnp.zeros((ORDER_ROWS, rows), F32)
    for p in range(n_pieces):
        now = pieces[p][rows : rows + ORDER_ROWS, :rows]
        tail = jnp.where(source(me, p, n_pieces) == me[0] - 1, now.astype(F32), tail)
        if p < orders_o.shape[0]:
            row = dot(now, to_row)
            orders_o[p : p + 1, :] = row[0:1] * 128.0 + row[1:2]
    for k in range(1, lags + 1):
        extra = jnp.where(sub == k, tail[0:1, rows - k : rows - k + 1] * 128.0 + tail[1:2, rows - k : rows - k + 1], extra)
    own = order_column(to_row, order_digits(order))
    column_o[0] = own
    if n_pieces == len(CUBE):
        column_o[1] = order_column(to_row, pieces[CUBE.index(1)][rows : rows + ORDER_ROWS, :rows])
    column = jnp.concatenate([own, extra], axis=0)
    trans = gather_rows(wide(column, rows), [p[0:rows, :] for p in pieces], me, rows)
    trans_o[...] = trans[:rows].astype(BF16)
    for copy in copies[:1] + copies[2:]:
        copy.wait()
    meta = scalars(me, lengths, rows)
    bias, dt_bias = as_row(conv_b), as_row(dt_b)
    rows_o[0 : lags + 1, :] = conv_w[...]
    rows_o[lags + 1 : lags + 2, :] = as_row(skip)
    inv_rms = lax.rsqrt(jnp.mean(trans * trans, axis=1, keepdims=True) + EPSILON)
    normed = (trans * inv_rms * as_row(gain)).astype(BF16)
    normed_o[...] = normed[:rows]
    conv_in[...] = dot(normed, w_in[:, :inner]).astype(BF16).astype(F32)
    gate_o[...] = dot(normed[:rows], w_in[:, inner:])
    pad = lags * CHUNKS
    ext_o[pad : pad + rows, :] = conv_in[:rows, :]
    first_sub = lax.broadcasted_iota(jnp.int32, (CHUNKS, inner), 0) == 0
    for k in range(1, lags + 1):
        tile = conv_in[(steps - k) * CHUNKS : (steps - k + 1) * CHUNKS, :]
        before = conv_in[rows + k : rows + k + 1, :]
        ext_o[(lags - k) * CHUNKS : (lags - k + 1) * CHUNKS, :] = jnp.where(
            first_sub, before, pltpu.roll(tile, 1, 0)
        )
    for thin, full in ((w_x, wx_o), (w_dt, wdt_o)):
        blank = jnp.zeros((LANES - thin.shape[0], inner), F32)
        full[...] = jnp.concatenate([thin[...].astype(F32), blank], axis=0).astype(BF16)
    fill_valid(valid, meta, clouds, rows, lags)

    def conv_body(j, carry):
        r0 = pl.multiple_of(j * BLOCK, BLOCK)
        out = bias + conv_w[lags : lags + 1, :] * ext_o[pl.ds(r0 + pad, BLOCK), :]
        for k in range(1, lags + 1):
            ok = wide(valid[k - 1, pl.ds(r0, BLOCK), :], inner)
            shifted = ext_o[pl.ds(pl.multiple_of(r0 + pad - k * CHUNKS, CHUNKS), BLOCK), :]
            out = out + conv_w[lags - k : lags - k + 1, :] * shifted * ok
        conv_o[pl.ds(r0, BLOCK), :] = out
        act_o[pl.ds(r0, BLOCK), :] = (out * sigmoid(out)).astype(BF16)
        return carry

    lax.fori_loop(0, rows // BLOCK, conv_body, 0)
    xproj = dot(act_o[...], wx_o[...], ((1,), (1,)))
    xproj_o[...] = xproj
    step_o[...] = dot(xproj.astype(BF16), wdt_o[...])

    def step_body(j, carry):
        r0 = pl.multiple_of(j * BLOCK, BLOCK)
        pre = step_o[pl.ds(r0, BLOCK), :] + dt_bias
        step = jnp.maximum(pre, 0.0) + jnp.log1p(jnp.exp(-jnp.abs(pre)))
        step_o[pl.ds(r0, BLOCK), :] = step
        keep = wide(valid[0, pl.ds(r0, BLOCK), :], inner)
        distance = jnp.where(keep > 0.5, step, FAR)
        far[pl.ds(r0, BLOCK), :] = distance
        use[pl.ds(r0, BLOCK), :] = step * act_o[pl.ds(r0, BLOCK), :].astype(F32)
        return carry + distance[:CHUNKS] + distance[CHUNKS:]

    sums_o[...] = lax.fori_loop(0, rows // BLOCK, step_body, jnp.zeros((CHUNKS, inner), F32))
    fill_broadcast(bbc, xproj_o, rank, state)
    a2[...] = rates(alog) * LOG2E
    for lb in range(inner // LANES):
        ls = slice(lb * LANES, (lb + 1) * LANES)
        rate = [jnp.broadcast_to(a2[n : n + 1, ls], (CHUNKS, LANES)) for n in range(state)]

        def scan_body(i, states):
            r = pl.ds(pl.multiple_of(i * CHUNKS, CHUNKS), CHUNKS)
            distance, u = far[r, ls], use[r, ls]
            return tuple(
                jnp.exp2(distance * rate[n]) * states[n] + u * bbc[r, n * LANES : (n + 1) * LANES]
                for n in range(state)
            )

        zero = jnp.zeros((CHUNKS, LANES), F32)
        last = lax.fori_loop(0, steps, scan_body, (zero,) * state, unroll=True)
        for n in range(state):
            chunkf_o[lb, n * CHUNKS : (n + 1) * CHUNKS, :] = last[n]
    total = jnp.zeros((state, inner), F32)
    for c in range(CHUNKS):
        total = jnp.exp2(a2[...] * sums_o[c : c + 1, :]) * total + chunk_of(chunkf_o, c, state)
    f_o[...] = total


def gather_kernel(core, me, column, own, two, four, six, out):
    rows = own.shape[0]
    whole = jnp.concatenate([p[...] for p in (own, two, four, six)], axis=0)
    lane = lax.broadcasted_iota(jnp.int32, (rows, rows), 1).astype(F32)
    place = wide(column[core], rows)
    match = [(place - (source(me, p, len(CUBE)) * rows).astype(F32) == lane).astype(F32).astype(BF16) for p in range(4)]
    out[...] = dot(jnp.concatenate(match, axis=1), whole).astype(BF16)


def back_kernel(sizes, n_pieces, me, *refs):
    rows, width, inner, rank, state, lags, clouds = sizes
    steps = rows // CHUNKS
    pieces = refs[:n_pieces]
    gate, far, xproj, a2, w_out, sums, f, column, normed = refs[n_pieces : n_pieces + 9]
    n_out = len(SENT) if n_pieces == 2 else 1
    dy_o, gg_o, gm, cbc, chunkb_o, near_out, factor_o = refs[n_pieces + 9 : n_pieces + 16]
    carries_o = refs[n_pieces + 16 : n_pieces + 16 + n_out]
    (copied,) = refs[n_pieces + 16 + n_out :]
    copy = pltpu.make_async_copy(w_out, near_out, copied)
    copy.start()
    if n_pieces == 2:
        trans_dy = (pieces[0][...].astype(F32) + pieces[1][...].astype(F32)).astype(BF16)
    else:
        trans_dy = gather_rows(wide(column[0], rows), [p[...] for p in pieces], me, rows).astype(BF16)
    dy_o[...] = trans_dy
    factor_o[...] = jnp.where(jnp.bitwise_and(me[0], 1) == 1, trans_dy, normed[...])
    copy.wait()
    gg_o[...] = dot(trans_dy, near_out[...], ((1,), (1,)))

    def body(j, carry):
        r = pl.ds(pl.multiple_of(j * BLOCK, BLOCK), BLOCK)
        z = gate[r, :]
        gm[r, :] = gg_o[r, :] * (z * sigmoid(z))
        return carry

    lax.fori_loop(0, rows // BLOCK, body, 0)
    fill_broadcast(cbc, xproj, rank + state, state)
    for lb in range(inner // LANES):
        ls = slice(lb * LANES, (lb + 1) * LANES)
        rate = [jnp.broadcast_to(a2[n : n + 1, ls], (CHUNKS, LANES)) for n in range(state)]

        def scan_body(k, flows):
            r = pl.ds(pl.multiple_of((steps - 1 - k) * CHUNKS, CHUNKS), CHUNKS)
            distance, g = far[r, ls], gm[r, ls]
            return tuple(
                jnp.exp2(distance * rate[n]) * (flows[n] + g * cbc[r, n * LANES : (n + 1) * LANES])
                for n in range(state)
            )

        zero = jnp.zeros((CHUNKS, LANES), F32)
        last = lax.fori_loop(0, steps, scan_body, (zero,) * state, unroll=True)
        for n in range(state):
            chunkb_o[lb, n * CHUNKS : (n + 1) * CHUNKS, :] = last[n]
    total = jnp.zeros((state, inner), F32)
    for c in reversed(range(CHUNKS)):
        total = jnp.exp2(a2[...] * sums[c : c + 1, :]) * total + chunk_of(chunkb_o, c, state)
    passed = jnp.sum(sums[...], axis=0, keepdims=True)
    blocks = inner // LANES
    passed = jnp.concatenate([passed[:, b * LANES : (b + 1) * LANES] for b in range(blocks)], axis=0)
    passed = jnp.concatenate([passed, jnp.zeros((state - blocks, LANES), F32)], axis=0)
    if n_out == 1:
        carries_o[0][:state, :inner] = f[...]
        carries_o[0][state:, :inner] = total
        carries_o[0][:state, inner:] = passed
        carries_o[0][state:, inner:] = passed
        return
    for out, d in zip(carries_o, SENT):
        later = jnp.bitwise_xor(me[0], d) > me[0]
        out[:, :inner] = jnp.where(later, f[...], total)
        out[:, inner:] = passed


def core_of(me, devices):
    return jnp.bitwise_and(me, 1) if devices == len(CUBE) else jnp.int32(0)


def hold_carries(held, carries, me):
    n_pieces, count, inner = len(carries), carries[0].shape[0], held.shape[1]
    devices = len(CUBE) if n_pieces == len(CUBE) - 1 else n_pieces
    size = count + CHUNKS
    for p in range(n_pieces):
        whence = source(me, p + 1, devices) if devices > n_pieces else p
        base = whence * size
        held[pl.ds(pl.multiple_of(base, CHUNKS), count), :] = carries[p][:, :inner]
        passed = [carries[p][b : b + 1, inner:] for b in range(inner // LANES)]
        passed = jnp.broadcast_to(jnp.concatenate(passed, axis=1), (CHUNKS, inner))
        held[pl.ds(pl.multiple_of(base + count, CHUNKS), CHUNKS), :] = passed
    return devices, size


def scan_forward_kernel(sizes, n_pieces, me_ref, *refs):
    rows, width, inner, rank, state, lags, clouds = sizes
    steps = rows // CHUNKS
    carries = refs[:n_pieces]
    (gg, gate, act, far, use, bbc, cbc, chunkf, sums, a2, consts) = refs[n_pieces : n_pieces + 11]
    blocks = inner // LANES
    states = refs[n_pieces + 11 : n_pieces + 11 + blocks]
    (gated, gz_o, send_o) = refs[n_pieces + 11 + blocks : n_pieces + 14 + blocks]
    (mixed, sstart, held) = refs[n_pieces + 14 + blocks :]
    me = me_ref[0]
    skips = consts[lags + 1 : lags + 2, :]
    devices, size = hold_carries(held, carries, me_ref)

    def ahead(s, flow):
        base = pl.multiple_of(s * size, CHUNKS)
        p_s = jnp.exp2(a2[...] * held[pl.ds(base + size - CHUNKS, 1), :])
        return jnp.where(s < me, p_s * flow + held[pl.ds(base, state), :], flow)

    now = lax.fori_loop(0, devices, ahead, jnp.zeros((state, inner), F32))
    for c in range(CHUNKS):
        set_chunk(sstart, c, now)
        now = jnp.exp2(a2[...] * sums[c : c + 1, :]) * now + chunk_of(chunkf, c, state)

    for lb in range(inner // LANES):
        ls = slice(lb * LANES, (lb + 1) * LANES)
        rate = [jnp.broadcast_to(a2[n : n + 1, ls], (CHUNKS, LANES)) for n in range(state)]
        begin = []
        for n in range(state):
            tile = sstart[lb, n * CHUNKS : (n + 1) * CHUNKS, :]
            states[lb][n, 0:CHUNKS, :] = tile
            begin.append(tile)

        def forward(i, now):
            r0 = pl.multiple_of(i * CHUNKS, CHUNKS)
            r = pl.ds(r0, CHUNKS)
            nxt = pl.ds(pl.multiple_of(r0 + CHUNKS, CHUNKS), CHUNKS)
            distance, u = far[r, ls], use[r, ls]
            new, out = [], None
            for n in range(state):
                value = jnp.exp2(distance * rate[n]) * now[n] + u * bbc[r, n * LANES : (n + 1) * LANES]
                states[lb][n, nxt, :] = value
                part = value * cbc[r, n * LANES : (n + 1) * LANES]
                out = part if out is None else out + part
                new.append(value)
            mixed[r, ls] = out
            return tuple(new)

        lax.fori_loop(0, steps, forward, tuple(begin), unroll=True)

    second = jnp.bitwise_and(me, 1) == 1

    def gating(j, carry):
        r = pl.ds(pl.multiple_of(j * BLOCK, BLOCK), BLOCK)
        z, a = gate[r, :], act[r, :].astype(F32)
        s = sigmoid(z)
        m = mixed[r, :] + skips * a
        out = (m * (z * s)).astype(BF16)
        grad = (gg[r, :] * m * s * (1.0 + z * (1.0 - s))).astype(BF16)
        gated[r, :] = out
        gz_o[r, :] = grad
        send_o[r, :] = jnp.where(second, out, grad)
        return carry

    lax.fori_loop(0, rows // BLOCK, gating, 0)


def branch_kernel(sizes, n_pieces, me_ref, *refs):
    rows, width, inner, rank, state, lags, clouds = sizes
    carries = refs[:n_pieces]
    chunkb, sums, a2, gated, gz, trans_dy, normed, w_out, gstart, branch_o, part_o, held = refs[n_pieces:]
    me = me_ref[0]
    branch_o[...] = dot(gated[...], w_out[...]).astype(BF16)
    second = jnp.bitwise_and(me, 1) == 1
    factor = jnp.where(second, normed[...], trans_dy[...])
    part_o[...] = dot(factor, jnp.where(second, gz[...], gated[...]), ((0,), (0,)))
    devices, size = hold_carries(held, carries, me_ref)
    back = size - CHUNKS - state

    def behind(k, flow):
        s = devices - 1 - k
        base = pl.multiple_of(s * size, CHUNKS)
        p_s = jnp.exp2(a2[...] * held[pl.ds(base + size - CHUNKS, 1), :])
        return jnp.where(s > me, p_s * flow + held[pl.ds(pl.multiple_of(base + back, CHUNKS), state), :], flow)

    now = lax.fori_loop(0, devices, behind, jnp.zeros((state, inner), F32))
    for c in reversed(range(CHUNKS)):
        set_chunk(gstart, c, now)
        now = jnp.exp2(a2[...] * sums[c : c + 1, :]) * now + chunk_of(chunkb, c, state)


def scan_backward_kernel(sizes, *refs):
    rows, width, inner, rank, state, lags, clouds = sizes
    steps = rows // CHUNKS
    states, refs = refs[: inner // LANES], refs[inner // LANES :]
    (gstart, far, use, bbc, cbc, gm, step, act, conv, valid, a2, conv_w, w_x, w_dt) = refs[:14]
    (gconv, rim_o, gpre, gxproj_o, galog_o) = refs[14:19]
    (gs, lamb, gb, gc) = refs[19:]
    skips = conv_w[lags + 1 : lags + 2, :]
    group, pair = 3, 4
    for lg in range(inner // LANES // group):
        lanes = [slice((lg * group + k) * LANES, (lg * group + k + 1) * LANES) for k in range(group)]
        for ng in range(state // pair):
            ns = [ng * pair + k for k in range(pair)]
            rate = [[jnp.broadcast_to(a2[n : n + 1, ls], (CHUNKS, LANES)) for ls in lanes] for n in ns]
            begin = [gstart[lg * group + k, n * CHUNKS : (n + 1) * CHUNKS, :] for n in ns for k in range(group)]
            zero = jnp.zeros((CHUNKS, LANES), F32)

            def backward(k, carry):
                flows, sums_a = carry
                r0 = pl.multiple_of((steps - 1 - k) * CHUNKS, CHUNKS)
                r = pl.ds(r0, CHUNKS)
                nxt = pl.ds(pl.multiple_of(r0 + CHUNKS, CHUNKS), CHUNKS)
                gs_t = [None] * group
                lamb_t = [None] * group
                g_t = [gm[r, ls] for ls in lanes]
                u_t = [use[r, ls] for ls in lanes]
                d_t = [step[r, ls] for ls in lanes]
                f_t = [far[r, ls] for ls in lanes]
                new_flows, new_sums = [], []
                for q, n in enumerate(ns):
                    b = bbc[r, n * LANES : (n + 1) * LANES]
                    c = cbc[r, n * LANES : (n + 1) * LANES]
                    gb_t = gc_t = None
                    for x, ls in enumerate(lanes):
                        lam = g_t[x] * c + flows[q * group + x]
                        flow = jnp.exp2(f_t[x] * rate[q][x]) * lam
                        part = flow * states[lg * group + x][n, r, :]
                        one, two = part * rate[q][x], lam * b
                        gs_t[x] = one if gs_t[x] is None else gs_t[x] + one
                        lamb_t[x] = two if lamb_t[x] is None else lamb_t[x] + two
                        three, four = lam * u_t[x], g_t[x] * states[lg * group + x][n, nxt, :]
                        gb_t = three if gb_t is None else gb_t + three
                        gc_t = four if gc_t is None else gc_t + four
                        new_flows.append(flow)
                        new_sums.append(sums_a[q * group + x] + part * d_t[x])
                    nl = slice(n * LANES, (n + 1) * LANES)
                    if lg == 0:
                        gb[r, nl] = gb_t
                        gc[r, nl] = gc_t
                    else:
                        gb[r, nl] += gb_t
                        gc[r, nl] += gc_t
                for x, ls in enumerate(lanes):
                    if ng == 0:
                        gs[r, ls] = gs_t[x]
                        lamb[r, ls] = lamb_t[x]
                    else:
                        gs[r, ls] += gs_t[x]
                        lamb[r, ls] += lamb_t[x]
                return tuple(new_flows), tuple(new_sums)

            flows, sums_a = lax.fori_loop(
                0, steps, backward, (tuple(begin), (zero,) * (pair * group)), unroll=True
            )
            for q, n in enumerate(ns):
                for x, ls in enumerate(lanes):
                    galog_o[n : n + 1, ls] = (
                        jnp.sum(sums_a[q * group + x], axis=0, keepdims=True) * rate[q][x][0:1] * (1.0 / LOG2E)
                    )
    col = lax.broadcasted_iota(jnp.int32, (state * LANES, LANES), 1)
    row = lax.div(lax.broadcasted_iota(jnp.int32, (state * LANES, LANES), 0), LANES)
    pick_b = (col == row + rank).astype(F32).astype(BF16)
    pick_c = (col == row + rank + state).astype(F32).astype(BF16)

    def lane_sums(ref, pick):
        return dot(ref[...].astype(BF16), pick)

    grad_bc = lane_sums(gb, pick_b) + lane_sums(gc, pick_c)

    def pre_body(j, carry):
        r = pl.ds(pl.multiple_of(j * BLOCK, BLOCK), BLOCK)
        grad_step = gs[r, :] * (1.0 / LOG2E) + lamb[r, :] * act[r, :].astype(F32)
        gpre[r, :] = (grad_step * (1.0 - jnp.exp(-step[r, :]))).astype(BF16)
        return carry

    lax.fori_loop(0, rows // BLOCK, pre_body, 0)
    grad_xproj = (dot(gpre[...], w_dt[...], ((1,), (1,))) + grad_bc).astype(BF16)
    gxproj_o[...] = grad_xproj
    gs[...] = dot(grad_xproj, w_x[...])

    def conv_body(j, carry):
        r = pl.ds(pl.multiple_of(j * BLOCK, BLOCK), BLOCK)
        grad_act = gm[r, :] * skips + lamb[r, :] * step[r, :] + gs[r, :]
        v = conv[r, :]
        s = sigmoid(v)
        gconv[r, :] = grad_act * (s * (1.0 + v * (1.0 - s)))
        return carry

    lax.fori_loop(0, rows // BLOCK, conv_body, 0)
    rim_o[...] = jnp.zeros((CHUNKS, inner), F32)
    for b in range(1, lags + 1):
        total = jnp.zeros((1, inner), F32)
        for k in range(b, lags + 1):
            total = total + masked_tile(gconv, valid, conv_w, k - b, k, lags)[0:1]
        rim_o[b : b + 1, :] = total


def masked_tile(gconv, valid, conv_w, i, k, lags):
    r = pl.ds(pl.multiple_of(i * CHUNKS, CHUNKS), CHUNKS)
    tile = gconv[r, :] * conv_w[lags - k : lags - k + 1, :]
    return tile if k == 0 else tile * wide(valid[k - 1, r, :], tile.shape[1])


def small_kernel(sizes, gpre, gxproj, xproj, act, gconv, ext, valid, gm, conv_w, galog, small_o, gci_o):
    rows, width, inner, rank, state, lags, clouds = sizes
    steps = rows // CHUNKS

    def spread(i, carry):
        total = masked_tile(gconv, valid, conv_w, i, 0, lags)
        for k in range(1, lags + 1):
            total = total + masked_tile(gconv, valid, conv_w, i + k, k, lags)
        gci_o[pl.ds(pl.multiple_of(i * CHUNKS, CHUNKS), CHUNKS), :] = total
        return carry

    lax.fori_loop(0, steps - lags, spread, 0)
    sub = lax.broadcasted_iota(jnp.int32, (CHUNKS, inner), 0)
    for i in range(steps - lags, steps):
        total = masked_tile(gconv, valid, conv_w, i, 0, lags)
        for k in range(1, lags + 1):
            if i + k < steps:
                total = total + masked_tile(gconv, valid, conv_w, i + k, k, lags)
            else:
                moved = pltpu.roll(masked_tile(gconv, valid, conv_w, i + k - steps, k, lags), CHUNKS - 1, 0)
                total = total + jnp.where(sub == CHUNKS - 1, 0.0, moved)
        gci_o[i * CHUNKS : (i + 1) * CHUNKS, :] = total

    def sum_body(j, carry):
        r0 = pl.multiple_of(j * BLOCK, BLOCK)
        r = pl.ds(r0, BLOCK)
        grad = gconv[r, :]
        parts = [gm[r, :] * act[r, :].astype(F32), gpre[r, :].astype(F32), grad]
        for k in reversed(range(lags + 1)):
            masked = grad if k == 0 else grad * wide(valid[k - 1, r, :], inner)
            parts.append(masked * ext[pl.ds(pl.multiple_of(r0 + (lags - k) * CHUNKS, CHUNKS), BLOCK), :])
        return tuple(total + part[:CHUNKS] + part[CHUNKS:] for total, part in zip(carry, parts))

    sums = lax.fori_loop(0, rows // BLOCK, sum_body, (jnp.zeros((CHUNKS, inner), F32),) * (lags + 4))
    small_o[0:state, :] = galog[...]
    at = state
    small_o[at : at + rank + 2 * state, :] = dot(gxproj[...], act[...], ((0,), (0,)))[: rank + 2 * state]
    at += rank + 2 * state
    small_o[at : at + rank, :] = dot(xproj[...].astype(BF16), gpre[...], ((0,), (0,)))[:rank]
    at += rank
    for k, part in enumerate(sums):
        small_o[at + k : at + k + 1, :] = jnp.sum(part, axis=0, keepdims=True)
    at += len(sums)
    small_o[at:, :] = jnp.zeros((small_o.shape[0] - at, inner), F32)


def final_kernel(sizes, devices, me, trans, normed, gci, gz, rim, small, gain, w_in, back_o, keep_o, send_o, both):
    rows, width, inner, rank, state, lags, clouds = sizes
    steps = rows // CHUNKS
    r = lax.broadcasted_iota(jnp.int32, (rows, inner), 0)
    total = gci[...]
    for k in range(1, lags + 1):
        total = total + jnp.where(r == (steps - k) * CHUNKS + CHUNKS - 1, rim[k : k + 1, :], 0.0)
    grad_ci = total.astype(BF16)
    grad_z = gz[...]
    grad_normed = dot(grad_ci, w_in[:, :inner], ((1,), (1,))) + dot(grad_z, w_in[:, inner:], ((1,), (1,)))
    x = trans[...].astype(F32)
    inv_rms = lax.rsqrt(jnp.mean(x * x, axis=1, keepdims=True) + EPSILON)
    scaled = grad_normed * as_row(gain)
    back_o[...] = (
        inv_rms * scaled
        - inv_rms * inv_rms * inv_rms * x * jnp.mean(scaled * x, axis=1, keepdims=True)
    ).astype(BF16)
    both[0:width, :] = dot(normed[...], grad_ci, ((0,), (0,))).astype(BF16)
    gain_row = jnp.sum(grad_normed * x * inv_rms, axis=0, keepdims=True)
    gain_row = jnp.concatenate([gain_row, jnp.zeros((1, inner - width), F32)], axis=1)
    n_small = small.shape[0]
    last = lax.broadcasted_iota(jnp.int32, (n_small, inner), 0) == n_small - 1
    both[width : width + n_small, :] = jnp.where(last, gain_row, small[...]).astype(BF16)
    both[width + n_small :, :] = jnp.zeros((both.shape[0] - width - n_small, inner), BF16)
    half = keep_o.shape[0]
    core = core_of(me[0], devices)
    keep_o[...] = both[pl.ds(pl.multiple_of(core * half, BLOCK), half), :]
    send_o[...] = both[pl.ds(pl.multiple_of((1 - core) * half, BLOCK), half), :]


def small_rows(sizes):
    rows, width, inner, rank, state, lags, clouds = sizes
    return state + (rank + 2 * state) + rank + 3 + lags + 1 + 1


def halves_kernel(me, kept, got, own_o, *sent_o):
    part = own_o.shape[0]
    chip = lax.div(me[0], 2)
    for d, out in enumerate((own_o,) + sent_o):
        r = pl.ds(pl.multiple_of(jnp.bitwise_xor(chip, d) * part, BLOCK), part)
        out[...] = (kept[r, :].astype(F32) + got[r, :].astype(F32)).astype(BF16)


def beside(out, rows):
    half, width = rows.shape[0] // 2, rows.shape[1]
    out[0:half, 0:width] = rows[0:half, :]
    out[0:half, width:] = rows[half:, :]


def unfold(piece, rows, width):
    if piece.shape == (rows, width):
        return piece[...]
    half = rows // 2
    return jnp.concatenate([piece[0:half, 0:width], piece[0:half, width : 2 * width]], axis=0)


def first_halves_kernel(me, kept, factor, got, rows, own_o, *sent_o):
    whole, sent_o = sent_o[-1], sent_o[:-1]
    part = own_o.shape[0]
    half = rows.shape[0] // 2
    chip = lax.div(me[0], 2)
    whole[...] = kept[...] + dot(factor[...], got[...], ((0,), (0,)))
    for d, out in enumerate((own_o,) + sent_o):
        r = pl.ds(pl.multiple_of(jnp.bitwise_xor(chip, d) * part, BLOCK), part)
        total = whole[r, :].astype(BF16)
        if d == 0:
            out[...] = total
        else:
            beside(out, rows)
            out[half:, :] = total


def products_kernel(trans_dy, gated, normed, gz, wout_o, gate_o):
    wout_o[...] = dot(trans_dy[...], gated[...], ((0,), (0,)))
    gate_o[...] = dot(normed[...], gz[...], ((0,), (0,)))


def sum_kernel(a, b, c, d, out):
    one, two, three, four = (x[x.shape[0] - a.shape[0] :, :].astype(F32) for x in (a, b, c, d))
    out[...] = ((one + two) + (three + four)).astype(BF16)


def pair_kernel(a, b, out):
    out[...] = (a[...].astype(F32) + b[...].astype(F32)).astype(BF16)


def chips_kernel(me, own, two, four, six, out):
    part = own.shape[0]
    for d, piece in enumerate((own, two, four, six)):
        chip = jnp.bitwise_xor(lax.div(me[0], 2), d)
        out[pl.ds(pl.multiple_of(chip * part, BLOCK), part), :] = piece[...]


def share_kernel(rows, width, me, orders, own, two, four, six, mine_o, theirs_o):
    pieces = (own, two, four, six)
    whole = jnp.concatenate([unfold(p, rows, width) for p in pieces], axis=0)
    for core, out in enumerate((mine_o, theirs_o)):
        first = jnp.bitwise_xor(me[0], core) * rows
        place = (first + lax.broadcasted_iota(jnp.int32, (rows, rows), 0)).astype(F32)
        match = [(orders[p : p + 1, :] == place).astype(F32).astype(BF16) for p in range(len(pieces))]
        moved = dot(jnp.concatenate(match, axis=1), whole).astype(BF16)
        if core == 0:
            out[...] = moved
        else:
            out[:, 0:width] = moved[: rows // 2]
            out[:, width:] = moved[rows // 2 :]


def share_both_kernel(rows, width, me, orders, *refs):
    one, two, (mine_one, mine_two, theirs_o) = refs[0:4], refs[4:8], refs[8:]
    share_kernel(rows, width, me, orders, *one, mine_one, theirs_o.at[pl.ds(0, rows // 2)])
    share_kernel(rows, width, me, orders, *two, mine_two, theirs_o.at[pl.ds(rows // 2, rows // 2)])


def arrive_both_kernel(here_one, here_two, mine_one, mine_two, theirs, out_one, out_two):
    half = here_one.shape[0] // 2
    arrive_kernel(here_one, mine_one, theirs.at[pl.ds(0, half)], out_one)
    arrive_kernel(here_two, mine_two, theirs.at[pl.ds(half, half)], out_two)


def arrive_kernel(here, mine, theirs, out):
    rows, width = here.shape
    moved = mine[...].astype(F32) + unfold(theirs, rows, width).astype(F32)
    out[...] = (here[...].astype(F32) + moved).astype(BF16)


def halves_of(own, other, me, devices):
    second = core_of(me[0], devices) == 1
    return jnp.where(second, other, own), jnp.where(second, own, other)


def first_results_kernel(half, devices, me, own, other, wout_o, win_o, turned, copied):
    wout, gate = halves_of(own[own.shape[0] - half :, :], other[other.shape[0] - half :, :], me, devices)
    turned[...] = gate.astype(F32)
    inner = turned.shape[1]
    copy = pltpu.make_async_copy(turned, win_o.at[:, pl.ds(inner, inner)], copied)
    copy.start()
    wout_o[...] = wout.astype(F32).T
    copy.wait()


def last_results_kernel(sizes, half, devices, me, own, other, win, *refs):
    rows, width, inner, rank, state, lags, clouds = sizes
    (gain_o, win_o, taps_o, convb_o, wx_o, wdt_o, dtb_o, alog_o, skip_o, near, copied) = refs
    first, second = halves_of(own[0:half, :], other[0:half, :], me, devices)
    whole = jnp.concatenate([first, second], axis=0)
    copies = []
    for k in range(width // LANES):
        r = pl.ds(k * LANES, LANES)
        near[r, :] = whole[k * LANES : (k + 1) * LANES].astype(F32)
        copies.append(pltpu.make_async_copy(near.at[r], win_o.at[r, pl.ds(0, inner)], copied.at[k]))
        copies[-1].start()
    n_small = small_rows(sizes)
    small = whole[width : width + n_small].astype(F32)
    alog_o[...] = small[0:state]
    at = state
    wx_o[...] = small[at : at + rank + 2 * state]
    at += rank + 2 * state
    wdt_o[...] = small[at : at + rank]
    at += rank
    for k, out in enumerate((skip_o, dtb_o, convb_o)):
        out[...] = small[at + k : at + k + 1].reshape(inner)
    at += 3
    taps_o[...] = small[at : at + lags + 1]
    gain_o[...] = small[n_small - 1 : n_small, :width].reshape(width)
    for copy in copies:
        copy.wait()


def place_kernel(rows, n_pieces, me, here, orders, *refs):
    pieces, out = refs[:n_pieces], refs[n_pieces]
    place = (me[0] * rows + lax.broadcasted_iota(jnp.int32, (rows, rows), 0)).astype(F32)
    mine = [(orders[p : p + 1, :] == place).astype(F32).astype(BF16) for p in range(n_pieces)]
    moved = dot(jnp.concatenate(mine, axis=1), jnp.concatenate([p[...] for p in pieces], axis=0))
    out[...] = (here[...].astype(F32) + moved).astype(BF16)


def call(kernel, outs, scratch, n_smem, name, room, far_ins=(), far_outs=(), aliases={}):
    vmem = pl.BlockSpec(memory_space=pltpu.VMEM)
    smem = pl.BlockSpec(memory_space=pltpu.SMEM)
    anywhere = pl.BlockSpec(memory_space=pltpu.HBM)

    def run(*args):
        args = [pltpu.with_memory_space_constraint(v, pltpu.HBM) if k in far_ins else v for k, v in enumerate(args)]
        return pl.pallas_call(
            kernel,
            out_shape=[jax.ShapeDtypeStruct(*part) if isinstance(part, tuple) else part for part in outs],
            in_specs=[smem if k < n_smem else anywhere if k in far_ins else vmem for k in range(len(args))],
            out_specs=[anywhere if k in far_outs else vmem for k in range(len(outs))],
            input_output_aliases=aliases,
            scratch_shapes=[pltpu.VMEM(*part) if isinstance(part, tuple) else part for part in scratch],
            compiler_params=pltpu.CompilerParams(vmem_limit_bytes=room * MIB),
            cost_estimate=pl.CostEstimate(
                flops=1, bytes_accessed=1, transcendentals=0
            ),
            name=name,
        )(*args)

    return run


def after(value, *others):
    return lax.optimization_barrier((value, others))[0]


def swap(block, axis, distance):
    devices = lax.axis_size(axis)
    return lax.ppermute(block, axis, [(i, i ^ distance) for i in range(devices)])


def spread_pieces(block, axis):
    whole = lax.all_gather(block, axis)
    return [whole[i] for i in range(lax.axis_size(axis))]


def spread_carries(blocks, axis):
    if len(blocks) == 1:
        return spread_pieces(blocks[0], axis)
    across = [swap(block, axis, d) for block, d in zip(blocks, SENT)]
    return across[:3] + [across[3]] + [swap(part, axis, 1) for part in across[:3]]


def from_behind(block, axis, distance):
    devices = range(lax.axis_size(axis))
    route = [(i - distance, i) for i in devices if i - distance in devices]
    return lax.ppermute(block, axis, route)


def shards(
    tokens,
    lengths,
    order,
    norm_gain,
    w_in,
    conv_weight,
    conv_bias,
    w_x,
    w_dt,
    dt_bias,
    a_log,
    d_skip,
    w_out,
    cotangent,
):
    rows, width = tokens.shape[1:]
    inner, rank, state, taps = w_out.shape[0], w_dt.shape[0], a_log.shape[1], conv_weight.shape[1]
    lags, clouds, steps = taps - 1, lengths.shape[1], rows // CHUNKS
    sizes = (rows, width, inner, rank, state, lags, clouds)
    devices = lax.axis_size("seq")
    me = lax.axis_index("seq").astype(jnp.int32)[None]
    here_x, here_dy = tokens[0], cotangent[0]
    cube = devices == len(CUBE) and lax.axis_size("dp") == 4
    if devices == len(CUBE) and not cube:
        raise ValueError("unknown mesh")
    (payload,) = call(
        payload_kernel,
        [((rows + ORDER_ROWS, width), BF16)],
        [(order.shape, order.dtype), pltpu.SemaphoreType.DMA((2,))],
        0,
        "tokens_and_order",
        4,
        far_ins=(0, 1),
    )(here_x, order)
    weights = (lengths, order, norm_gain, w_in, conv_weight.T, conv_bias, w_x.T, w_dt, dt_bias, a_log.T, d_skip)
    if cube:
        across_x = [payload] + [swap(payload, "seq", d) for d in CUBE[1:4]]
        send_dy = after(here_dy, across_x[2])
        across_dy = [send_dy] + [swap(send_dy, "seq", d) for d in CUBE[1:4]]
        pieces_x = across_x + [swap(part, "seq", 1) for part in across_x]
    else:
        pieces_x, pieces_dy = spread_pieces(payload, "seq"), spread_pieces(here_dy, "seq")
    n = len(pieces_x)
    big, lane = (rows, inner), (rows, LANES)
    carried = (inner // LANES, state * CHUNKS, LANES)
    spread = (rows, state * LANES)
    ext_rows = rows + lags * CHUNKS
    (trans, normed, gate, ext, conv, act, step, xproj, chunkf, sums, f, column, orders, valid, far, use, bbc, w_x_pad, w_dt_pad, a2, row_consts) = call(
        functools.partial(pre_kernel, sizes, n, len(weights)),
        [
            ((rows, width), BF16),
            ((rows, width), BF16),
            (big, F32),
            ((ext_rows, inner), F32),
            (big, F32),
            (big, BF16),
            (big, F32),
            (lane, F32),
            (carried, F32),
            ((CHUNKS, inner), F32),
            ((state, inner), F32),
            ((1 + cube, *lane), F32),
            ((4 if cube else n, rows), F32),
            ((lags, rows, LANES), F32),
            (big, F32),
            (big, F32),
            (spread, F32),
            ((LANES, inner), BF16),
            ((LANES, inner), BF16),
            ((state, inner), F32),
            ((lags + 2, inner), F32),
        ],
        [((rows + BLOCK, inner), F32), pltpu.SMEM(lengths.shape, jnp.int32)]
        + [(v.shape, v.dtype) for v in weights[1:]]
        + [pltpu.SemaphoreType.DMA((len(weights),))],
        1,
        "forward_local",
        24,
        far_ins=tuple(range(n + 1, n + 1 + len(weights))),
    )(me, *pieces_x, *weights)
    if cube:
        gather = lambda core: call(
            functools.partial(gather_kernel, core), [((rows, width), BF16)], [], 1, ("gather", "gather_other")[core], 8
        )
        (theirs,) = gather(1)(me, column, *across_dy)
        (mine,) = gather(0)(me, after(column, theirs), *across_dy)
        pieces_dy = [mine, swap(theirs, "seq", 1)]
    carry_rows = (state, 2 * state)[not cube]
    n_sent = (len(SENT), 1)[not cube]
    trans_dy, gg, gm, cbc, chunkb, near_out, factor, *carries = call(
        functools.partial(back_kernel, sizes, len(pieces_dy)),
        [((rows, width), BF16), (big, F32), (big, F32), (spread, F32), (carried, F32), (w_out.shape, BF16), ((rows, width), BF16)]
        + [((carry_rows, inner + LANES), F32)] * n_sent,
        [pltpu.SemaphoreType.DMA],
        1,
        "backward_local",
        20,
        far_ins=(len(pieces_dy) + 5,),
    )(me, *pieces_dy, gate, far, xproj, a2, w_out, sums, f, column, normed)
    carries = spread_carries(carries, "seq")
    if cube:
        factor = swap(factor, "seq", 1)
        gate = after(gate, factor)
    n_small = small_rows(sizes)
    held = ((n * (carry_rows + CHUNKS), inner), F32)
    kept = [pltpu.VMEM((state, rows + CHUNKS, LANES), F32)] * (inner // LANES)
    *states, gated, gz, send = call(
        functools.partial(scan_forward_kernel, sizes, len(carries)),
        [*kept, (big, BF16), (big, BF16), (big, BF16)],
        [(big, F32), (carried, F32), held],
        1,
        "scan_forward",
        18,
    )(me, *carries, gg, gate, act, far, use, bbc, cbc, chunkf, sums, a2, row_consts)
    half_one, half_two = width, -(-(width + n_small) // (8 * BLOCK)) * (4 * BLOCK)
    if cube:
        got = swap(send, "seq", 1)
    gstart, branch, part = call(
        functools.partial(branch_kernel, sizes, len(carries)),
        [(carried, F32), ((rows, width), BF16), ((width, inner), F32)],
        [held],
        1,
        "adjoint_carries_and_branch",
        8,
    )(me, *carries, chunkb, sums, a2, gated, gz, trans_dy, normed, near_out)
    if cube:
        part_one = half_one // 4
        beside_one = ((rows // 2 + part_one, inner), BF16)
        own_one, *sent = call(
            first_halves_kernel,
            [((part_one, inner), BF16)] + [beside_one] * 3,
            [((width, inner), F32)],
            1,
            "first_halves",
            12,
        )(me, part, factor, got, branch)
        six, four, two = [swap(sent[k], "seq", SENT[k]) for k in (2, 1, 0)]
        away_one = [two, four, six]
    gconv, rim, gpre, gxproj, galog = call(
        functools.partial(scan_backward_kernel, sizes),
        [(big, F32), ((CHUNKS, inner), F32), (big, BF16), (lane, BF16), ((state, inner), F32)],
        [(big, F32), (big, F32), (spread, F32), (spread, F32)],
        0,
        "scan_backward",
        20,
    )(
        *[pltpu.with_memory_space_constraint(part, pltpu.VMEM) for part in states],
        gstart, far, use, bbc, cbc, gm, step, act, conv, valid, a2, row_consts, w_x_pad, w_dt_pad,
    )
    rim = from_behind(rim, "seq", -1)
    small, gci = call(
        functools.partial(small_kernel, sizes),
        [((n_small, inner), F32), (big, F32)],
        [],
        0,
        "small_grads",
        16,
    )(gpre, gxproj, xproj, act, gconv, ext, valid, gm, row_consts, galog)
    if cube:
        (one,) = call(sum_kernel, [((part_one, inner), BF16)], [], 0, "add_parts", 4)(
            after(own_one, small), *away_one
        )
        small = after(small, one)
    back, keep, send = call(
        functools.partial(final_kernel, sizes, devices),
        [((rows, width), BF16), ((half_two, inner), BF16), ((half_two, inner), BF16)],
        [((2 * half_two, inner), BF16)],
        1,
        "input_projection_grads",
        16,
    )(me, trans, normed, gci, gz, rim, small, norm_gain, w_in)
    cores = devices if cube else 0

    def first_results(own, other):
        return call(
            functools.partial(first_results_kernel, half_one, cores),
            [((inner, width), F32), ((width, 2 * inner), F32)],
            [((width, inner), F32), pltpu.SemaphoreType.DMA],
            1,
            "first_results",
            16,
            far_outs=(1,),
        )(me, own, other)

    if cube:
        part_two = half_two // 4
        piece_one, piece_two = ((part_one, inner), BF16), ((part_two, inner), BF16)
        pair_one, pair_two = [call(pair_kernel, [piece], [], 0, "add_pair", 4) for piece in (piece_one, piece_two)]
        got = swap(send, "seq", 1)
        one = after(one, send)
        z_one = swap(one, "dp", 1)
        own_two, *sent = call(halves_kernel, [piece_two] * 4, [], 1, "add_halves", 4)(me, keep, got)
        away_two = [swap(block, "seq", d) for block, d in zip(sent, SENT)]
        (one,) = pair_one(after(one, away_two[0]), z_one)
        z_here, z_one = z_one, swap(one, "dp", 2)
        (two,) = call(sum_kernel, [piece_two], [], 0, "add_parts", 4)(after(own_two, z_here), *away_two)
        (two,) = pair_two(two, swap(two, "dp", 1))
        z_two = swap(two, "dp", 2)
        back = after(back, own_two)
        away_back = [swap(back, "seq", d) for d in SENT[:3]]
        mine_b, mine_g, theirs = call(
            functools.partial(share_both_kernel, rows, width),
            [((rows, width), BF16)] * 2 + [((rows, inner), BF16)],
            [],
            1,
            "share_rows",
            12,
        )(me, orders, after(branch, two), *away_one, back, *away_back)
        output, input_grad = call(arrive_both_kernel, [((rows, width), BF16)] * 2, [], 0, "add_arrived", 8)(
            here_x, here_dy, mine_b, mine_g, swap(theirs, "seq", 1)
        )
        paired = two
        (two,) = pair_two(two, z_two)
        (one,) = pair_one(one, z_one)
        away_one = []
        for d in SENT[:3]:
            held_back = one
            for there in (*away_back, paired):
                held_back = after(held_back, there)
            away_one.append(swap(held_back, "seq", d))
        order_parts = lambda half: call(chips_kernel, [((half, inner), BF16)], [], 1, "order_parts", 4)
        (own_one,) = order_parts(half_one)(me, after(one, two), *away_one)
        f_wout, f_win = first_results(own_one, swap(own_one, "seq", 1))
        away_two = [swap(two, "seq", d) for d in SENT[:3]]
        (own_two,) = order_parts(half_two)(me, after(two, f_wout), *away_two)
        totals = (own_two, swap(own_two, "seq", 1))
    else:
        first = call(products_kernel, [((width, inner), F32)] * 2, [], 0, "products", 12)(trans_dy, gated, normed, gz)
        totals = [lax.psum(half.astype(F32), ("dp", "seq")).astype(BF16) for half in (*first, keep, send)]
        f_wout, f_win = first_results(*totals[:2])
        totals = totals[2:]
        place = call(functools.partial(place_kernel, rows, n), [((rows, width), BF16)], [], 1, "to_hilbert", 24)
        (output,) = place(me, here_x, orders, *spread_pieces(branch, "seq"))
        (input_grad,) = place(me, here_dy, orders, *spread_pieces(back, "seq"))
    gain, f_win, taps_g, convb, wx, wdt, dtb, alog, skip = call(
        functools.partial(last_results_kernel, sizes, half_two, cores),
        [
            ((width,), F32),
            ((width, 2 * inner), F32),
            ((taps, inner), F32),
            ((inner,), F32),
            ((rank + 2 * state, inner), F32),
            ((rank, inner), F32),
            ((inner,), F32),
            ((state, inner), F32),
            ((inner,), F32),
        ],
        [((width, inner), F32), pltpu.SemaphoreType.DMA((width // LANES,))],
        1,
        "last_results",
        16,
        far_ins=(3,),
        far_outs=(1,),
        aliases={3: 1},
    )(me, *totals, f_win)
    return (output[None], input_grad[None], gain, f_win, taps_g.T, convb, wx.T, wdt, dtb, alog.T, skip, f_wout)


def solution(mesh):
    placed = (
        P("dp", "seq", None),
        P("dp", None),
        P("dp", "seq"),
        P(),
        P(),
        P(),
        P(),
        P(),
        P(),
        P(),
        P(),
        P(),
        P(),
        P("dp", "seq", None),
    )
    return jax.shard_map(
        shards,
        mesh=mesh,
        in_specs=placed,
        out_specs=(
            P("dp", "seq", None),
            P("dp", "seq", None),
            P(),
            P(),
            P(),
            P(),
            P(),
            P(),
            P(),
            P(),
            P(),
            P(),
        ),
        check_vma=False,
    )
```
